128 devices in a mesh: dp: 32 (over z, y_lo, x), tensor: 4 (over y_hi, core).
Axes of the slice: x: 4, y: 4 (y_hi: 2, y_lo: 2; y = y_hi * 2 + y_lo), z: 4, core: 2. Of those that a mesh axis runs over, the one named last changes fastest.
Arguments:
- layer_input: bfloat16 [49152, 768], P('dp'), may hold values from -6 to 6
- flags: int32 [49152], P('dp'), may hold values from 0 to 1, as said below
- loss_mask: int32 [49152], P('dp'), may hold values 0 or 1
- cotangent: bfloat16 [49152, 768], P('dp'), may hold values from -6 to 6
- gain_one: float32 [768], replicated, may hold values from 0.5 to 1.5
- shift_one: float32 [768], replicated, may hold values from -1.8 to 1.8
- w_qkv: bfloat16 [3, 768, 768], P(None, None, 'tensor'), may hold values from -0.21875 to 0.21875
- b_qv: float32 [2, 768], P(None, 'tensor'), may hold values from -1.8 to 1.8
- w_out: bfloat16 [768, 768], P('tensor'), may hold values from -0.875 to 0.875
- b_out: float32 [768], replicated, may hold values from -1.8 to 1.8
- gain_two: float32 [768], replicated, may hold values from 0.5 to 1.5
- shift_two: float32 [768], replicated, may hold values from -1.8 to 1.8
- w_up: bfloat16 [768, 3072], P(None, 'tensor'), may hold values from -0.21875 to 0.21875
- b_up: float32 [3072], P('tensor'), may hold values from -3 to 3
- w_down: bfloat16 [3072, 768], P('tensor'), may hold values from -0.109375 to 0.109375
- b_down: float32 [768], replicated, may hold values from -1.8 to 1.8
Outputs:
- output: bfloat16 [49152, 768], P('dp')
- grad_input: bfloat16 [49152, 768], P('dp')
- grad_gain_one: float32 [768], replicated
- grad_shift_one: float32 [768], replicated
- grad_w_qkv: float32 [3, 768, 768], P(None, None, 'tensor')
- grad_b_qv: float32 [2, 768], P(None, 'tensor')
- grad_w_out: float32 [768, 768], P('tensor')
- grad_b_out: float32 [768], replicated
- grad_gain_two: float32 [768], replicated
- grad_shift_two: float32 [768], replicated
- grad_w_up: float32 [768, 3072], P(None, 'tensor')
- grad_b_up: float32 [3072], P('tensor')
- grad_w_down: float32 [3072, 768], P('tensor')
- grad_b_down: float32 [768], replicated
The draws below stay inside these ranges and needn't reach their ends.
Inputs may be any that keep to these rules, and one draw needn't show every extreme that they name: Within each sequence of 512 consecutive rows the flags are 1 on a leading run of 1 to 511 rows and 0 after it.
All inputs are finite; a program needn't handle non-finite values. No bound on the sum of `loss_mask` on one device may be relied on, other than what follows from the above.
Results may differ from the reference program's by a relative error of at most 0.01.
Values may be sent and summed in bfloat16 or wider, within the bound.
A program may use at most 192 MiB of HBM per device.

```python
import jax
import jax.numpy as jnp
from jax import lax

D = 768
HEADS = 12
FF = 3072
HDIM = 64
LEN = 512
SEQ_DEV = 3
TOKENS = 49152


def draw_flags(key, part):
    key = jax.random.fold_in(key, 11)
    boundary = jax.random.randint(key, (TOKENS // LEN, 1), 1, LEN)
    position = jnp.arange(LEN, dtype=jnp.int32)[None, :]
    return (position < boundary).astype(jnp.int32).reshape(TOKENS)


def with_ends(values, stream_key, smallest, top_value):
    dims = values.shape
    index_at = [jax.random.randint(jax.random.fold_in(stream_key, axis), (), 0, dims[axis]) for axis in range(len(dims))]
    values = values.at[tuple(index_at)].set(smallest)
    longest = dims.index(max(dims))
    index_at[longest] = (index_at[longest] + 1) % dims[longest]
    return values.at[tuple(index_at)].set(top_value)


def level_of(key, shape, shards, low, largest):
    level = 1.0
    for dim, blocks in shards:
        heights = jax.random.uniform(jax.random.fold_in(jax.random.fold_in(key, 6), dim), (blocks,), jnp.float32, low / len(shards), largest / len(shards))
        level = level * jnp.repeat(jnp.exp(heights), shape[dim] // blocks).reshape((-1,) + (1,) * (len(shape) - 1 - dim))
    return level


def bell_draw(stream_key, extent, deviation, reach, pieces=(), held_as=jnp.bfloat16):
    entries = deviation * jax.random.normal(stream_key, extent, jnp.float32)
    if pieces:
        entries = entries * level_of(stream_key, extent, pieces, -0.22, 0.18)
    return jnp.clip(entries, -reach, reach).astype(held_as)


def setup_inputs(seed: int = 0) -> dict:
    key_list = jax.random.split(jax.random.key(seed), 17)
    layer_input = bell_draw(key_list[0], (TOKENS, D), 1.0, 6.0, ((0, 32),))
    flags = draw_flags(jax.random.fold_in(key_list[16], 71), 0)
    loss_mask = with_ends((jax.random.randint(key_list[2], (TOKENS,), 0, 2) < 1).astype(jnp.int32), jax.random.fold_in(key_list[2], 1), 0, 1)
    cotangent = bell_draw(key_list[3], (TOKENS, D), 1.0, 6.0, ((0, 32),))
    gain_one = jnp.clip(1.0 + 0.1 * jax.random.normal(key_list[4], (D,), jnp.float32), 0.5, 1.5)
    shift_one = bell_draw(key_list[5], (D,), 0.3, 1.8, (), jnp.float32)
    w_qkv = bell_draw(key_list[6], (3, D, D), D ** -0.5, 0.21875, ((2, 4),))
    b_qv = bell_draw(key_list[7], (2, D), 0.3, 1.8, ((1, 4),), jnp.float32)
    w_out = bell_draw(key_list[8], (D, D), (D // 16) ** -0.5, 0.875, ((0, 4),))
    b_out = bell_draw(key_list[9], (D,), 0.3, 1.8, (), jnp.float32)
    gain_two = jnp.clip(1.0 + 0.1 * jax.random.normal(key_list[10], (D,), jnp.float32), 0.5, 1.5)
    shift_two = bell_draw(key_list[11], (D,), 0.3, 1.8, (), jnp.float32)
    w_up = bell_draw(key_list[12], (D, FF), D ** -0.5, 0.21875, ((1, 4),))
    b_up = bell_draw(key_list[13], (FF,), 0.5, 3.0, ((0, 4),), jnp.float32)
    w_down = bell_draw(key_list[14], (FF, D), FF ** -0.5, 0.109375, ((0, 4),))
    b_down = bell_draw(key_list[15], (D,), 0.3, 1.8, (), jnp.float32)
    return dict(layer_input=layer_input, flags=flags, loss_mask=loss_mask, cotangent=cotangent, gain_one=gain_one, shift_one=shift_one, w_qkv=w_qkv, b_qv=b_qv, w_out=w_out, b_out=b_out, gain_two=gain_two, shift_two=shift_two, w_up=w_up, b_up=b_up, w_down=w_down, b_down=b_down)


@jax.custom_vjp
def low(v):
    return lax.optimization_barrier(v.astype(jnp.bfloat16)).astype(jnp.float32)

@jax.custom_vjp
def low_back(v):
    return v

def low_keep(v):
    return (low(v), None)

def low_pass(kept, grad):
    return (grad,)

def back_keep(v):
    return (v, None)

def back_low(kept, grad):
    return (low(grad),)
low.defvjp(low_keep, low_pass)
low_back.defvjp(back_keep, back_low)
epsilon = 1e-05
highest = lax.Precision.HIGHEST

def layer_norm(source, scaling, offset):
    average = lax.optimization_barrier(jnp.mean(source, axis=-1, keepdims=True))
    centred = source - average
    spread = lax.optimization_barrier(jnp.mean(centred * centred, axis=-1, keepdims=True))
    return centred * lax.rsqrt(spread + epsilon) * scaling + offset

def attend_group(packed):
    query_part, key_part, value_part = packed
    score_scale = HDIM ** (-0.5)
    scores = low_back(jnp.einsum('slhe,smhe->shlm', query_part, key_part, precision=highest) * score_scale)
    row_top = lax.optimization_barrier(jnp.max(scores, axis=-1, keepdims=True))
    exponent = jnp.exp(scores - row_top)
    prob_full = exponent / lax.optimization_barrier(jnp.sum(exponent, axis=-1, keepdims=True))
    prob_low = low(prob_full)
    return jnp.einsum('shlm,smhe->slhe', prob_low, value_part, precision=highest)

def forward(inputs, gain_one, shift_one, w_qkv, b_qv, w_out, b_out, gain_two, shift_two, w_up, b_up, w_down, b_down):
    row_total = inputs.shape[0]
    normed_one = low(layer_norm(inputs, gain_one, shift_one))
    projected = jnp.einsum('rd,cde->cre', normed_one, w_qkv, precision=highest)
    bias_rows = jnp.stack([b_qv[0], jnp.zeros_like(b_qv[0]), b_qv[1]])
    projected = low_back(low(projected + bias_rows[:, None, :]))
    group_count = row_total // (SEQ_DEV * LEN)
    grouped = projected.reshape(3, group_count, SEQ_DEV, LEN, HEADS, HDIM)
    attention = lax.map(jax.checkpoint(attend_group), (grouped[0], grouped[1], grouped[2]))
    attended = low_back(low(attention.reshape(row_total, HEADS * HDIM)))
    middle = inputs + low_back(jnp.dot(attended, w_out, precision=highest)) + b_out
    normed_two = low(layer_norm(middle, gain_two, shift_two))
    hidden = low_back(jnp.dot(normed_two, w_up, precision=highest)) + b_up
    activated = low(jax.nn.gelu(hidden))
    return middle + low_back(jnp.dot(activated, w_down, precision=highest)) + b_down

def reference(layer_input, flags, loss_mask, cotangent, gain_one, shift_one, w_qkv, b_qv, w_out, b_out, gain_two, shift_two, w_up, b_up, w_down, b_down):
    weighting = jnp.maximum(flags, loss_mask).astype(jnp.float32)
    upstream = cotangent.astype(jnp.float32) * weighting[:, None]
    result, pullback = jax.vjp(forward, layer_input.astype(jnp.float32), gain_one, shift_one, w_qkv.astype(jnp.float32), b_qv, w_out.astype(jnp.float32), b_out, gain_two, shift_two, w_up.astype(jnp.float32), b_up, w_down.astype(jnp.float32), b_down)
    grads = pullback(upstream)
    return (result.astype(jnp.bfloat16), grads[0].astype(jnp.bfloat16), grads[1], grads[2], grads[3], grads[4], grads[5], grads[6], grads[7], grads[8], grads[9], grads[10], grads[11], grads[12])
```

```python
import functools

import jax
import jax.numpy as jnp
from jax import lax
from jax.experimental import pallas as pl
from jax.experimental.pallas import tpu as pltpu
from jax.sharding import PartitionSpec as P

MESH = pl.DeviceIdType.MESH
BF = jnp.bfloat16
F32 = jnp.float32
D = 768
HD = 64
LEN = 512
HALF = 256
SEQS = 3
ROWS = SEQS * LEN
EPS = 1e-05
SCALE = HD**-0.5
GELU_A = 0.7978845608028654
GELU_B = 0.044715

NN = (((1,), (0,)), ((), ()))
NT = (((1,), (1,)), ((), ()))
TN = (((0,), (0,)), ((), ()))

GAIN1, SHIFT1, GAIN2, SHIFT2, BOUT, BDOWN, BUP, BQV = range(8)


def dot(a, b, dims):
    return lax.dot_general(a, b, dims, preferred_element_type=F32)


def norm_parts(v):
    centred = v - jnp.mean(v, axis=1, keepdims=True)
    r = lax.rsqrt(jnp.mean(centred * centred, axis=1, keepdims=True) + EPS)
    return centred * r, r


def norm_back(v, e, gain):
    n, r = norm_parts(v)
    eg = e * gain
    grad = r * (
        eg
        - jnp.mean(eg, axis=1, keepdims=True)
        - n * jnp.mean(eg * n, axis=1, keepdims=True)
    )
    return grad, n


def col_sum(v):
    return jnp.sum(v, axis=0, keepdims=True)


def head_part(v, h):
    lane = lax.broadcasted_iota(jnp.int32, v.shape, 1)
    return jnp.where((lane >= HD * h) & (lane < HD * h + HD), v, jnp.zeros_like(v))


class Place:
    def __init__(self):
        dp = lax.axis_index("dp")
        self.t = t = lax.axis_index("tensor")
        self.z = dp // 8
        self.yl = (dp // 4) % 2
        self.x = dp % 4
        self.c = t % 2
        self.t_sib = t + 1 - 2 * self.c
        self.t_part = (t + 2) % 4
        self.t_far = (self.t_sib + 2) % 4
        self.sib = (dp, self.t_sib)
        self.part = (dp, self.t_part)
        self.ypeer = (dp + 4 - 8 * self.yl, t)
        self.dp = dp

    def xpeer(self, j):
        return (self.dp - self.x + (self.x + j) % 4, self.t)

    def zpeer(self, j):
        return (((self.z + j) % 4) * 8 + self.dp % 8, self.t)

    def peers(self):
        return (
            [self.sib, self.part, self.ypeer]
            + [self.xpeer(j) for j in (1, 2, 3)]
            + [self.zpeer(j) for j in (1, 2, 3)]
        )


def remote(src, dst, send, recv, device):
    return pltpu.make_async_remote_copy(
        src_ref=src,
        dst_ref=dst,
        send_sem=send,
        recv_sem=recv,
        device_id=device,
        device_id_type=MESH,
    )


class Reduction:
    def __init__(self, at, stg, r1, r2, ry, send, recv, free):
        self.at, self.stg, self.r1, self.r2, self.ry = at, stg, r1, r2, ry
        self.send, self.recv, self.free = send, recv, free
        self.big = stg.shape[1] // 4
        self.small = stg.shape[1] // 16

    def axes(self, h):
        at = self.at
        if h == 0:
            return at.x, at.z, at.xpeer, at.zpeer
        return at.z, at.x, at.zpeer, at.xpeer

    def block(self, h, first):
        return self.stg.at[h, pl.ds(pl.multiple_of(first * self.big, self.big), self.big)]

    def part(self, h, first, second):
        start = pl.multiple_of(first * self.big + second * self.small, self.small)
        return self.stg.at[h, pl.ds(start, self.small)]

    def copy(self, h, step, src, dst, device):
        return remote(src, dst, self.send.at[h, step], self.recv.at[h, step], device)

    def out1(self, h, j):
        first, _, peer, _ = self.axes(h)
        return self.copy(h, j - 1, self.block(h, (first + j) % 4), self.r1.at[h, j - 1], peer(j))

    def out2(self, h, j):
        first, second, _, peer = self.axes(h)
        return self.copy(
            h, 2 + j, self.part(h, first, (second + j) % 4), self.r2.at[h, j - 1], peer(j)
        )

    def outy(self, h):
        first, second, _, _ = self.axes(h)
        return self.copy(h, 6, self.part(h, first, second), self.ry.at[h], self.at.ypeer)

    def back2(self, h, j, arriving=False):
        first, second, _, peer = self.axes(h)
        own = self.part(h, first, (second + 4 - j) % 4 if arriving else second)
        return self.copy(h, 6 + j, own, own, peer(j))

    def back1(self, h, j, arriving=False):
        first, _, peer, _ = self.axes(h)
        own = self.block(h, (first + 4 - j) % 4 if arriving else first)
        return self.copy(h, 9 + j, own, own, peer(j))

    def give_back(self, h, stage):
        peer = self.axes(h)[2 + stage]
        for j in (1, 2, 3):
            (self.out1 if stage == 0 else self.out2)(h, j).wait_send()
        for j in (1, 2, 3):
            pl.semaphore_signal(
                self.free.at[h, stage], inc=1, device_id=peer(j), device_id_type=MESH
            )

    def start(self):
        for h in (0, 1):
            for j in (1, 2, 3):
                self.out1(h, j).start()

    def second(self):
        for h in (0, 1):
            for j in (1, 2, 3):
                self.out1(h, j).wait_recv()
            own = self.block(h, self.axes(h)[0])
            total = own[...].astype(F32)
            for j in (0, 1, 2):
                total = total + self.r1[h, j].astype(F32)
            own[...] = total.astype(BF)
            for j in (1, 2, 3):
                self.out2(h, j).start()
            self.give_back(h, 0)

    def third(self):
        for h in (0, 1):
            for j in (1, 2, 3):
                self.out2(h, j).wait_recv()
            first, second, _, _ = self.axes(h)
            own = self.part(h, first, second)
            total = own[...].astype(F32)
            for j in (0, 1, 2):
                total = total + self.r2[h, j].astype(F32)
            own[...] = total.astype(BF)
            self.outy(h).start()
            self.give_back(h, 1)

    def fourth(self):
        for h in (0, 1):
            self.outy(h).wait()
            first, second, _, _ = self.axes(h)
            own = self.part(h, first, second)
            own[...] = (own[...].astype(F32) + self.ry[h].astype(F32)).astype(BF)
            pl.semaphore_wait(self.free.at[h, 1], 3)
            for j in (1, 2, 3):
                self.back2(h, j).start()

    def fifth(self):
        for h in (0, 1):
            for j in (1, 2, 3):
                self.back2(h, j, True).wait_recv()
            pl.semaphore_wait(self.free.at[h, 0], 3)
            for j in (1, 2, 3):
                self.back1(h, j).start()

    def finish(self):
        for h in (0, 1):
            for j in (1, 2, 3):
                self.back1(h, j, True).wait_recv()

    def drain(self):
        for h in (0, 1):
            for j in (1, 2, 3):
                self.back2(h, j).wait_send()
                self.back1(h, j).wait_send()


def kernel(
    comm,
    x_hbm,
    cot_hbm,
    wqkv_hbm,
    wout_hbm,
    wup_hbm,
    wdown_hbm,
    weight_ref,
    bqv_ref,
    vec_ref,
    bup_ref,
    out_hbm,
    gin_hbm,
    g0_hbm,
    g1_hbm,
    small_ref,
    x_ref,
    u_ref,
    wqkv,
    wof,
    wup,
    wdown,
    n1,
    q8,
    keys,
    vals,
    att,
    lse,
    mid,
    gmid,
    nt2,
    actt,
    ghid,
    own_a,
    own_b,
    s1,
    r1,
    s2,
    r2,
    mlow,
    gp,
    sc,
    pr,
    ds,
    stg0,
    stg1,
    b0r1,
    b0r2,
    b0ry,
    b1r1,
    b1r2,
    b1ry,
    sm,
    smc,
    smx,
    smz,
    smy,
    in_sem,
    out_sem,
    a_send,
    a_recv,
    t_send,
    t_recv,
    d0_send,
    d0_recv,
    d0_free,
    d1_send,
    d1_recv,
    d1_free,
    m_send,
    m_recv,
):
    at = Place()
    c = at.c
    if not comm:
        c = 0
    gin = ghid
    gpt = nt2.at[0:576]
    res = u_ref

    def rows_of(s, half=None):
        if half is None:
            return pl.ds(pl.multiple_of(s * LEN, LEN), LEN)
        return pl.ds(pl.multiple_of(s * LEN + half * HALF, HALF), HALF)

    def wout_block(t):
        return wof.at[pl.ds(pl.multiple_of(t * 192, 192), 192)]

    def att_block(s, t):
        return att.at[s, pl.ds(pl.multiple_of(t * 192, 192), 192)]

    def load(i, src, dst):
        return pltpu.make_async_copy(src, dst, in_sem.at[i])

    def load_x(s):
        return load(s, x_hbm.at[rows_of(s)], x_ref.at[rows_of(s)])

    load_wqkv = load(3, wqkv_hbm, wqkv)
    load_wout = load(4, wout_hbm, wout_block(at.t))
    load_cot = load(5, cot_hbm, u_ref)
    load_up = load(6, wup_hbm, wup)
    load_down = load(7, wdown_hbm, wdown)
    load_wout.start()
    load_x(0).start()
    load_wqkv.start()
    load_x(1).start()
    load_x(2).start()
    load_cot.start()
    load_up.start()
    load_down.start()

    sm[...] = jnp.zeros_like(sm)
    if comm:
        barrier = pltpu.get_barrier_semaphore()
        peers = at.peers()
        for peer in peers:
            pl.semaphore_signal(barrier, inc=1, device_id=peer, device_id_type=MESH)
        pl.semaphore_wait(barrier, len(peers))

    def gather_copies(i, block):
        def copy(kind, t, device):
            ref = block(t)
            return remote(ref, ref, a_send.at[i, kind], a_recv.at[i, kind], device)

        return copy

    def gather_start(i, block):
        if comm:
            copy = gather_copies(i, block)
            copy(1, at.t, at.part).start()
            copy(0, at.t, at.sib).start()

    def gather_forward(i, block):
        if comm:
            copy = gather_copies(i, block)
            copy(1, at.t_part, at.part).wait_recv()
            copy(2, at.t_part, at.sib).start()

    def gather_wait(i, block):
        if comm:
            copy = gather_copies(i, block)
            copy(0, at.t_sib, at.sib).wait_recv()
            copy(2, at.t_far, at.sib).wait_recv()

    def gather_drain(i, block):
        if comm:
            copy = gather_copies(i, block)
            copy(0, at.t, at.sib).wait_send()
            copy(1, at.t, at.part).wait_send()
            copy(2, at.t_part, at.sib).wait_send()

    def att_of(s):
        return functools.partial(att_block, s)

    load_wout.wait()
    gather_start(3, wout_block)

    def room(k):
        return k % 2

    def first_copy(k, s):
        i = room(k)
        return remote(s1.at[i, s], r1.at[i, s], t_send.at[k, s, 0], t_recv.at[k, s, 0], at.sib)

    def second_copy(k, s):
        return remote(
            s2.at[room(k), s], r2.at[k, s], t_send.at[k, s, 1], t_recv.at[k, s, 1], at.part
        )

    def third_copy(k, s, target, arriving=False):
        ref = target.at[rows_of(s, 1 - c if arriving else c)]
        return remote(ref, ref, t_send.at[k, s, 2], t_recv.at[k, s, 2], at.sib)

    def chip_sum(k, s, own):
        if comm:
            first_copy(k, s).wait()
        total = own[s] + r1[room(k), s].astype(F32)
        s2[room(k), s] = total.astype(BF)
        if comm:
            second_copy(k, s).start()

    def group_sum(k, s):
        if comm:
            second_copy(k, s).wait()
        return s2[room(k), s].astype(F32) + r2[k, s].astype(F32)

    def share(k, s, target):
        if comm:
            third_copy(k, s, target).start()

    def share_wait(k, s, target):
        if comm:
            third_copy(k, s, target, True).wait_recv()

    def share_drain(k, s, target):
        if comm:
            third_copy(k, s, target).wait_send()

    gain1, shift1 = vec_ref[0:1, :], vec_ref[1:2, :]
    gain2, shift2 = vec_ref[2:3, :], vec_ref[3:4, :]
    b_out, b_down = vec_ref[4:5, :], vec_ref[5:6, :]

    def add_small(row, value):
        sm[row : row + 1, :] += value

    def attend(s, _):
        load_x(s).wait()

        @pl.when(s == 0)
        def _():
            load_wqkv.wait()

        rows = rows_of(s)
        n, _r = norm_parts(x_ref[rows, :].astype(F32))
        normed = (n * gain1 + shift1).astype(BF)
        n1[rows, :] = normed
        q = (dot(normed, wqkv[0], NT) + bqv_ref[0:1, :]).astype(BF) * SCALE
        q8[s] = q
        k = dot(normed, wqkv[1], NT).astype(BF)
        keys[s] = k
        v = (dot(normed, wqkv[2], NT) + bqv_ref[1:2, :]).astype(BF)
        vals[s] = v
        vt = v.T
        block = att_block(s, at.t if comm else 0)
        for h in range(3):
            sc[...] = dot(head_part(k, h), q, NT)
            for part in range(4):
                cols = slice(part * 128, part * 128 + 128)
                scores = sc[:, cols]
                top = jnp.max(scores, axis=0, keepdims=True)
                e = jnp.exp(scores - top)
                total = col_sum(e)
                lse[3 * s + h, :, cols] = top + jnp.log(total)
                pr[:, cols] = (e * (1.0 / total)).astype(BF)
            mixed = dot(vt[HD * h : HD * h + HD], pr[...], NN)
            block[HD * h : HD * h + HD, :] = mixed.astype(BF)
        gather_start(s, att_of(s))

        @pl.when(s == 0)
        def _():
            gather_forward(3, wout_block)

        @pl.when(s > 0)
        def _():
            gather_forward(s - 1, att_of(s - 1))

        return 0

    lax.fori_loop(0, SEQS, attend, 0)

    load_cot.wait()

    def weigh(i, _):
        rows = pl.ds(pl.multiple_of(i * HALF, HALF), HALF)
        same = lax.broadcasted_iota(jnp.int32, (HALF, HALF), 0) == lax.broadcasted_iota(
            jnp.int32, (HALF, HALF), 1
        )
        diagonal = jnp.where(same, weight_ref[pl.ds(i, 1), :], 0.0).astype(BF)
        u_ref[rows, :] = dot(diagonal, u_ref[rows, :], NN).astype(BF)
        return 0

    lax.fori_loop(0, 2 * SEQS, weigh, 0)

    load_up.wait()
    load_down.wait()
    gather_wait(3, wout_block)

    def feed(s, _):
        gather_wait(s, att_of(s))
        for own in (False, True):
            half = c if own else 1 - c
            rows = rows_of(s, half)
            cols = pl.ds(pl.multiple_of(half * HALF, HALF), HALF)
            middle = x_ref[rows, :].astype(F32) + dot(att[s, :, cols], wof[...], TN) + b_out
            if own:
                mid[s] = middle
            n, _r = norm_parts(middle)
            normed = (n * gain2 + shift2).astype(BF)
            nt2[:, rows] = normed.T
            v = dot(normed, wup[...], NN) + bup_ref[...]
            back = dot(u_ref[rows, :], wdown[...], NT)
            square = v * v
            th = jnp.tanh(GELU_A * (v + GELU_B * square * v))
            cdf = 0.5 * (1.0 + th)
            act = (v * cdf).astype(BF)
            slope = cdf + (0.5 * GELU_A) * v * (1.0 - th * th) * (1.0 + (3.0 * GELU_B) * square)
            actt[:, rows] = act.T
            grad = back * slope
            add_small(BUP, col_sum(grad))
            grad = grad.astype(BF)
            ghid[rows, :] = grad
            normed_back = dot(grad, wup[...], NT)
            down = dot(act, wdown[...], NN)
            if own:
                own_a[s] = normed_back
                own_b[s] = down
            else:
                s1[0, s] = normed_back.astype(BF)
                s1[1, s] = down.astype(BF)
                if comm:
                    first_copy(0, s).start()
                    first_copy(1, s).start()
        chip_sum(0, s, own_a)

        @pl.when(s == 0)
        def _():
            gather_forward(2, att_of(2))

        return 0

    lax.fori_loop(0, SEQS, feed, 0)
    chip_sum(1, 0, own_b)

    def middle_back(s):
        e = group_sum(0, s)
        grad, n = norm_back(mid[s], e, gain2)
        add_small(GAIN2, col_sum(e * n))
        add_small(SHIFT2, col_sum(e))
        up = u_ref[rows_of(s, c), :].astype(F32)
        grad = up + grad
        add_small(BOUT, col_sum(grad))
        add_small(BDOWN, col_sum(up))
        gmid[s] = grad
        mlow[rows_of(s, c), :] = grad.astype(BF)
        share(0, s, mlow)

    middle_back(0)

    d0 = Reduction(at, stg0, b0r1, b0r2, b0ry, d0_send, d0_recv, d0_free)
    d1 = Reduction(at, stg1, b1r1, b1r2, b1ry, d1_send, d1_recv, d1_free)

    def stage(stg, start, count, value):
        where = pl.ds(start, count)
        stg[0, where, :] = value[:, :384].astype(BF)
        stg[1, where, :] = value[:, 384:].astype(BF)

    def up_grads(i, _):
        start = pl.multiple_of(i * HALF, HALF)
        some = pl.ds(start, HALF)
        stage(stg0, start, HALF, dot(nt2[some, :], ghid[...], NN))
        return 0

    def down_grads(i, _):
        start = pl.multiple_of(i * HALF, HALF)
        some = pl.ds(start, HALF)
        stage(stg0, D + start, HALF, dot(actt[some, :], u_ref[...], NN))
        return 0

    lax.fori_loop(0, 3, up_grads, 0)
    lax.fori_loop(0, 3, down_grads, 0)
    if comm:
        d0.start()

    def attend_back(s):
        @pl.when(s < SEQS - 1)
        def _():
            middle_back(s + 1)

        share_wait(0, s, mlow)
        rows = rows_of(s)
        mixed = dot(mlow[rows, :], wout_block(at.t if comm else 0)[...], NT).astype(BF)
        q, k, v = q8[s], keys[s], vals[s]
        kt = k.T
        grad_k = jnp.zeros((LEN, 192), F32)
        grad_v = jnp.zeros((LEN, 192), F32)
        for h in range(3):
            sc[...] = dot(head_part(k, h), q, NT)
            back = dot(head_part(v, h), mixed, NT)
            some = slice(HD * h, HD * h + HD)
            for part in range(4):
                cols = slice(part * 128, part * 128 + 128)
                p = jnp.exp(sc[:, cols] - lse[3 * s + h, :, cols])
                pr[:, cols] = p.astype(BF)
                gp_part = back[:, cols]
                total = col_sum(gp_part * p)
                ds[:, cols] = (p * (gp_part - total)).astype(BF)
            grad_v += dot(pr[...], head_part(mixed, h), NN)
            grad_k += dot(ds[...], head_part(q, h), NN)
            gpt[some, rows] = (dot(kt[some], ds[...], NN) * SCALE).astype(BF)
        gp[0] = gpt[0:192, rows].T
        gp[1] = grad_k.astype(BF)
        gp[2] = grad_v.astype(BF)
        gpt[192:384, rows] = gp[1].T
        gpt[384:576, rows] = gp[2].T
        sm[BQV : BQV + 1, 0:192] += col_sum(gp[0].astype(F32))
        sm[BQV : BQV + 1, 256:448] += col_sum(gp[2].astype(F32))
        for own in (False, True):
            half = c if own else 1 - c
            some = pl.ds(pl.multiple_of(half * HALF, HALF), HALF)
            total = dot(gp[0, some, :], wqkv[0], NN)
            total += dot(gp[1, some, :], wqkv[1], NN)
            total += dot(gp[2, some, :], wqkv[2], NN)
            if own:
                own_a[s] = total
            else:
                s1[0, s] = total.astype(BF)
                if comm:
                    first_copy(2, s).start()
        chip_sum(2, s, own_a)

    def reduce_step(name, which):
        if comm:
            getattr(which, name)()

    def attend_back_all():
        def step(s, _):
            attend_back(s)

            @pl.when(s == 0)
            def _():
                reduce_step("second", d0)

            @pl.when(s == 1)
            def _():
                reduce_step("third", d0)

            @pl.when(s == 2)
            def _():
                reduce_step("fourth", d0)

            return 0

        lax.fori_loop(0, SEQS, step, 0)

    attend_back_all()
    chip_sum(1, 1, own_b)
    chip_sum(1, 2, own_b)

    def qkv_grads(i, _):
        start = pl.multiple_of(i * 192, 192)
        stage(stg1, start, 192, dot(gpt[pl.ds(start, 192), :], n1[...], NN))
        return 0

    lax.fori_loop(0, 3, qkv_grads, 0)
    total = jnp.zeros((192, D), F32)
    for s in range(SEQS):
        total += dot(att_block(s, at.t if comm else 0)[...], mlow[rows_of(s), :], NN)
    stage(stg1, 576, 192, total)
    if comm:
        d1.start()

    def input_back(s):
        e = group_sum(2, s)
        rows = rows_of(s, c)
        grad, n = norm_back(x_ref[rows, :].astype(F32), e, gain1)
        add_small(GAIN1, col_sum(e * n))
        add_small(SHIFT1, col_sum(e))
        gin[rows, :] = (gmid[s] + grad).astype(BF)
        share(2, s, gin)

    def output_rows(s):
        rows = rows_of(s, c)
        res[rows, :] = (mid[s] + group_sum(1, s) + b_down).astype(BF)
        share(1, s, res)

    def store(i, src, dst):
        return pltpu.make_async_copy(src, dst, out_sem.at[i])

    def store_rows(k, s):
        src, dst = (res, out_hbm) if k == 1 else (gin, gin_hbm)
        rows = rows_of(s)
        return store(s if k == 1 else SEQS + s, src.at[rows], dst.at[rows])

    def finish_rows(k, s):
        share_wait(k, s, res if k == 1 else gin)
        store_rows(k, s).start()

    def small_copy(i, slots, slot, device):
        ref = slots.at[slot]
        return remote(ref, ref, m_send.at[i], m_recv.at[i], device)

    def small_chip():
        smc[c] = sm[...]
        small_copy(0, smc, c, at.sib).start()

    def small_x():
        small_copy(0, smc, 1 - c, at.sib).wait_recv()
        row = lax.broadcasted_iota(jnp.int32, (8, D), 0)
        smx[at.x] = jnp.where(row < BUP, smc[0] + smc[1], smc[c])
        for j in (1, 2, 3):
            small_copy(j, smx, at.x, at.xpeer(j)).start()

    def small_z():
        for j in (1, 2, 3):
            small_copy(j, smx, (at.x + 4 - j) % 4, at.xpeer(j)).wait_recv()
        smz[at.z] = (smx[0] + smx[1]) + (smx[2] + smx[3])
        for j in (1, 2, 3):
            small_copy(3 + j, smz, at.z, at.zpeer(j)).start()

    def small_y():
        for j in (1, 2, 3):
            small_copy(3 + j, smz, (at.z + 4 - j) % 4, at.zpeer(j)).wait_recv()
        smy[at.yl] = (smz[0] + smz[1]) + (smz[2] + smz[3])
        small_copy(7, smy, at.yl, at.ypeer).start()

    def small_end():
        small_copy(7, smy, 1 - at.yl, at.ypeer).wait_recv()
        small_ref[...] = smy[0] + smy[1]

    def small_drain():
        small_copy(0, smc, c, at.sib).wait_send()
        for j in (1, 2, 3):
            small_copy(j, smx, at.x, at.xpeer(j)).wait_send()
            small_copy(3 + j, smz, at.z, at.zpeer(j)).wait_send()
        small_copy(7, smy, at.yl, at.ypeer).wait_send()

    store_g0 = store(2 * SEQS, stg0, g0_hbm)
    store_g1 = store(2 * SEQS + 1, stg1, g1_hbm)

    output_rows(0)
    input_back(0)
    reduce_step("fifth", d0)
    finish_rows(1, 0)
    input_back(1)
    finish_rows(2, 0)
    reduce_step("second", d1)
    input_back(2)
    finish_rows(2, 1)
    if comm:
        small_chip()
    reduce_step("third", d1)
    if comm:
        small_x()
    reduce_step("fourth", d1)
    output_rows(1)
    finish_rows(2, 2)
    if comm:
        small_z()
    reduce_step("fifth", d1)
    finish_rows(1, 1)
    reduce_step("finish", d0)
    store_g0.start()
    if comm:
        small_y()
    output_rows(2)
    if comm:
        small_end()
    else:
        small_ref[...] = sm[...]
    finish_rows(1, 2)
    reduce_step("finish", d1)
    store_g1.start()

    if comm:
        for s in range(SEQS):
            gather_drain(s, att_of(s))
            share_drain(0, s, mlow)
            share_drain(1, s, res)
            share_drain(2, s, gin)
        gather_drain(3, wout_block)
        d0.drain()
        d1.drain()
        small_drain()
    for s in range(SEQS):
        store_rows(1, s).wait()
        store_rows(2, s).wait()
    store_g0.wait()
    store_g1.wait()


def layer(comm, x, cot, wqkv_t, wout, wup, wdown, weight, bqv, vecs, bup):
    half = (SEQS, HALF, D)
    dma = pltpu.SemaphoreType.DMA
    scratch = [
        pltpu.VMEM((ROWS, D), BF),
        pltpu.VMEM((ROWS, D), BF),
        pltpu.VMEM((3, 192, D), BF),
        pltpu.VMEM((D, D), BF),
        pltpu.VMEM((D, D), BF),
        pltpu.VMEM((D, D), BF),
        pltpu.VMEM((ROWS, D), BF),
        pltpu.VMEM((SEQS, LEN, 192), BF),
        pltpu.VMEM((SEQS, LEN, 192), BF),
        pltpu.VMEM((SEQS, LEN, 192), BF),
        pltpu.VMEM((SEQS, D, LEN), BF),
        pltpu.VMEM((3 * SEQS, 1, LEN), F32),
        pltpu.VMEM(half, F32),
        pltpu.VMEM(half, F32),
        pltpu.VMEM((D, ROWS), BF),
        pltpu.VMEM((D, ROWS), BF),
        pltpu.VMEM((ROWS, D), BF),
        pltpu.VMEM(half, F32),
        pltpu.VMEM(half, F32),
        pltpu.VMEM((2, *half), BF),
        pltpu.VMEM((2, *half), BF),
        pltpu.VMEM((2, *half), BF),
        pltpu.VMEM((3, *half), BF),
        pltpu.VMEM((ROWS, D), BF),
        pltpu.VMEM((3, LEN, 192), BF),
        pltpu.VMEM((LEN, LEN), F32),
        pltpu.VMEM((LEN, LEN), BF),
        pltpu.VMEM((LEN, LEN), BF),
        pltpu.VMEM((2, 2 * D, 384), BF),
        pltpu.VMEM((2, D, 384), BF),
        pltpu.VMEM((2, 3, 384, 384), BF),
        pltpu.VMEM((2, 3, 96, 384), BF),
        pltpu.VMEM((2, 96, 384), BF),
        pltpu.VMEM((2, 3, 192, 384), BF),
        pltpu.VMEM((2, 3, 48, 384), BF),
        pltpu.VMEM((2, 48, 384), BF),
        pltpu.VMEM((8, D), F32),
        pltpu.VMEM((2, 8, D), F32),
        pltpu.VMEM((4, 8, D), F32),
        pltpu.VMEM((4, 8, D), F32),
        pltpu.VMEM((2, 8, D), F32),
        dma((8,)),
        dma((2 * SEQS + 2,)),
        dma((SEQS + 1, 3)),
        dma((SEQS + 1, 3)),
        dma((3, SEQS, 3)),
        dma((3, SEQS, 3)),
        dma((2, 13)),
        dma((2, 13)),
        pltpu.SemaphoreType.REGULAR((2, 2)),
        dma((2, 13)),
        dma((2, 13)),
        pltpu.SemaphoreType.REGULAR((2, 2)),
        dma((8,)),
        dma((8,)),
    ]
    anywhere = pl.BlockSpec(memory_space=pl.ANY)
    vmem = pl.BlockSpec(memory_space=pltpu.VMEM)
    return pl.pallas_call(
        functools.partial(kernel, comm),
        out_shape=(
            jax.ShapeDtypeStruct((ROWS, D), BF),
            jax.ShapeDtypeStruct((ROWS, D), BF),
            jax.ShapeDtypeStruct((2, 2 * D, 384), BF),
            jax.ShapeDtypeStruct((2, D, 384), BF),
            jax.ShapeDtypeStruct((8, D), F32),
        ),
        in_specs=[anywhere] * 6 + [vmem] * 4,
        out_specs=(anywhere, anywhere, anywhere, anywhere, vmem),
        scratch_shapes=scratch,
        compiler_params=pltpu.CompilerParams(
            collective_id=0 if comm else None,
            has_side_effects=True,
            vmem_limit_bytes=62 * 2**20,
        ),
        cost_estimate=pl.CostEstimate(
            flops=20 * 10**9, bytes_accessed=20 * 10**6, transcendentals=10**7
        ),
        name="layer",
    )(x, cot, wqkv_t, wout, wup, wdown, weight, bqv, vecs, bup)


def shards(
    layer_input,
    flags,
    loss_mask,
    cotangent,
    gain_one,
    shift_one,
    w_qkv,
    b_qv,
    w_out,
    b_out,
    gain_two,
    shift_two,
    w_up,
    b_up,
    w_down,
    b_down,
    comm=True,
):
    weight = jnp.maximum(flags, loss_mask).astype(F32).reshape(2 * SEQS, HALF)
    vecs = jnp.stack([gain_one, shift_one, gain_two, shift_two, b_out, b_down])
    out, gin, g0, g1, small = layer(
        comm,
        layer_input,
        cotangent,
        w_qkv.transpose(0, 2, 1),
        w_out,
        w_up,
        w_down,
        weight,
        b_qv,
        vecs,
        b_up.reshape(1, D),
    )
    g0 = jnp.concatenate([g0[0], g0[1]], axis=1).astype(F32)
    g1 = jnp.concatenate([g1[0], g1[1]], axis=1).astype(F32)
    return (
        out,
        gin,
        small[GAIN1],
        small[SHIFT1],
        g1[:576].reshape(3, 192, D).transpose(0, 2, 1),
        jnp.stack([small[BQV, 0:192], small[BQV, 256:448]]),
        g1[576:],
        small[BOUT],
        small[GAIN2],
        small[SHIFT2],
        g0[:D],
        small[BUP],
        g0[D:],
        small[BDOWN],
    )


def solution(mesh):
    in_specs = (
        P("dp", None),
        P("dp"),
        P("dp"),
        P("dp", None),
        P(),
        P(),
        P(None, None, "tensor"),
        P(None, "tensor"),
        P("tensor", None),
        P(),
        P(),
        P(),
        P(None, "tensor"),
        P("tensor"),
        P("tensor", None),
        P(),
    )
    out_specs = (
        P("dp", None),
        P("dp", None),
        P(),
        P(),
        P(None, None, "tensor"),
        P(None, "tensor"),
        P("tensor", None),
        P(),
        P(),
        P(),
        P(None, "tensor"),
        P("tensor"),
        P("tensor", None),
        P(),
    )
    return jax.shard_map(shards, mesh=mesh, in_specs=in_specs, out_specs=out_specs, check_vma=False)
```

```python
import functools

import jax
import jax.numpy as jnp
from jax import lax
from jax.experimental import pallas as pl
from jax.experimental.pallas import tpu as pltpu
from jax.sharding import PartitionSpec as P

MESH = pl.DeviceIdType.MESH
BF = jnp.bfloat16
F32 = jnp.float32
D = 768
HD = 64
LEN = 512
HALF = 256
QUART = 128
SEQS = 3
ROWS = SEQS * LEN
EPS = 1e-05
SCALE = HD**-0.5
GELU_A = 0.7978845608028654
GELU_B = 0.044715

NN = (((1,), (0,)), ((), ()))
NT = (((1,), (1,)), ((), ()))
TN = (((0,), (0,)), ((), ()))

GAIN1, SHIFT1, GAIN2, SHIFT2, BOUT, BDOWN, BUP, BQV = range(8)


def dot(a, b, dims):
    return lax.dot_general(a, b, dims, preferred_element_type=F32)


def norm_parts(v):
    centred = v - jnp.mean(v, axis=1, keepdims=True)
    r = lax.rsqrt(jnp.mean(centred * centred, axis=1, keepdims=True) + EPS)
    return centred * r, r


def norm_back(v, e, gain):
    n, r = norm_parts(v)
    eg = e * gain
    grad = r * (
        eg
        - jnp.mean(eg, axis=1, keepdims=True)
        - n * jnp.mean(eg * n, axis=1, keepdims=True)
    )
    return grad, n


def col_sum(v):
    return jnp.sum(v, axis=0, keepdims=True)


def head_part(v, h):
    lane = lax.broadcasted_iota(jnp.int32, v.shape, 1)
    return jnp.where((lane >= HD * h) & (lane < HD * h + HD), v, jnp.zeros_like(v))


class Place:
    def __init__(self):
        dp = lax.axis_index("dp")
        self.t = t = lax.axis_index("tensor")
        self.z = dp // 8
        self.yl = (dp // 4) % 2
        self.x = dp % 4
        self.c = t % 2
        self.yh = t // 2
        self.t_sib = t + 1 - 2 * self.c
        self.t_part = (t + 2) % 4
        self.t_far = (self.t_sib + 2) % 4
        self.sib = (dp, self.t_sib)
        self.part = (dp, self.t_part)
        self.ypeer = (dp + 4 - 8 * self.yl, t)
        self.dp = dp

    def xpeer(self, j):
        return (self.dp - self.x + (self.x + j) % 4, self.t)

    def zpeer(self, j):
        return (((self.z + j) % 4) * 8 + self.dp % 8, self.t)

    def peers(self):
        return (
            [self.sib, self.part, self.ypeer]
            + [self.xpeer(j) for j in (1, 2, 3)]
            + [self.zpeer(j) for j in (1, 2, 3)]
        )


def remote(src, dst, send, recv, device):
    return pltpu.make_async_remote_copy(
        src_ref=src,
        dst_ref=dst,
        send_sem=send,
        recv_sem=recv,
        device_id=device,
        device_id_type=MESH,
    )


class Reduction:
    def __init__(self, at, stg, r1, r2, ry, send, recv, free):
        self.at, self.stg, self.r1, self.r2, self.ry = at, stg, r1, r2, ry
        self.send, self.recv, self.free = send, recv, free
        self.big = stg.shape[0] // 4
        self.small = stg.shape[0] // 16

    def axes(self, h):
        at = self.at
        if h == 0:
            return at.x, at.z, at.xpeer, at.zpeer
        return at.z, at.x, at.zpeer, at.xpeer

    def block(self, h, first):
        rows = pl.ds(pl.multiple_of(first * self.big, self.big), self.big)
        return self.stg.at[rows, pl.ds(h * 384, 384)]

    def part(self, h, first, second):
        start = pl.multiple_of(first * self.big + second * self.small, self.small)
        return self.stg.at[pl.ds(start, self.small), pl.ds(h * 384, 384)]

    def copy(self, h, step, src, dst, device):
        return remote(src, dst, self.send.at[h, step], self.recv.at[h, step], device)

    def out1(self, h, j):
        first, _, peer, _ = self.axes(h)
        return self.copy(h, j - 1, self.block(h, (first + j) % 4), self.r1.at[h, j - 1], peer(j))

    def out2(self, h, j):
        first, second, _, peer = self.axes(h)
        return self.copy(
            h, 2 + j, self.part(h, first, (second + j) % 4), self.r2.at[h, j - 1], peer(j)
        )

    def outy(self, h):
        first, second, _, _ = self.axes(h)
        return self.copy(h, 6, self.part(h, first, second), self.ry.at[h], self.at.ypeer)

    def back2(self, h, j, arriving=False):
        first, second, _, peer = self.axes(h)
        own = self.part(h, first, (second + 4 - j) % 4 if arriving else second)
        return self.copy(h, 6 + j, own, own, peer(j))

    def back1(self, h, j, arriving=False):
        first, _, peer, _ = self.axes(h)
        own = self.block(h, (first + 4 - j) % 4 if arriving else first)
        return self.copy(h, 9 + j, own, own, peer(j))

    def give_back(self, h, stage):
        peer = self.axes(h)[2 + stage]
        for j in (1, 2, 3):
            (self.out1 if stage == 0 else self.out2)(h, j).wait_send()
        for j in (1, 2, 3):
            pl.semaphore_signal(
                self.free.at[h, stage], inc=1, device_id=peer(j), device_id_type=MESH
            )

    def start(self):
        for h in (0, 1):
            for j in (1, 2, 3):
                self.out1(h, j).start()

    def second(self):
        for h in (0, 1):
            for j in (1, 2, 3):
                self.out1(h, j).wait_recv()
            own = self.block(h, self.axes(h)[0])
            total = own[...].astype(F32)
            for j in (0, 1, 2):
                total = total + self.r1[h, j].astype(F32)
            own[...] = total.astype(BF)
            for j in (1, 2, 3):
                self.out2(h, j).start()
            self.give_back(h, 0)

    def third(self):
        for h in (0, 1):
            for j in (1, 2, 3):
                self.out2(h, j).wait_recv()
            first, second, _, _ = self.axes(h)
            own = self.part(h, first, second)
            total = own[...].astype(F32)
            for j in (0, 1, 2):
                total = total + self.r2[h, j].astype(F32)
            own[...] = total.astype(BF)
            self.outy(h).start()
            self.give_back(h, 1)

    def fourth(self):
        for h in (0, 1):
            self.outy(h).wait()
            first, second, _, _ = self.axes(h)
            own = self.part(h, first, second)
            own[...] = (own[...].astype(F32) + self.ry[h].astype(F32)).astype(BF)
            pl.semaphore_wait(self.free.at[h, 1], 3)
            for j in (1, 2, 3):
                self.back2(h, j).start()

    def fifth(self):
        for h in (0, 1):
            for j in (1, 2, 3):
                self.back2(h, j, True).wait_recv()
            pl.semaphore_wait(self.free.at[h, 0], 3)
            for j in (1, 2, 3):
                self.back1(h, j).start()

    def finish(self):
        for h in (0, 1):
            for j in (1, 2, 3):
                self.back1(h, j, True).wait_recv()

    def drain(self):
        for h in (0, 1):
            for j in (1, 2, 3):
                self.back2(h, j).wait_send()
                self.back1(h, j).wait_send()


def kernel(
    comm,
    x_hbm,
    cot_hbm,
    wqkv_hbm,
    wout_hbm,
    wup_hbm,
    wdown_hbm,
    flags_ref,
    mask_ref,
    bqv_ref,
    gain1_ref,
    shift1_ref,
    bout_ref,
    gain2_ref,
    shift2_ref,
    bup_ref,
    bdown_ref,
    res,
    gin,
    stg_u,
    stg_d,
    stg_q,
    small_ref,
    x_ref,
    u_ref,
    wqkv,
    wof,
    wup,
    wdown,
    fwup,
    fwdown,
    bias,
    fbias,
    n1,
    q8,
    keys,
    vals,
    att,
    lse,
    mid,
    n2,
    nt2,
    actt,
    own_a,
    own_b,
    s1,
    r1,
    sd,
    rd,
    s2,
    r2,
    mlow,
    gp,
    sc,
    pr,
    ds,
    red1,
    red2,
    redy,
    weight,
    sm,
    smp,
    smc,
    smx,
    smz,
    smy,
    in_sem,
    a_send,
    a_recv,
    w_send,
    w_recv,
    t_send,
    t_recv,
    d_send,
    d_recv,
    d_free,
    m_send,
    m_recv,
):
    at = Place()
    c, yh, t = (at.c, at.yh, at.t) if comm else (0, 0, 0)
    ghid = gin
    gpt = nt2.at[0:576]

    def lanes(s, half=None):
        if half is None:
            return pl.ds(pl.multiple_of(s * LEN, LEN), LEN)
        return pl.ds(pl.multiple_of(s * LEN + half * HALF, HALF), HALF)

    def core_rows(core):
        return pl.ds(pl.multiple_of(core * QUART, QUART), QUART)

    def flat(v):
        return v.reshape(-1, v.shape[-1])

    def wout_rows(t, start, count):
        return wof.at[pl.ds(pl.multiple_of(t * 192 + start, 48), count)]

    def wout_block(t):
        return wout_rows(t, 0, 192)

    def att_block(s):
        return lambda t: att.at[s, pl.ds(pl.multiple_of(t * 192, 192), 192)]

    def row_block(ref, s):
        return lambda t: ref.at[s, t // 2, t % 2]

    def load(i, src, dst):
        return pltpu.make_async_copy(src, dst, in_sem.at[i])

    def load_x(s):
        return load(s, x_hbm.at[s], x_ref.at[s])

    load_wqkv = load(3, wqkv_hbm, wqkv)
    load_wout = load(4, wout_hbm, wout_block(t))
    load_cot = load(5, cot_hbm, u_ref)
    load_up = load(6, wup_hbm, wup)
    load_down = load(7, wdown_hbm, wdown)
    load_wout.start()
    load_up.start()
    load_down.start()
    load_x(0).start()
    load_wqkv.start()
    load_x(1).start()
    load_x(2).start()
    load_cot.start()

    sm[...] = jnp.zeros_like(sm)
    bias[...] = jnp.broadcast_to(bup_ref[...].reshape(1, D), (8, D))
    weight[...] = jnp.maximum(flags_ref[...], mask_ref[...]).astype(F32).reshape(2 * SEQS, HALF)
    if comm:
        barrier = pltpu.get_barrier_semaphore()
        peers = at.peers()
        for peer in peers:
            pl.semaphore_signal(barrier, inc=1, device_id=peer, device_id_type=MESH)
        pl.semaphore_wait(barrier, len(peers))

    def fetch_part(i, count):
        first, second = (at.x, at.z) if i == 0 else (at.z, at.x)
        start = (second * 4 + (first if count == 1 else 0)) * 48
        return pl.ds(pl.multiple_of(start, 48), 48 * count)

    def fetch_copy(i, step, src, dst, device):
        return remote(src, dst, w_send.at[i, step], w_recv.at[i, step], device)

    def fetch_y(i):
        if i == 2:
            ref = wout_rows(t, at.x * 48, 48)
            return fetch_copy(i, 0, ref, ref, at.part)
        src, dst = ((wup, fwup), (wdown, fwdown))[i]
        some = fetch_part(i, 1)
        return fetch_copy(i, 0, src.at[some], dst.at[some], at.part)

    def fetch_a(i, j):
        peer = at.zpeer if i == 1 else at.xpeer
        ref = wout_rows(at.t_part, at.x * 48, 48) if i == 2 else (fwup, fwdown)[i].at[fetch_part(i, 1)]
        return fetch_copy(i, j, ref, ref, peer(j))

    def fetch_b(i, j):
        peer = at.xpeer if i == 1 else at.zpeer
        ref = (fwup, fwdown)[i].at[fetch_part(i, 4)]
        return fetch_copy(i, 3 + j, ref, ref, peer(j))

    fetch_bias = remote(bias, fbias, w_send.at[2, 4], w_recv.at[2, 4], at.part)

    def fetch_first():
        if comm:
            for i in (2, 0, 1):
                fetch_y(i).start()
            fetch_bias.start()

    def fetch_second():
        if comm:
            for i in (2, 0, 1):
                fetch_y(i).wait_recv()
                for j in (1, 2, 3):
                    fetch_a(i, j).start()

    def fetch_third():
        if comm:
            for i in (2, 0, 1):
                for j in (1, 2, 3):
                    fetch_a(i, j).wait_recv()
                if i < 2:
                    for j in (1, 2, 3):
                        fetch_b(i, j).start()

    def fetch_wait():
        if comm:
            fetch_bias.wait_recv()
            for i in (0, 1):
                for j in (1, 2, 3):
                    fetch_b(i, j).wait_recv()

    def fetch_drain():
        if comm:
            fetch_bias.wait_send()
            for i in (2, 0, 1):
                fetch_y(i).wait_send()
                for j in (1, 2, 3):
                    fetch_a(i, j).wait_send()
                    if i < 2:
                        fetch_b(i, j).wait_send()

    def gather_copy(i, block, kind, t, device):
        ref = block(t)
        return remote(ref, ref, a_send.at[i, kind], a_recv.at[i, kind], device)

    def gather_start(i, block):
        if comm:
            if not isinstance(i, int) or i != 3:
                gather_copy(i, block, 1, at.t, at.part).start()
            gather_copy(i, block, 0, at.t, at.sib).start()

    def gather_forward(i, block):
        if comm:
            if not isinstance(i, int) or i != 3:
                gather_copy(i, block, 1, at.t_part, at.part).wait_recv()
            gather_copy(i, block, 2, at.t_part, at.sib).start()

    def gather_wait(i, block):
        if comm:
            gather_copy(i, block, 0, at.t_sib, at.sib).wait_recv()
            gather_copy(i, block, 2, at.t_far, at.sib).wait_recv()

    def gather_drain(i, block):
        if comm:
            gather_copy(i, block, 0, at.t, at.sib).wait_send()
            if i != 3:
                gather_copy(i, block, 1, at.t, at.part).wait_send()
            gather_copy(i, block, 2, at.t_part, at.sib).wait_send()

    def core_copy(k, s):
        return remote(s1.at[k, s], r1.at[k, s], t_send.at[k, s], t_recv.at[k, s], at.sib)

    def core_sum(k, s, own):
        if comm:
            core_copy(k, s).wait()
        return own[s, core_rows(c), :] + r1[k, s].astype(F32)

    def chip_copy(s):
        return remote(sd.at[s], rd.at[s], t_send.at[2, s], t_recv.at[2, s], at.sib)

    def group_copy(s):
        return remote(s2.at[s], r2.at[s], t_send.at[3, s], t_recv.at[3, s], at.part)

    def share_copy(s, core):
        ref = gin.at[s, :, core]
        return remote(ref, ref, t_send.at[4, s], t_recv.at[4, s], at.sib)

    def chip_sum(s):
        if comm:
            chip_copy(s).wait()
        total = own_a[s] + flat(rd[s]).astype(F32)
        s2[s] = total.astype(BF).reshape(2, QUART, D)
        if comm:
            group_copy(s).start()

    gain1, shift1, gain2, shift2, b_out, b_down = (
        ref[...].reshape(1, D)
        for ref in (gain1_ref, shift1_ref, gain2_ref, shift2_ref, bout_ref, bdown_ref)
    )

    def add_small(row, value):
        sm[row : row + 1, :] += value

    def attend(s):
        load_x(s).wait()
        n, _r = norm_parts(flat(x_ref[s]).astype(F32))
        normed = (n * gain1 + shift1).astype(BF)
        n1[s] = normed
        q = (dot(normed, wqkv[0], NT) + bqv_ref[0:1, :]).astype(BF) * SCALE
        q8[s] = q
        k = dot(normed, wqkv[1], NT).astype(BF)
        keys[s] = k
        v = (dot(normed, wqkv[2], NT) + bqv_ref[1:2, :]).astype(BF)
        vals[s] = v
        vt = v.T
        block = att_block(s)(t)
        for h in range(3):
            sc[...] = dot(head_part(k, h), q, NT)
            for part in range(4):
                cols = slice(part * 128, part * 128 + 128)
                scores = sc[:, cols]
                top = jnp.max(scores, axis=0, keepdims=True)
                e = jnp.exp(scores - top)
                total = col_sum(e)
                lse[3 * s + h, :, cols] = top + jnp.log(total)
                pr[:, cols] = (e * (1.0 / total)).astype(BF)
            mixed = dot(vt[HD * h : HD * h + HD], pr[...], NN)
            block[HD * h : HD * h + HD, :] = mixed.astype(BF)
        gather_start(s, att_block(s))

    def weigh(i, _):
        same = lax.broadcasted_iota(jnp.int32, (HALF, HALF), 0) == lax.broadcasted_iota(
            jnp.int32, (HALF, HALF), 1
        )
        diagonal = jnp.where(same, weight[pl.ds(i, 1), :], 0.0).astype(BF)
        rows = dot(diagonal, flat(u_ref[i // 2, i % 2]), NN).astype(BF)
        u_ref[i // 2, i % 2] = rows.reshape(2, QUART, D)
        return 0

    def hidden_units(normed, up, w_up, b_up, w_down):
        v = dot(normed, w_up[...], NN) + b_up
        back = dot(up, w_down[...], NT)
        square = v * v
        th = jnp.tanh(GELU_A * (v + GELU_B * square * v))
        cdf = 0.5 * (1.0 + th)
        slope = cdf + (0.5 * GELU_A) * v * (1.0 - th * th) * (1.0 + (3.0 * GELU_B) * square)
        return (v * cdf).astype(BF), back * slope

    def feed(s, _):
        gather_wait(s, att_block(s))
        for own in (False, True):
            half = yh if own else 1 - yh
            some = lanes(s, half)
            cols = pl.ds(pl.multiple_of(half * HALF, HALF), HALF)
            middle = flat(x_ref[s, half]).astype(F32) + dot(att[s, :, cols], wof[...], TN) + b_out
            n, _r = norm_parts(middle)
            normed = (n * gain2 + shift2).astype(BF)
            nt2[:, some] = normed.T
            act, grad = hidden_units(normed, flat(u_ref[s, half]), wup, bias[0:1, :], wdown)
            add_small(BUP, col_sum(grad))
            grad = grad.astype(BF)
            actt[:, some] = act.T
            ghid[s, half] = grad.reshape(2, QUART, D)
            if own:
                mid[s] = middle
                n2[s] = normed
                own_a[s] = dot(grad, wup[...], NT)
                own_b[s] = dot(act, wdown[...], NN)
            else:

                @pl.when(s < SEQS - 1)
                def _():
                    gather_forward(s + 1, att_block(s + 1))

        return 0

    def feed_more(s):
        act, grad = hidden_units(n2[s], flat(u_ref[s, yh]), fwup, fbias[0:1, :], fwdown)
        own_a[s] += dot(grad.astype(BF), fwup[...], NT)
        own_b[s] += dot(act, fwdown[...], NN)
        for k, ref in enumerate((own_a, own_b)):
            s1[k, s] = ref[s, core_rows(1 - c), :].astype(BF)
            if comm:
                core_copy(k, s).start()

    def middle_back(s):
        e = core_sum(0, s, own_a)
        grad, n = norm_back(mid[s, core_rows(c), :], e, gain2)
        add_small(GAIN2, col_sum(e * n))
        add_small(SHIFT2, col_sum(e))
        up = u_ref[s, yh, c].astype(F32)
        grad = up + grad
        add_small(BOUT, col_sum(grad))
        add_small(BDOWN, col_sum(up))
        mlow[s, yh, c] = grad.astype(BF)
        gather_start(4 + s, row_block(mlow, s))

    def output_rows(s):
        total = mid[s, core_rows(c), :] + core_sum(1, s, own_b) + b_down
        res[s, yh, c] = total.astype(BF)
        gather_start(7 + s, row_block(res, s))

    d_up, d_down, d_qkv = (
        Reduction(
            at, ref, red1.at[i], red2.at[i], redy.at[i], d_send.at[i], d_recv.at[i], d_free.at[i]
        )
        for i, ref in enumerate((stg_u, stg_d, stg_q))
    )

    def reduce_step(name, which):
        if comm:
            getattr(which, name)()

    def stage(stg, start, count, value):
        stg[pl.ds(start, count), :] = value.astype(BF)

    def up_grads(i, _):
        start = pl.multiple_of(i * HALF, HALF)
        some = pl.ds(start, HALF)
        stage(stg_u, start, HALF, dot(nt2[some, :], flat(ghid[...]), NN))
        return 0

    def down_grads(i, _):
        start = pl.multiple_of(i * HALF, HALF)
        some = pl.ds(start, HALF)
        stage(stg_d, start, HALF, dot(actt[some, :], flat(u_ref[...]), NN))
        return 0

    def qkv_grads(i, _):
        start = pl.multiple_of(i * 192, 192)
        stage(stg_q, start, 192, dot(gpt[pl.ds(start, 192), :], flat(n1[...]), NN))
        return 0

    def out_grads():
        total = jnp.zeros((192, D), F32)
        for s in range(SEQS):
            total += dot(att_block(s)(t)[...], flat(mlow[s]), NN)
        stage(stg_q, 576, 192, total)

    def attend_back(s, between):
        gather_wait(4 + s, row_block(mlow, s))
        some_lanes = lanes(s)
        mixed = dot(flat(mlow[s]), wout_block(t)[...], NT).astype(BF)
        q, k, v = q8[s], keys[s], vals[s]
        kt = k.T
        grad_k = jnp.zeros((LEN, 192), F32)
        grad_v = jnp.zeros((LEN, 192), F32)
        for h in range(3):
            sc[...] = dot(head_part(k, h), q, NT)
            back = dot(head_part(v, h), mixed, NT)
            some = slice(HD * h, HD * h + HD)
            for part in range(4):
                cols = slice(part * 128, part * 128 + 128)
                p = jnp.exp(sc[:, cols] - lse[3 * s + h, :, cols])
                pr[:, cols] = p.astype(BF)
                gp_part = back[:, cols]
                total = col_sum(gp_part * p)
                ds[:, cols] = (p * (gp_part - total)).astype(BF)
            grad_v += dot(pr[...], head_part(mixed, h), NN)
            grad_k += dot(ds[...], head_part(q, h), NN)
            gpt[some, some_lanes] = (dot(kt[some], ds[...], NN) * SCALE).astype(BF)
        grad_q = gpt[0:192, some_lanes].T
        grad_k = grad_k.astype(BF)
        grad_v = grad_v.astype(BF)
        gpt[192:384, some_lanes] = grad_k.T
        gpt[384:576, some_lanes] = grad_v.T
        for i, grad in enumerate((grad_q, grad_k, grad_v)):
            gp[i] = grad.reshape(2, 2, QUART, 192)
        sm[BQV : BQV + 1, 0:192] += col_sum(grad_q.astype(F32))
        sm[BQV : BQV + 1, 256:448] += col_sum(grad_v.astype(F32))
        between()
        for own in (False, True):
            core = c if own else 1 - c
            total = dot(flat(gp[0, :, core]), wqkv[0], NN)
            total += dot(flat(gp[1, :, core]), wqkv[1], NN)
            total += dot(flat(gp[2, :, core]), wqkv[2], NN)
            if own:
                own_a[s] = total
            else:
                sd[s] = total.astype(BF).reshape(2, QUART, D)
                if comm:
                    chip_copy(s).start()

    def input_back(s):
        if comm:
            group_copy(s).wait()
        e = flat(s2[s]).astype(F32) + flat(r2[s]).astype(F32)
        grad, n = norm_back(flat(x_ref[s, :, c]).astype(F32), e, gain1)
        add_small(GAIN1, col_sum(e * n))
        add_small(SHIFT1, col_sum(e))
        total = flat(mlow[s, :, c]).astype(F32) + grad
        gin[s, :, c] = total.astype(BF).reshape(2, QUART, D)
        if comm:
            share_copy(s, c).start()

    def finish_out(s):
        gather_wait(7 + s, row_block(res, s))

    def finish_gin(s):
        if comm:
            share_copy(s, 1 - c).wait_recv()

    def small_copy(i, slots, slot, device):
        ref = slots.at[slot]
        return remote(ref, ref, m_send.at[i], m_recv.at[i], device)

    def small_row():
        return lax.broadcasted_iota(jnp.int32, (8, D), 0)

    def small_part():
        smp[yh] = sm[...]
        if comm:
            small_copy(8, smp, yh, at.part).start()

    def small_chip():
        small_copy(8, smp, 1 - yh, at.part).wait_recv()
        row = small_row()
        smc[c] = jnp.where((row >= GAIN2) & (row < BUP), smp[0] + smp[1], sm[...])
        small_copy(0, smc, c, at.sib).start()

    def small_x():
        small_copy(0, smc, 1 - c, at.sib).wait_recv()
        smx[at.x] = jnp.where(small_row() < BUP, smc[0] + smc[1], smc[c])
        for j in (1, 2, 3):
            small_copy(j, smx, at.x, at.xpeer(j)).start()

    def small_z():
        for j in (1, 2, 3):
            small_copy(j, smx, (at.x + 4 - j) % 4, at.xpeer(j)).wait_recv()
        smz[at.z] = (smx[0] + smx[1]) + (smx[2] + smx[3])
        for j in (1, 2, 3):
            small_copy(3 + j, smz, at.z, at.zpeer(j)).start()

    def small_y():
        for j in (1, 2, 3):
            small_copy(3 + j, smz, (at.z + 4 - j) % 4, at.zpeer(j)).wait_recv()
        smy[at.yl] = (smz[0] + smz[1]) + (smz[2] + smz[3])
        small_copy(7, smy, at.yl, at.ypeer).start()

    def small_end():
        small_copy(7, smy, 1 - at.yl, at.ypeer).wait_recv()
        small_ref[...] = smy[0] + smy[1]

    def small_drain():
        small_copy(8, smp, yh, at.part).wait_send()
        small_copy(0, smc, c, at.sib).wait_send()
        for j in (1, 2, 3):
            small_copy(j, smx, at.x, at.xpeer(j)).wait_send()
            small_copy(3 + j, smz, at.z, at.zpeer(j)).wait_send()
        small_copy(7, smy, at.yl, at.ypeer).wait_send()

    load_up.wait()
    load_down.wait()
    load_wout.wait()
    fetch_first()
    gather_start(3, wout_block)
    load_wqkv.wait()

    def attend_all(s, _):
        attend(s)

        @pl.when(s == 1)
        def _():
            fetch_second()

        return 0

    lax.fori_loop(0, SEQS, attend_all, 0)
    load_cot.wait()
    lax.fori_loop(0, 2 * SEQS, weigh, 0)
    gather_forward(0, att_block(0))
    fetch_third()
    gather_forward(3, wout_block)
    gather_wait(3, wout_block)
    lax.fori_loop(0, SEQS, feed, 0)
    lax.fori_loop(0, 3, up_grads, 0)
    reduce_step("start", d_up)
    fetch_wait()
    feed_more(0)
    feed_more(1)
    middle_back(0)
    feed_more(2)
    middle_back(1)
    lax.fori_loop(0, 3, down_grads, 0)
    middle_back(2)
    small_part()
    reduce_step("second", d_up)
    reduce_step("start", d_down)
    gather_forward(4, row_block(mlow, 0))

    def attend_back_all(s, _):
        def between():
            @pl.when(s < SEQS - 1)
            def _():
                gather_forward(5 + s, row_block(mlow, s + 1))

            @pl.when(s == 0)
            def _():
                reduce_step("third", d_up)
                output_rows(0)

            @pl.when(s == 1)
            def _():
                reduce_step("fourth", d_up)
                reduce_step("second", d_down)

            @pl.when(s == 2)
            def _():
                reduce_step("fifth", d_up)
                reduce_step("third", d_down)

            @pl.when(s > 0)
            def _():
                chip_sum(s - 1)

        attend_back(s, between)
        return 0

    lax.fori_loop(0, SEQS, attend_back_all, 0)
    lax.fori_loop(0, 3, qkv_grads, 0)
    out_grads()
    reduce_step("start", d_qkv)
    chip_sum(2)
    input_back(0)
    gather_forward(7, row_block(res, 0))
    reduce_step("fourth", d_down)
    finish_gin(0)
    finish_out(0)
    reduce_step("second", d_qkv)
    reduce_step("fifth", d_down)
    input_back(1)
    finish_gin(1)
    reduce_step("third", d_qkv)
    output_rows(1)
    output_rows(2)
    input_back(2)
    if comm:
        small_chip()
    finish_gin(2)
    if comm:
        small_x()
    reduce_step("fourth", d_qkv)
    if comm:
        small_z()
    reduce_step("fifth", d_qkv)
    if comm:
        small_y()
    gather_forward(8, row_block(res, 1))
    reduce_step("finish", d_up)
    reduce_step("finish", d_down)
    gather_forward(9, row_block(res, 2))
    finish_out(1)
    if comm:
        small_end()
    else:
        small_ref[...] = sm[...]
    finish_out(2)
    reduce_step("finish", d_qkv)

    if comm:
        fetch_drain()
        gather_drain(3, wout_block)
        for s in range(SEQS):
            gather_drain(s, att_block(s))
            gather_drain(4 + s, row_block(mlow, s))
            gather_drain(7 + s, row_block(res, s))
            share_copy(s, c).wait_send()
        for which in (d_up, d_down, d_qkv):
            which.drain()
        small_drain()


def layer(comm, x, cot, *rest):
    rows = (SEQS, 2, 2, QUART, D)
    half = (SEQS, HALF, D)
    pair = (SEQS, 2, QUART, D)
    dma = pltpu.SemaphoreType.DMA
    scratch = [
        pltpu.VMEM(rows, BF),
        pltpu.VMEM(rows, BF),
        pltpu.VMEM((3, 192, D), BF),
        pltpu.VMEM((D, D), BF),
        pltpu.VMEM((D, D), BF),
        pltpu.VMEM((D, D), BF),
        pltpu.VMEM((D, D), BF),
        pltpu.VMEM((D, D), BF),
        pltpu.VMEM((8, D), F32),
        pltpu.VMEM((8, D), F32),
        pltpu.VMEM((SEQS, LEN, D), BF),
        pltpu.VMEM((SEQS, LEN, 192), BF),
        pltpu.VMEM((SEQS, LEN, 192), BF),
        pltpu.VMEM((SEQS, LEN, 192), BF),
        pltpu.VMEM((SEQS, D, LEN), BF),
        pltpu.VMEM((3 * SEQS, 1, LEN), F32),
        pltpu.VMEM(half, F32),
        pltpu.VMEM(half, BF),
        pltpu.VMEM((D, ROWS), BF),
        pltpu.VMEM((D, ROWS), BF),
        pltpu.VMEM(half, F32),
        pltpu.VMEM(half, F32),
        pltpu.VMEM((2, SEQS, QUART, D), BF),
        pltpu.VMEM((2, SEQS, QUART, D), BF),
        pltpu.VMEM(pair, BF),
        pltpu.VMEM(pair, BF),
        pltpu.VMEM(pair, BF),
        pltpu.VMEM(pair, BF),
        pltpu.VMEM(rows, BF),
        pltpu.VMEM((3, 2, 2, QUART, 192), BF),
        pltpu.VMEM((LEN, LEN), F32),
        pltpu.VMEM((LEN, LEN), BF),
        pltpu.VMEM((LEN, LEN), BF),
        pltpu.VMEM((3, 2, 3, 192, 384), BF),
        pltpu.VMEM((3, 2, 3, 48, 384), BF),
        pltpu.VMEM((3, 2, 48, 384), BF),
        pltpu.VMEM((2 * SEQS, HALF), F32),
        pltpu.VMEM((8, D), F32),
        pltpu.VMEM((2, 8, D), F32),
        pltpu.VMEM((2, 8, D), F32),
        pltpu.VMEM((4, 8, D), F32),
        pltpu.VMEM((4, 8, D), F32),
        pltpu.VMEM((2, 8, D), F32),
        dma((8,)),
        dma((10, 3)),
        dma((10, 3)),
        dma((3, 7)),
        dma((3, 7)),
        dma((5, SEQS)),
        dma((5, SEQS)),
        dma((3, 2, 13)),
        dma((3, 2, 13)),
        pltpu.SemaphoreType.REGULAR((3, 2, 2)),
        dma((9,)),
        dma((9,)),
    ]
    anywhere = pl.BlockSpec(memory_space=pl.ANY)
    vmem = pl.BlockSpec(memory_space=pltpu.VMEM)
    return pl.pallas_call(
        functools.partial(kernel, comm),
        out_shape=(
            pltpu.VMEM(rows, BF),
            pltpu.VMEM(rows, BF),
            pltpu.VMEM((D, D), BF),
            pltpu.VMEM((D, D), BF),
            pltpu.VMEM((D, D), BF),
            pltpu.VMEM((8, D), F32),
        ),
        in_specs=[anywhere] * 6 + [vmem] * 10,
        out_specs=(vmem,) * 6,
        scratch_shapes=scratch,
        compiler_params=pltpu.CompilerParams(
            collective_id=0 if comm else None,
            has_side_effects=True,
            vmem_limit_bytes=54 * 2**20,
        ),
        cost_estimate=pl.CostEstimate(
            flops=20 * 10**9, bytes_accessed=20 * 10**6, transcendentals=10**7
        ),
        name="layer",
    )(x.reshape(rows), cot.reshape(rows), *rest)


def shards(
    layer_input,
    flags,
    loss_mask,
    cotangent,
    gain_one,
    shift_one,
    w_qkv,
    b_qv,
    w_out,
    b_out,
    gain_two,
    shift_two,
    w_up,
    b_up,
    w_down,
    b_down,
    comm=True,
):
    out, gin, g_up, g_down, g_qkv, small = layer(
        comm,
        layer_input,
        cotangent,
        w_qkv.transpose(0, 2, 1),
        w_out,
        w_up,
        w_down,
        flags,
        loss_mask,
        b_qv,
        gain_one,
        shift_one,
        b_out,
        gain_two,
        shift_two,
        b_up,
        b_down,
    )
    return (
        out.reshape(ROWS, D),
        gin.reshape(ROWS, D),
        small[GAIN1],
        small[SHIFT1],
        g_qkv[:576].reshape(3, 192, D).transpose(0, 2, 1).astype(F32),
        jnp.stack([small[BQV, 0:192], small[BQV, 256:448]]),
        g_qkv[576:].astype(F32),
        small[BOUT],
        small[GAIN2],
        small[SHIFT2],
        g_up.astype(F32),
        small[BUP],
        g_down.astype(F32),
        small[BDOWN],
    )


def solution(mesh):
    in_specs = (
        P("dp", None),
        P("dp"),
        P("dp"),
        P("dp", None),
        P(),
        P(),
        P(None, None, "tensor"),
        P(None, "tensor"),
        P("tensor", None),
        P(),
        P(),
        P(),
        P(None, "tensor"),
        P("tensor"),
        P("tensor", None),
        P(),
    )
    out_specs = (
        P("dp", None),
        P("dp", None),
        P(),
        P(),
        P(None, None, "tensor"),
        P(None, "tensor"),
        P("tensor", None),
        P(),
        P(),
        P(),
        P(None, "tensor"),
        P("tensor"),
        P("tensor", None),
        P(),
    )
    return jax.shard_map(shards, mesh=mesh, in_specs=in_specs, out_specs=out_specs, check_vma=False)
```

```python
import functools

import jax
import jax.numpy as jnp
from jax import lax
from jax.experimental import pallas as pl
from jax.experimental.pallas import tpu as pltpu
from jax.sharding import PartitionSpec as P

MESH = pl.DeviceIdType.MESH
BF = jnp.bfloat16
F32 = jnp.float32
D = 768
HD = 64
LEN = 512
HALF = 256
QUART = 128
SEQS = 3
ROWS = SEQS * LEN
EPS = 1e-05
SCALE = HD**-0.5
GELU_A = 0.7978845608028654
GELU_B = 0.044715

NN = (((1,), (0,)), ((), ()))
NT = (((1,), (1,)), ((), ()))
TN = (((0,), (0,)), ((), ()))

GAIN1, SHIFT1, GAIN2, SHIFT2, BOUT, BDOWN, BUP, BQV = range(8)


def dot(a, b, dims):
    return lax.dot_general(a, b, dims, preferred_element_type=F32)


def norm_parts(v):
    centred = v - jnp.mean(v, axis=1, keepdims=True)
    r = lax.rsqrt(jnp.mean(centred * centred, axis=1, keepdims=True) + EPS)
    return centred * r, r


def norm_back(v, e, gain):
    n, r = norm_parts(v)
    eg = e * gain
    grad = r * (
        eg
        - jnp.mean(eg, axis=1, keepdims=True)
        - n * jnp.mean(eg * n, axis=1, keepdims=True)
    )
    return grad, n


def col_sum(v):
    return jnp.sum(v, axis=0, keepdims=True)


def head_part(v, h):
    lane = lax.broadcasted_iota(jnp.int32, v.shape, 1)
    return jnp.where((lane >= HD * h) & (lane < HD * h + HD), v, jnp.zeros_like(v))


class Place:
    def __init__(self):
        dp = lax.axis_index("dp")
        self.t = t = lax.axis_index("tensor")
        self.z = dp // 8
        self.yl = (dp // 4) % 2
        self.x = dp % 4
        self.c = t % 2
        self.yh = t // 2
        self.t_sib = t + 1 - 2 * self.c
        self.t_part = (t + 2) % 4
        self.t_far = (self.t_sib + 2) % 4
        self.sib = (dp, self.t_sib)
        self.part = (dp, self.t_part)
        self.ypeer = (dp + 4 - 8 * self.yl, t)
        self.dp = dp

    def xpeer(self, j):
        return (self.dp - self.x + (self.x + j) % 4, self.t)

    def zpeer(self, j):
        return (((self.z + j) % 4) * 8 + self.dp % 8, self.t)

    def core_and_x(self, k):
        dp, _ = self.xpeer(k % 4)
        return (dp, self.t if k < 4 else self.t_sib)

    def y_and_z(self, k):
        dp, _ = self.zpeer(k % 4)
        return (dp if k < 4 else dp + 4 - 8 * self.yl, self.t)

    def peers(self):
        return (
            [self.part]
            + [self.core_and_x(k) for k in range(1, 5)]
            + [self.y_and_z(k) for k in range(1, 5)]
        )


def remote(src, dst, send, recv, device):
    return pltpu.make_async_remote_copy(
        src_ref=src,
        dst_ref=dst,
        send_sem=send,
        recv_sem=recv,
        device_id=device,
        device_id_type=MESH,
    )


class Reduction:
    def __init__(self, at, stg, r1, r2, ry, send, recv, free):
        self.at, self.stg, self.r1, self.r2, self.ry = at, stg, r1, r2, ry
        self.send, self.recv, self.free = send, recv, free
        self.big = stg.shape[0] // 4
        self.small = stg.shape[0] // 16

    def axes(self, h):
        at = self.at
        if h == 0:
            return at.x, at.z, at.xpeer, at.zpeer
        return at.z, at.x, at.zpeer, at.xpeer

    def block(self, h, first):
        rows = pl.ds(pl.multiple_of(first * self.big, self.big), self.big)
        return self.stg.at[rows, pl.ds(h * 384, 384)]

    def part(self, h, first, second):
        start = pl.multiple_of(first * self.big + second * self.small, self.small)
        return self.stg.at[pl.ds(start, self.small), pl.ds(h * 384, 384)]

    def copy(self, step, src, dst, device):
        return remote(src, dst, self.send.at[step], self.recv.at[step], device)

    def all_of(self, step):
        ref = (self.r1, self.r2, self.ry, self.r2, self.r1)[step]
        return self.copy(step, ref, ref, self.at.sib)

    def arrived(self, step):
        self.all_of(step).wait_recv()

    def left(self, step):
        self.all_of(step).wait_send()

    def give_back(self, stage):
        self.left(stage)
        for h in (0, 1):
            peer = self.axes(h)[2 + stage]
            for j in (1, 2, 3):
                pl.semaphore_signal(
                    self.free.at[stage], inc=1, device_id=peer(j), device_id_type=MESH
                )

    def start(self):
        for h in (0, 1):
            first, _, peer, _ = self.axes(h)
            for j in (1, 2, 3):
                src = self.block(h, (first + j) % 4)
                self.copy(0, src, self.r1.at[h, j - 1], peer(j)).start()

    def second(self):
        self.arrived(0)
        for h in (0, 1):
            first, second, _, peer = self.axes(h)
            own = self.block(h, first)
            total = own[...].astype(F32)
            for j in (0, 1, 2):
                total = total + self.r1[h, j].astype(F32)
            own[...] = total.astype(BF)
            for j in (1, 2, 3):
                src = self.part(h, first, (second + j) % 4)
                self.copy(1, src, self.r2.at[h, j - 1], peer(j)).start()
        self.give_back(0)

    def third(self):
        self.arrived(1)
        for h in (0, 1):
            first, second, _, _ = self.axes(h)
            own = self.part(h, first, second)
            total = own[...].astype(F32)
            for j in (0, 1, 2):
                total = total + self.r2[h, j].astype(F32)
            own[...] = total.astype(BF)
            self.copy(2, own, self.ry.at[h], self.at.ypeer).start()
        self.give_back(1)

    def fourth(self):
        self.arrived(2)
        self.left(2)
        pl.semaphore_wait(self.free.at[1], 6)
        for h in (0, 1):
            first, second, _, peer = self.axes(h)
            own = self.part(h, first, second)
            own[...] = (own[...].astype(F32) + self.ry[h].astype(F32)).astype(BF)
            for j in (1, 2, 3):
                self.copy(3, own, own, peer(j)).start()

    def fifth(self):
        self.arrived(3)
        pl.semaphore_wait(self.free.at[0], 6)
        for h in (0, 1):
            first, _, peer, _ = self.axes(h)
            own = self.block(h, first)
            for j in (1, 2, 3):
                self.copy(4, own, own, peer(j)).start()

    def finish(self):
        self.arrived(4)

    def drain(self):
        self.left(3)
        self.left(4)


def kernel(
    comm,
    x_hbm,
    cot_hbm,
    wqkv_hbm,
    wout_hbm,
    wup_hbm,
    wdown_hbm,
    flags_hbm,
    mask_hbm,
    bqv_hbm,
    gain1_hbm,
    shift1_hbm,
    bout_hbm,
    gain2_hbm,
    shift2_hbm,
    bup_hbm,
    bdown_hbm,
    res,
    gin,
    stg_u,
    stg_d,
    stg_q,
    small_ref,
    flags_ref,
    mask_ref,
    bqv_ref,
    gain1_ref,
    shift1_ref,
    bout_ref,
    gain2_ref,
    shift2_ref,
    bup_ref,
    bdown_ref,
    x_ref,
    u_ref,
    wqkv,
    wof,
    wup,
    wdown,
    fwup,
    fwdown,
    bias,
    fbias,
    n1,
    q8,
    keys,
    vals,
    att,
    lse,
    mid,
    n2,
    nt2,
    actt,
    own_a,
    own_b,
    s1,
    r1,
    ex,
    mlow,
    gp,
    sc,
    pr,
    ds,
    red1,
    red2,
    redy,
    remy,
    weight,
    sm,
    smp,
    smx,
    smz,
    in_sem,
    a_send,
    a_recv,
    w_send,
    w_recv,
    t_send,
    t_recv,
    x_send,
    x_recv,
    d_send,
    d_recv,
    d_free,
    m_send,
    m_recv,
):
    at = Place()
    c, yh, t = (at.c, at.yh, at.t) if comm else (0, 0, 0)
    ghid = gin
    gpt = nt2.at[0:576]

    def lanes(s, half=None):
        if half is None:
            return pl.ds(pl.multiple_of(s * LEN, LEN), LEN)
        return pl.ds(pl.multiple_of(s * LEN + half * HALF, HALF), HALF)

    def core_rows(core):
        return pl.ds(pl.multiple_of(core * QUART, QUART), QUART)

    def flat(v):
        return v.reshape(-1, v.shape[-1])

    def wout_rows(t, start, count):
        return wof.at[pl.ds(pl.multiple_of(t * 192 + start, 48), count)]

    def wout_block(t):
        return wout_rows(t, 0, 192)

    def att_block(s):
        def block(t):
            return att.at[s, pl.ds(pl.multiple_of(t * 192, 192), 192)]

        block.rows = 192
        return block

    def row_block(ref, s):
        def block(t):
            return ref.at[s, t // 2, t % 2]

        block.rows = QUART
        return block

    def load(i, src, dst):
        return pltpu.make_async_copy(src, dst, in_sem.at[i])

    def load_x(s):
        return load(s, x_hbm.at[s], x_ref.at[s])

    load_wqkv = load(3, wqkv_hbm, wqkv)
    load_wout = load(4, wout_hbm, wout_block(t))
    load_cot = load(5, cot_hbm, u_ref)
    load_up = load(6, wup_hbm, wup)
    load_down = load(7, wdown_hbm, wdown)
    small_loads = [
        load(8 + i, src, dst)
        for i, (src, dst) in enumerate(
            (
                (gain1_hbm, gain1_ref),
                (shift1_hbm, shift1_ref),
                (bqv_hbm, bqv_ref),
                (bup_hbm, bup_ref),
                (flags_hbm, flags_ref),
                (mask_hbm, mask_ref),
                (bout_hbm, bout_ref),
                (gain2_hbm, gain2_ref),
                (shift2_hbm, shift2_ref),
                (bdown_hbm, bdown_ref),
            )
        )
    ]
    load_x(0).start()
    load_wqkv.start()
    if comm:
        barrier = pltpu.get_barrier_semaphore()
        peers = at.peers()
        for peer in peers:
            pl.semaphore_signal(barrier, inc=1, device_id=peer, device_id_type=MESH)
    for copy in small_loads:
        copy.start()
    load_wout.start()
    load_up.start()
    load_down.start()
    load_x(1).start()
    load_x(2).start()
    load_cot.start()
    sm[...] = jnp.zeros_like(sm)
    for copy in small_loads:
        copy.wait()
    bias[...] = jnp.broadcast_to(bup_ref[...].reshape(1, D), (8, D))
    weight[...] = jnp.maximum(flags_ref[...], mask_ref[...]).astype(F32).reshape(2 * SEQS, HALF)

    def fetch_part(i, count):
        first, second = (at.x, at.z) if i == 0 else (at.z, at.x)
        start = (second * 4 + (first if count == 1 else 0)) * 48
        return pl.ds(pl.multiple_of(start, 48), 48 * count)

    def fetch_copy(step, src, dst, device):
        return remote(src, dst, w_send.at[step], w_recv.at[step], device)

    def fetch_y(i):
        if i == 2:
            ref = wout_rows(t, at.x * 48, 48)
            return fetch_copy(0, ref, ref, at.part)
        src, dst = ((wup, fwup), (wdown, fwdown))[i]
        some = fetch_part(i, 1)
        return fetch_copy(1, src.at[some], dst.at[some], at.part)

    def fetch_a(i, j):
        peer = at.zpeer if i == 1 else at.xpeer
        if i == 2:
            ref = wout_rows(at.t_part, at.x * 48, 48)
            return fetch_copy(3, ref, ref, peer(j))
        ref = (fwup, fwdown)[i].at[fetch_part(i, 1)]
        return fetch_copy(4, ref, ref, peer(j))

    def fetch_b(i, j):
        peer = at.xpeer if i == 1 else at.zpeer
        ref = (fwup, fwdown)[i].at[fetch_part(i, 4)]
        return fetch_copy(5, ref, ref, peer(j))

    def fetch_all(step):
        ref = (wof.at[0:48], fwup.at[0:96], fbias, wof.at[0:144], fwup.at[0:288], nt2.at[0:576])[step]
        return fetch_copy(step, ref, ref, at.part)

    def fetch_first(kinds):
        if comm:
            for i in kinds:
                fetch_y(i).start()
            if 0 in kinds:
                fetch_copy(2, bias, fbias, at.part).start()

    def fetch_second(kinds):
        if comm:
            fetch_all(0 if 2 in kinds else 1).wait_recv()
            for i in kinds:
                for j in (1, 2, 3):
                    fetch_a(i, j).start()

    def fetch_third(kinds):
        if comm:
            fetch_all(3 if 2 in kinds else 4).wait_recv()
            for i in kinds:
                if i < 2:
                    for j in (1, 2, 3):
                        fetch_b(i, j).start()

    def fetch_wait():
        if comm:
            fetch_all(2).wait_recv()
            fetch_all(5).wait_recv()

    def fetch_left():
        if comm:
            for step in (0, 1, 2):
                fetch_all(step).wait_send()

    def fetch_drain():
        if comm:
            for step in (3, 4, 5):
                fetch_all(step).wait_send()

    def gather_copy(i, block, kind, t, device):
        ref = block(t)
        return remote(ref, ref, a_send.at[i], a_recv.at[i, kind], device)

    def gather_start(i, block):
        if comm:
            if not isinstance(i, int) or i != 3:
                gather_copy(i, block, 1, at.t, at.part).start()
            gather_copy(i, block, 0, at.t, at.sib).start()

    def gather_forward(i, block):
        if comm:
            if not isinstance(i, int) or i != 3:
                gather_copy(i, block, 1, at.t_part, at.part).wait_recv()
            gather_copy(i, block, 0, at.t_part, at.sib).start()

    def gather_all(i, block, count):
        if block is wout_block:
            ref = wof.at[0 : 192 * count]
        elif block.rows == 192:
            ref = att.at[0, 0 : 192 * count]
        else:
            ref = n1.at[0, 0 : QUART * count]
        return remote(ref, ref, a_send.at[i], a_recv.at[i, 0], at.sib)

    def gather_wait(i, block):
        if comm:
            gather_all(i, block, 2).wait_recv()

    def gather_drain(i, block):
        if comm:
            gather_all(i, block, 2 if block is wout_block else 3).wait_send()

    def core_copy(k, s):
        return remote(s1.at[k, s - 1], r1.at[k, s - 1], t_send.at[k, s - 1], t_recv.at[k, s - 1], at.sib)

    def core_sum(k, s, own):
        if comm:
            core_copy(k, s).wait()
        return own[s, core_rows(c), :] + r1[k, s - 1].astype(F32)

    def slot(kind, i):
        if isinstance(i, int) and i >= SEQS:
            return ex.at[kind, i - SEQS]
        rows = pl.ds(pl.multiple_of(i * HALF, HALF), HALF)
        if kind % 2 == 0:
            return actt.at[rows, pl.ds(kind // 2 * D, D)]
        return (wup, wdown)[kind // 2].at[rows]

    def chip_copy(i):
        return remote(slot(0, i), slot(1, i), x_send.at[0, i], x_recv.at[0, i], at.sib)

    def group_copy(i):
        return remote(slot(2, i), slot(3, i), x_send.at[1, i], x_recv.at[1, i], at.part)

    def share_copy(i, ref, s, core):
        some = ref.at[s, :, core]
        return remote(some, some, x_send.at[2, i], x_recv.at[2, i], at.sib)

    def chip_sum(i, own):
        if comm:
            chip_copy(i).wait()
        slot(2, i)[...] = (own[...] + slot(1, i)[...].astype(F32)).astype(BF)
        if comm:
            group_copy(i).start()

    def group_arrived(i):
        if comm:
            group_copy(i).wait()

    def group_sum(i, piece):
        return slot(2, i)[piece, :].astype(F32) + slot(3, i)[piece, :].astype(F32)

    def share(i, ref, s):
        if comm:
            share_copy(i, ref, s, c).start()

    def share_wait(i, ref, s):
        if comm:
            share_copy(i, ref, s, 1 - c).wait_recv()

    def core_part(v, core):
        return jnp.where(core == 0, v[:QUART], v[QUART:])

    gain1, shift1, gain2, shift2, b_out, b_down = (
        ref[...].reshape(1, D)
        for ref in (gain1_ref, shift1_ref, gain2_ref, shift2_ref, bout_ref, bdown_ref)
    )

    def add_small(row, value):
        sm[row : row + 1, :] += value

    def project(s):
        load_x(s).wait()
        for half in range(2):
            n, _r = norm_parts(flat(x_ref[s, half]).astype(F32))
            n1[s, HALF * half : HALF * half + HALF, :] = (n * gain1 + shift1).astype(BF)
        normed = n1[s]
        q = (dot(normed, wqkv[0], NT) + bqv_ref[0:1, :]).astype(BF) * SCALE
        q8[s] = q
        k = dot(normed, wqkv[1], NT).astype(BF)
        keys[s] = k
        v = (dot(normed, wqkv[2], NT) + bqv_ref[1:2, :]).astype(BF)
        vals[s] = v

    def attend(s):
        q, k, vt = q8[s], keys[s], vals[s].T
        block = att_block(s)(t)
        for h in range(3):
            sc[...] = dot(head_part(k, h), q, NT)
            for part in range(4):
                cols = slice(part * 128, part * 128 + 128)
                scores = sc[:, cols]
                top = jnp.max(scores, axis=0, keepdims=True)
                e = jnp.exp(scores - top)
                total = col_sum(e)
                lse[3 * s + h, :, cols] = top + jnp.log(total)
                pr[:, cols] = (e * (1.0 / total)).astype(BF)
            mixed = dot(vt[HD * h : HD * h + HD], pr[...], NN)
            block[HD * h : HD * h + HD, :] = mixed.astype(BF)
        gather_start(s, att_block(s))

    def weigh(i, _):
        same = lax.broadcasted_iota(jnp.int32, (HALF, HALF), 0) == lax.broadcasted_iota(
            jnp.int32, (HALF, HALF), 1
        )
        diagonal = jnp.where(same, weight[pl.ds(i, 1), :], 0.0).astype(BF)
        rows = dot(diagonal, flat(u_ref[i // 2, i % 2]), NN).astype(BF)
        u_ref[i // 2, i % 2] = rows.reshape(2, QUART, D)
        return 0

    def hidden_units(normed, up, w_up, b_up, w_down):
        acts, grads = [], []
        for i in range(2):
            some = slice(i * 384, i * 384 + 384)
            v = dot(normed, w_up[:, some], NN) + b_up[:, some]
            back = dot(up, w_down[some, :], NT)
            square = v * v
            th = jnp.tanh(v * (GELU_A + (GELU_A * GELU_B) * square))
            cdf = 0.5 + 0.5 * th
            inner = v * (0.5 * GELU_A + (1.5 * GELU_A * GELU_B) * square)
            acts.append((v * cdf).astype(BF))
            grads.append(back * (cdf + inner * (1.0 - th * th)))
        total = jnp.concatenate([col_sum(grad) for grad in grads], axis=1)
        grad = jnp.concatenate([grad.astype(BF) for grad in grads], axis=1)
        return jnp.concatenate(acts, axis=1), grad, total

    def feed(s, between):
        gather_wait(s, att_block(s))
        for own in (False, True):
            half = yh if own else 1 - yh
            some = lanes(s, half)
            cols = pl.ds(pl.multiple_of(half * HALF, HALF), HALF)
            middle = flat(x_ref[s, half]).astype(F32) + dot(att[s, :, cols], wof[...], TN) + b_out
            n, _r = norm_parts(middle)
            normed = (n * gain2 + shift2).astype(BF)
            nt2[:, some] = normed.T
            act, grad, total = hidden_units(normed, flat(u_ref[s, half]), wup, bias[0:1, :], wdown)
            add_small(BUP, total)
            actt[:, some] = act.T
            ghid[s, half] = grad.reshape(2, QUART, D)
            if own:
                between(1)
            if isinstance(s, int):
                piece = pl.ds(pl.multiple_of(half * QUART, QUART), QUART)
                mid[s, piece, :] = core_part(middle, c)
                for k, (ref, total) in enumerate(
                    ((own_a, dot(grad, wup[...], NT)), (own_b, dot(act, wdown[...], NN)))
                ):
                    ref[s, piece, :] = core_part(total, c)
                    slot(0, 3 + k)[piece, :] = core_part(total, 1 - c).astype(BF)
            elif own:
                mid[s] = middle
                n2[s - 1] = normed
                own_a[s] = dot(grad, wup[...], NT)
                own_b[s] = dot(act, wdown[...], NN)
            if not own:
                between(0)
        if isinstance(s, int) and comm:
            chip_copy(3).start()
            chip_copy(4).start()

    def feed_more(s):
        act, grad, _ = hidden_units(n2[s - 1], flat(u_ref[s, yh]), fwup, fbias[0:1, :], fwdown)
        own_a[s] += dot(grad, fwup[...], NT)
        own_b[s] += dot(act, fwdown[...], NN)
        for k, ref in enumerate((own_a, own_b)):
            s1[k, s - 1] = ref[s, core_rows(1 - c), :].astype(BF)
            if comm:
                core_copy(k, s).start()

    def middle_back(s):
        e = core_sum(0, s, own_a)
        grad, n = norm_back(mid[s, core_rows(c), :], e, gain2)
        add_small(GAIN2, col_sum(e * n))
        add_small(SHIFT2, col_sum(e))
        up = u_ref[s, yh, c].astype(F32)
        grad = up + grad
        add_small(BOUT, col_sum(grad))
        add_small(BDOWN, col_sum(up))
        mlow[s, yh, c] = grad.astype(BF)
        gather_start(4 + s, row_block(mlow, s))

    def middle_back_first():
        group_arrived(3)
        for half in range(2):
            piece = slice(half * QUART, half * QUART + QUART)
            e = group_sum(3, piece)
            grad, n = norm_back(mid[0, piece, :], e, gain2)
            up = u_ref[0, half, c].astype(F32)
            grad = up + grad
            mlow[0, half, c] = grad.astype(BF)
            for row, v in ((GAIN2, e * n), (SHIFT2, e), (BOUT, grad), (BDOWN, up)):
                add_small(row, jnp.where(yh == half, col_sum(v), 0.0))
        share(3, mlow, 0)

    def output_rows_first():
        group_arrived(4)
        for half in range(2):
            piece = slice(half * QUART, half * QUART + QUART)
            total = mid[0, piece, :] + group_sum(4, piece) + b_down
            res[0, half, c] = total.astype(BF)
        share(4, res, 0)

    def output_rows(s):
        total = mid[s, core_rows(c), :] + core_sum(1, s, own_b) + b_down
        res[s, yh, c] = total.astype(BF)
        gather_start(7 + s, row_block(res, s))

    def reduction(i, ref, wide):
        if wide:
            r1, r2, ry = red1.at[i], red2.at[i], redy.at[i]
        else:
            j = i - 2
            r1 = red1.at[0, :, :, pl.ds(j * 64, 64)]
            r2 = red2.at[0, :, :, pl.ds(j * 16, 16)]
            ry = remy.at[j]
        return Reduction(at, ref, r1, r2, ry, d_send.at[i], d_recv.at[i], d_free.at[i])

    d_up, d_down = reduction(0, stg_u, True), reduction(1, stg_d, True)
    d_att = [reduction(2 + i, stg_q.at[pl.ds(i * HALF, HALF)], False) for i in range(3)]

    def reduce_step(name, which):
        if comm:
            getattr(which, name)()

    def stage(stg, start, count, value):
        stg[pl.ds(start, count), :] = value.astype(BF)

    def up_grads(i, _):
        start = pl.multiple_of(i * HALF, HALF)
        some = pl.ds(start, HALF)
        stage(stg_u, start, HALF, dot(nt2[some, :], flat(ghid[...]), NN))
        return 0

    def down_grads(i, _):
        start = pl.multiple_of(i * HALF, HALF)
        some = pl.ds(start, HALF)
        stage(stg_d, start, HALF, dot(actt[some, :], flat(u_ref[...]), NN))
        return 0

    def qkv_grads(start, count):
        stage(stg_q, start, count, dot(gpt[start : start + count, :], flat(n1[...]), NN))

    def out_grads():
        total = jnp.zeros((192, D), F32)
        for s in range(SEQS):
            total += dot(att_block(s)(t)[...], flat(mlow[s]), NN)
        stage(stg_q, 576, 192, total)

    def attend_back(s, between):
        some_lanes = lanes(s)
        mixed = dot(flat(mlow[s]), wout_block(t)[...], NT).astype(BF)
        q, k, v = q8[s], keys[s], vals[s]
        kt = k.T
        grad_k = jnp.zeros((LEN, 192), F32)
        grad_v = jnp.zeros((LEN, 192), F32)
        for h in range(3):
            sc[...] = dot(head_part(k, h), q, NT)
            back = dot(head_part(v, h), mixed, NT)
            some = slice(HD * h, HD * h + HD)
            for part in range(4):
                cols = slice(part * 128, part * 128 + 128)
                p = jnp.exp(sc[:, cols] - lse[3 * s + h, :, cols])
                pr[:, cols] = p.astype(BF)
                gp_part = back[:, cols]
                total = col_sum(gp_part * p)
                ds[:, cols] = (p * (gp_part - total)).astype(BF)
            grad_v += dot(pr[...], head_part(mixed, h), NN)
            grad_k += dot(ds[...], head_part(q, h), NN)
            gpt[some, some_lanes] = (dot(kt[some], ds[...], NN) * SCALE).astype(BF)
            between(h)
        grad_q = gpt[0:192, some_lanes].T
        grad_k = grad_k.astype(BF)
        grad_v = grad_v.astype(BF)
        gpt[192:384, some_lanes] = grad_k.T
        gpt[384:576, some_lanes] = grad_v.T
        for i, grad in enumerate((grad_q, grad_k, grad_v)):
            gp[i] = grad.reshape(2, 2, QUART, 192)
        sm[BQV : BQV + 1, 0:192] += col_sum(grad_q.astype(F32))
        sm[BQV : BQV + 1, 256:448] += col_sum(grad_v.astype(F32))
        for own in (False, True):
            core = c if own else 1 - c
            total = dot(flat(gp[0, :, core]), wqkv[0], NN)
            total += dot(flat(gp[1, :, core]), wqkv[1], NN)
            total += dot(flat(gp[2, :, core]), wqkv[2], NN)
            if own:
                own_a[s] = total
            else:
                slot(0, s)[...] = total.astype(BF)
                if comm:
                    chip_copy(s).start()

    def input_back(s):
        group_arrived(s)
        for half in range(2):
            e = group_sum(s, slice(half * QUART, half * QUART + QUART))
            grad, n = norm_back(x_ref[s, half, c].astype(F32), e, gain1)
            add_small(GAIN1, col_sum(e * n))
            add_small(SHIFT1, col_sum(e))
            gin[s, half, c] = (mlow[s, half, c].astype(F32) + grad).astype(BF)
        share(s, gin, s)

    def small_copy(i, slots, slot, device):
        ref = slots.at[slot]
        return remote(ref, ref, m_send.at[i], m_recv.at[i], device)

    def small_row():
        return lax.broadcasted_iota(jnp.int32, (8, D), 0)

    def small_part():
        smp[yh] = sm[...]
        if comm:
            small_copy(0, smp, yh, at.part).start()

    def small_all(i, slots):
        return remote(slots.at[0:7], slots.at[0:7], m_send.at[i], m_recv.at[i], at.sib)

    def first_slot():
        return at.c * 4 + at.x

    def second_slot():
        return at.yl * 4 + at.z

    def small_first():
        small_copy(0, smp, 1 - yh, at.part).wait_recv()
        row = small_row()
        smx[first_slot()] = jnp.where((row >= GAIN2) & (row < BUP), smp[0] + smp[1], sm[...])
        for k in range(1, 8):
            small_copy(1, smx, first_slot(), at.core_and_x(k)).start()

    def small_second():
        small_all(1, smx).wait_recv()
        cores = [
            (smx[4 * i] + smx[4 * i + 1]) + (smx[4 * i + 2] + smx[4 * i + 3]) for i in (0, 1)
        ]
        mine = jnp.where(c == 0, cores[0], cores[1])
        smz[second_slot()] = jnp.where(small_row() < BUP, cores[0] + cores[1], mine)
        for k in range(1, 8):
            small_copy(2, smz, second_slot(), at.y_and_z(k)).start()

    def small_end():
        small_all(2, smz).wait_recv()
        total = smz[0]
        for i in range(1, 8):
            total = total + smz[i]
        small_ref[...] = total

    def small_drain():
        small_copy(0, smp, yh, at.part).wait_send()
        small_all(1, smx).wait_send()
        small_all(2, smz).wait_send()

    load_wqkv.wait()
    project(0)
    load_wout.wait()
    load_up.wait()
    load_down.wait()
    if comm:
        pl.semaphore_wait(barrier, len(peers))
    fetch_first((2,))
    gather_start(3, wout_block)

    def attend_all(s, _):
        @pl.when(s > 0)
        def _():
            project(s)

        @pl.when(s == 1)
        def _():
            fetch_second((2,))

        attend(s)

        @pl.when(s == 0)
        def _():
            fetch_first((0, 1))

        return 0

    lax.fori_loop(0, SEQS, attend_all, 0)
    load_cot.wait()
    lax.fori_loop(0, 2, weigh, 0)
    fetch_third((2,))
    gather_forward(3, wout_block)
    lax.fori_loop(2, 2 * SEQS, weigh, 0)
    gather_forward(0, att_block(0))
    fetch_second((0, 1))
    gather_wait(3, wout_block)

    def feed_first(slot):
        if slot == 1:
            gather_forward(1, att_block(1))

    feed(0, feed_first)
    fetch_third((0, 1))

    def feed_all(s, _):
        def between(slot):
            @pl.when(s == 1)
            def _():
                if slot == 0:
                    chip_sum(3, own_a.at[0])
                    chip_sum(4, own_b.at[0])
                else:
                    gather_forward(2, att_block(2))

        feed(s, between)
        return 0

    lax.fori_loop(1, SEQS, feed_all, 0)
    fetch_left()
    lax.fori_loop(0, 3, up_grads, 0)
    reduce_step("start", d_up)
    lax.fori_loop(0, 3, down_grads, 0)
    middle_back_first()
    fetch_wait()
    feed_more(1)
    feed_more(2)
    middle_back(1)
    fetch_drain()
    gather_drain(3, wout_block)
    for s in range(SEQS):
        gather_drain(s, att_block(s))
    middle_back(2)
    small_part()
    share_wait(3, mlow, 0)

    def attend_back_all(s, _):
        def between(h):
            if h == 0:

                @pl.when(s == 0)
                def _():
                    reduce_step("second", d_up)
                    reduce_step("start", d_down)

                @pl.when(s == 2)
                def _():
                    reduce_step("fifth", d_up)
                    chip_sum(1, own_a.at[1])

            if h == 1:

                @pl.when(s == 0)
                def _():
                    output_rows_first()

                @pl.when(s == 1)
                def _():
                    gather_forward(6, row_block(mlow, 2))
                    reduce_step("fourth", d_up)

                @pl.when(s == 2)
                def _():
                    reduce_step("third", d_down)

            if h == 2:

                @pl.when(s == 1)
                def _():
                    reduce_step("second", d_down)

        attend_back(s, between)

        @pl.when(s == 0)
        def _():
            gather_forward(5, row_block(mlow, 1))
            reduce_step("third", d_up)
            chip_sum(0, own_a.at[0])
            gather_wait(5, row_block(mlow, 1))

        @pl.when(s == 1)
        def _():
            gather_wait(6, row_block(mlow, 2))

        return 0

    lax.fori_loop(0, SEQS, attend_back_all, 0)
    qkv_grads(0, HALF)
    reduce_step("start", d_att[0])
    qkv_grads(HALF, HALF)
    reduce_step("start", d_att[1])
    qkv_grads(2 * HALF, 64)
    out_grads()
    reduce_step("start", d_att[2])
    chip_sum(2, own_a.at[2])
    reduce_step("fourth", d_down)
    input_back(0)
    for s in (1, 2):
        gather_drain(4 + s, row_block(mlow, s))
    reduce_step("second", d_att[0])
    reduce_step("second", d_att[1])
    reduce_step("second", d_att[2])
    reduce_step("fifth", d_down)
    input_back(1)
    for part in d_att:
        reduce_step("third", part)
    output_rows(1)
    input_back(2)
    if comm:
        small_first()
    reduce_step("fourth", d_att[0])
    reduce_step("fourth", d_att[1])
    reduce_step("fourth", d_att[2])
    output_rows(2)
    for s in range(SEQS):
        share_wait(s, gin, s)
    share_wait(4, res, 0)
    reduce_step("fifth", d_att[0])
    if comm:
        small_second()
    reduce_step("fifth", d_att[1])
    reduce_step("fifth", d_att[2])
    gather_forward(8, row_block(res, 1))
    reduce_step("finish", d_up)
    reduce_step("drain", d_up)
    gather_forward(9, row_block(res, 2))
    reduce_step("finish", d_down)
    reduce_step("drain", d_down)
    if comm:
        for i, ref, s in ((0, gin, 0), (1, gin, 1), (2, gin, 2), (3, mlow, 0), (4, res, 0)):
            share_copy(i, ref, s, c).wait_send()
    for s in (1, 2):
        gather_wait(7 + s, row_block(res, s))
        gather_drain(7 + s, row_block(res, s))
    if comm:
        small_end()
        small_drain()
    else:
        small_ref[...] = sm[...]
    for part in d_att:
        reduce_step("finish", part)
        reduce_step("drain", part)


def layer(comm, x, cot, *rest):
    rows = (SEQS, 2, 2, QUART, D)
    half = (SEQS, HALF, D)
    dma = pltpu.SemaphoreType.DMA
    scratch = [
        pltpu.VMEM((ROWS,), jnp.int32),
        pltpu.VMEM((ROWS,), jnp.int32),
        pltpu.VMEM((2, 192), F32),
        pltpu.VMEM((D,), F32),
        pltpu.VMEM((D,), F32),
        pltpu.VMEM((D,), F32),
        pltpu.VMEM((D,), F32),
        pltpu.VMEM((D,), F32),
        pltpu.VMEM((D,), F32),
        pltpu.VMEM((D,), F32),
        pltpu.VMEM(rows, BF),
        pltpu.VMEM(rows, BF),
        pltpu.VMEM((3, 192, D), BF),
        pltpu.VMEM((D, D), BF),
        pltpu.VMEM((D, D), BF),
        pltpu.VMEM((D, D), BF),
        pltpu.VMEM((D, D), BF),
        pltpu.VMEM((D, D), BF),
        pltpu.VMEM((8, D), F32),
        pltpu.VMEM((8, D), F32),
        pltpu.VMEM((SEQS, LEN, D), BF),
        pltpu.VMEM((SEQS, LEN, 192), BF),
        pltpu.VMEM((SEQS, LEN, 192), BF),
        pltpu.VMEM((SEQS, LEN, 192), BF),
        pltpu.VMEM((SEQS, D, LEN), BF),
        pltpu.VMEM((3 * SEQS, 1, LEN), F32),
        pltpu.VMEM(half, F32),
        pltpu.VMEM((SEQS - 1, HALF, D), BF),
        pltpu.VMEM((D, ROWS), BF),
        pltpu.VMEM((D, ROWS), BF),
        pltpu.VMEM(half, F32),
        pltpu.VMEM(half, F32),
        pltpu.VMEM((2, SEQS - 1, QUART, D), BF),
        pltpu.VMEM((2, SEQS - 1, QUART, D), BF),
        pltpu.VMEM((4, 2, HALF, D), BF),
        pltpu.VMEM(rows, BF),
        pltpu.VMEM((3, 2, 2, QUART, 192), BF),
        pltpu.VMEM((LEN, LEN), F32),
        pltpu.VMEM((LEN, LEN), BF),
        pltpu.VMEM((LEN, LEN), BF),
        pltpu.VMEM((2, 2, 3, 192, 384), BF),
        pltpu.VMEM((2, 2, 3, 48, 384), BF),
        pltpu.VMEM((2, 2, 48, 384), BF),
        pltpu.VMEM((3, 2, 16, 384), BF),
        pltpu.VMEM((2 * SEQS, HALF), F32),
        pltpu.VMEM((8, D), F32),
        pltpu.VMEM((2, 8, D), F32),
        pltpu.VMEM((8, 8, D), F32),
        pltpu.VMEM((8, 8, D), F32),
        dma((18,)),
        dma((10,)),
        dma((10, 2)),
        dma((6,)),
        dma((6,)),
        dma((2, SEQS - 1)),
        dma((2, SEQS - 1)),
        dma((3, 5)),
        dma((3, 5)),
        dma((5, 5)),
        dma((5, 5)),
        pltpu.SemaphoreType.REGULAR((5, 2)),
        dma((3,)),
        dma((3,)),
    ]
    anywhere = pl.BlockSpec(memory_space=pl.ANY)
    vmem = pl.BlockSpec(memory_space=pltpu.VMEM)
    return pl.pallas_call(
        functools.partial(kernel, comm),
        out_shape=(
            pltpu.VMEM(rows, BF),
            pltpu.VMEM(rows, BF),
            pltpu.VMEM((D, D), BF),
            pltpu.VMEM((D, D), BF),
            pltpu.VMEM((D, D), BF),
            pltpu.VMEM((8, D), F32),
        ),
        in_specs=[anywhere] * 16,
        out_specs=(vmem,) * 6,
        scratch_shapes=scratch,
        compiler_params=pltpu.CompilerParams(
            collective_id=0 if comm else None,
            has_side_effects=True,
            vmem_limit_bytes=55 * 2**20,
        ),
        cost_estimate=pl.CostEstimate(
            flops=20 * 10**9, bytes_accessed=20 * 10**6, transcendentals=10**7
        ),
        name="layer",
    )(x.reshape(rows), cot.reshape(rows), *rest)


def results(out, gin, g_up, g_down, g_qkv, small):
    def kernel(out, gin, up, down, qkv, small, *rest):
        (out_to, gin_to, qkv_to, out_w_to, up_to, down_to, bqv_to), rest = rest[:7], rest[7:]
        vectors, (wide, sem) = rest[:7], rest[7:]
        copies = []

        def start(i, src, dst):
            copy = pltpu.make_async_copy(src, dst, sem.at[i])
            copy.start()
            copies.append(copy)

        start(0, out, out_to)
        start(1, gin, gin_to)
        for i, (src, first, rows, dst) in enumerate(
            (
                (up, 0, D, up_to),
                (down, 0, D, down_to),
                (qkv, 0, 576, qkv_to),
                (qkv, 576, 192, out_w_to),
            )
        ):
            at = (0, D, 2 * D, 2 * D + 576)[i]
            wide[at : at + rows, :] = src[first : first + rows, :].astype(F32)
            start(2 + i, wide.at[pl.ds(at, rows)], dst)
        for row, ref in zip((GAIN1, SHIFT1, BOUT, GAIN2, SHIFT2, BUP, BDOWN), vectors):
            ref[...] = small[row : row + 1, :].reshape(D)
        bqv_to[0:1, :] = small[BQV : BQV + 1, 0:192]
        bqv_to[1:2, :] = small[BQV : BQV + 1, 256:448]
        for copy in copies:
            copy.wait()

    anywhere = pl.BlockSpec(memory_space=pl.ANY)
    vmem = pl.BlockSpec(memory_space=pltpu.VMEM)

    def shape(*dims, dtype=F32):
        return jax.ShapeDtypeStruct(dims, dtype)

    return pl.pallas_call(
        kernel,
        out_shape=(
            shape(*out.shape, dtype=BF),
            shape(*gin.shape, dtype=BF),
            shape(576, D),
            shape(192, D),
            shape(D, D),
            shape(D, D),
            shape(2, 192),
        )
        + (shape(D),) * 7,
        in_specs=[vmem] * 6,
        out_specs=(anywhere,) * 6 + (vmem,) * 8,
        scratch_shapes=[pltpu.VMEM((3 * D, D), F32), pltpu.SemaphoreType.DMA((6,))],
        compiler_params=pltpu.CompilerParams(vmem_limit_bytes=12 * 2**20),
        name="results",
    )(
        *(
            pltpu.with_memory_space_constraint(v, pltpu.VMEM)
            for v in (out, gin, g_up, g_down, g_qkv, small)
        )
    )


def shards(
    layer_input,
    flags,
    loss_mask,
    cotangent,
    gain_one,
    shift_one,
    w_qkv,
    b_qv,
    w_out,
    b_out,
    gain_two,
    shift_two,
    w_up,
    b_up,
    w_down,
    b_down,
    comm=True,
):
    parts = layer(
        comm,
        layer_input,
        cotangent,
        w_qkv.transpose(0, 2, 1),
        w_out,
        w_up,
        w_down,
        flags,
        loss_mask,
        b_qv,
        gain_one,
        shift_one,
        b_out,
        gain_two,
        shift_two,
        b_up,
        b_down,
    )
    out, gin, g_qkv, g_out, g_up, g_down, g_bqv, *vectors = results(*parts)
    g_gain1, g_shift1, g_bout, g_gain2, g_shift2, g_bup, g_bdown = vectors
    return (
        out.reshape(ROWS, D),
        gin.reshape(ROWS, D),
        g_gain1,
        g_shift1,
        g_qkv.reshape(3, 192, D).transpose(0, 2, 1),
        g_bqv,
        g_out,
        g_bout,
        g_gain2,
        g_shift2,
        g_up,
        g_bup,
        g_down,
        g_bdown,
    )


def solution(mesh):
    in_specs = (
        P("dp", None),
        P("dp"),
        P("dp"),
        P("dp", None),
        P(),
        P(),
        P(None, None, "tensor"),
        P(None, "tensor"),
        P("tensor", None),
        P(),
        P(),
        P(),
        P(None, "tensor"),
        P("tensor"),
        P("tensor", None),
        P(),
    )
    out_specs = (
        P("dp", None),
        P("dp", None),
        P(),
        P(),
        P(None, None, "tensor"),
        P(None, "tensor"),
        P("tensor", None),
        P(),
        P(),
        P(),
        P(None, "tensor"),
        P("tensor"),
        P("tensor", None),
        P(),
    )
    return jax.shard_map(shards, mesh=mesh, in_specs=in_specs, out_specs=out_specs, check_vma=False)
```

```python
import functools

import jax
import jax.numpy as jnp
from jax import lax
from jax.experimental import pallas as pl
from jax.experimental.pallas import tpu as pltpu
from jax.sharding import PartitionSpec as P

MESH = pl.DeviceIdType.MESH
BF = jnp.bfloat16
F32 = jnp.float32
D = 768
HD = 64
LEN = 512
HALF = 256
QUART = 128
SEQS = 3
ROWS = SEQS * LEN
EPS = 1e-05
SCALE = HD**-0.5
GELU_A = 0.7978845608028654
GELU_B = 0.044715

NN = (((1,), (0,)), ((), ()))
NT = (((1,), (1,)), ((), ()))
TN = (((0,), (0,)), ((), ()))

GAIN1, SHIFT1, GAIN2, SHIFT2, BOUT, BDOWN, BUP, BQV = range(8)


def dot(a, b, dims):
    return lax.dot_general(a, b, dims, preferred_element_type=F32)


def norm_parts(v):
    centred = v - jnp.mean(v, axis=1, keepdims=True)
    r = lax.rsqrt(jnp.mean(centred * centred, axis=1, keepdims=True) + EPS)
    return centred * r, r


def norm_back(v, e, gain):
    n, r = norm_parts(v)
    eg = e * gain
    grad = r * (
        eg
        - jnp.mean(eg, axis=1, keepdims=True)
        - n * jnp.mean(eg * n, axis=1, keepdims=True)
    )
    return grad, n


def col_sum(v):
    return jnp.sum(v, axis=0, keepdims=True)


def head_part(v, h):
    lane = lax.broadcasted_iota(jnp.int32, v.shape, 1)
    return jnp.where((lane >= HD * h) & (lane < HD * h + HD), v, jnp.zeros_like(v))


class Place:
    def __init__(self):
        dp = lax.axis_index("dp")
        self.t = t = lax.axis_index("tensor")
        self.z = dp // 8
        self.yl = (dp // 4) % 2
        self.x = dp % 4
        self.c = t % 2
        self.yh = t // 2
        self.t_sib = t + 1 - 2 * self.c
        self.t_part = (t + 2) % 4
        self.t_far = (self.t_sib + 2) % 4
        self.sib = (dp, self.t_sib)
        self.part = (dp, self.t_part)
        self.ypeer = (dp + 4 - 8 * self.yl, t)
        self.dp = dp

    def xpeer(self, j):
        return (self.dp - self.x + (self.x + j) % 4, self.t)

    def zpeer(self, j):
        return (((self.z + j) % 4) * 8 + self.dp % 8, self.t)

    def core_and_x(self, k):
        dp, _ = self.xpeer(k % 4)
        return (dp, self.t if k < 4 else self.t_sib)

    def y_and_z(self, k):
        dp, _ = self.zpeer(k % 4)
        return (dp if k < 4 else dp + 4 - 8 * self.yl, self.t)

    def peers(self):
        return (
            [self.part]
            + [self.core_and_x(k) for k in range(1, 5)]
            + [self.y_and_z(k) for k in range(1, 5)]
        )


def remote(src, dst, send, recv, device):
    return pltpu.make_async_remote_copy(
        src_ref=src,
        dst_ref=dst,
        send_sem=send,
        recv_sem=recv,
        device_id=device,
        device_id_type=MESH,
    )


class Reduction:
    def __init__(self, at, stg, r1, r2, ry, send, recv, free):
        self.at, self.stg, self.r1, self.r2, self.ry = at, stg, r1, r2, ry
        self.send, self.recv, self.free = send, recv, free
        self.big = stg.shape[0] // 4
        self.small = stg.shape[0] // 16

    def axes(self, h):
        at = self.at
        if h == 0:
            return at.x, at.z, at.xpeer, at.zpeer
        return at.z, at.x, at.zpeer, at.xpeer

    def block(self, h, first):
        rows = pl.ds(pl.multiple_of(first * self.big, self.big), self.big)
        return self.stg.at[rows, pl.ds(h * 384, 384)]

    def part(self, h, first, second):
        start = pl.multiple_of(first * self.big + second * self.small, self.small)
        return self.stg.at[pl.ds(start, self.small), pl.ds(h * 384, 384)]

    def copy(self, step, src, dst, device):
        return remote(src, dst, self.send.at[step], self.recv.at[step], device)

    def all_of(self, step):
        ref = (self.r1, self.r2, self.ry, self.r2, self.r1)[step]
        return self.copy(step, ref, ref, self.at.sib)

    def arrived(self, step):
        self.all_of(step).wait_recv()

    def left(self, step):
        self.all_of(step).wait_send()

    def give_back(self, stage):
        self.left(stage)
        for h in (0, 1):
            peer = self.axes(h)[2 + stage]
            for j in (1, 2, 3):
                pl.semaphore_signal(
                    self.free.at[stage], inc=1, device_id=peer(j), device_id_type=MESH
                )

    def start(self):
        for h in (0, 1):
            first, _, peer, _ = self.axes(h)
            for j in (1, 2, 3):
                src = self.block(h, (first + j) % 4)
                self.copy(0, src, self.r1.at[h, j - 1], peer(j)).start()

    def second(self):
        self.arrived(0)
        for h in (0, 1):
            first, second, _, peer = self.axes(h)
            own = self.block(h, first)
            total = own[...].astype(F32)
            for j in (0, 1, 2):
                total = total + self.r1[h, j].astype(F32)
            own[...] = total.astype(BF)
            for j in (1, 2, 3):
                src = self.part(h, first, (second + j) % 4)
                self.copy(1, src, self.r2.at[h, j - 1], peer(j)).start()
        self.give_back(0)

    def third(self):
        self.arrived(1)
        for h in (0, 1):
            first, second, _, _ = self.axes(h)
            own = self.part(h, first, second)
            total = own[...].astype(F32)
            for j in (0, 1, 2):
                total = total + self.r2[h, j].astype(F32)
            own[...] = total.astype(BF)
            self.copy(2, own, self.ry.at[h], self.at.ypeer).start()
        self.give_back(1)

    def fourth(self):
        self.arrived(2)
        self.left(2)
        pl.semaphore_wait(self.free.at[1], 6)
        for h in (0, 1):
            first, second, _, peer = self.axes(h)
            own = self.part(h, first, second)
            own[...] = (own[...].astype(F32) + self.ry[h].astype(F32)).astype(BF)
            for j in (1, 2, 3):
                self.copy(3, own, own, peer(j)).start()

    def fifth(self):
        self.arrived(3)
        pl.semaphore_wait(self.free.at[0], 6)
        for h in (0, 1):
            first, _, peer, _ = self.axes(h)
            own = self.block(h, first)
            for j in (1, 2, 3):
                self.copy(4, own, own, peer(j)).start()

    def finish(self):
        self.arrived(4)

    def drain(self):
        self.left(3)
        self.left(4)


def kernel(
    comm,
    x_hbm,
    cot_hbm,
    wqkv_hbm,
    wout_hbm,
    wup_hbm,
    wdown_hbm,
    flags_hbm,
    mask_hbm,
    bqv_hbm,
    gain1_hbm,
    shift1_hbm,
    bout_hbm,
    gain2_hbm,
    shift2_hbm,
    bup_hbm,
    bdown_hbm,
    res,
    gin,
    stg_u,
    stg_d,
    stg_q,
    small_ref,
    flags_ref,
    mask_ref,
    bqv_ref,
    gain1_ref,
    shift1_ref,
    bout_ref,
    gain2_ref,
    shift2_ref,
    bup_ref,
    bdown_ref,
    x_ref,
    u_ref,
    wqkv,
    wof,
    wup,
    wdown,
    fwup,
    fwdown,
    bias,
    fbias,
    n1,
    q8,
    keys,
    vals,
    att,
    lse,
    mid,
    n2,
    nt2,
    actt,
    own_a,
    own_b,
    s1,
    r1,
    ex,
    mlow,
    gp,
    sc,
    pr,
    ds,
    red1,
    red2,
    redy,
    remy,
    weight,
    sm,
    smp,
    smx,
    smz,
    in_sem,
    a_send,
    a_recv,
    w_send,
    w_recv,
    t_send,
    t_recv,
    x_send,
    x_recv,
    d_send,
    d_recv,
    d_free,
    m_send,
    m_recv,
):
    at = Place()
    c, yh, t = (at.c, at.yh, at.t) if comm else (0, 0, 0)
    ghid = gin
    gpt = nt2.at[0:576]

    def lanes(s, half=None):
        if half is None:
            return pl.ds(pl.multiple_of(s * LEN, LEN), LEN)
        return pl.ds(pl.multiple_of(s * LEN + half * HALF, HALF), HALF)

    def core_rows(core):
        return pl.ds(pl.multiple_of(core * QUART, QUART), QUART)

    def flat(v):
        return v.reshape(-1, v.shape[-1])

    def wout_rows(t, start, count):
        return wof.at[pl.ds(pl.multiple_of(t * 192 + start, 48), count)]

    def wout_block(t):
        return wout_rows(t, 0, 192)

    def att_block(s):
        def block(t):
            return att.at[s, pl.ds(pl.multiple_of(t * 192, 192), 192)]

        block.rows = 192
        return block

    def row_block(ref, s):
        def block(t):
            return ref.at[s, t // 2, t % 2]

        block.rows = QUART
        return block

    def load(i, src, dst):
        return pltpu.make_async_copy(src, dst, in_sem.at[i])

    def load_x(s):
        return load(s, x_hbm.at[s], x_ref.at[s])

    load_wqkv = load(3, wqkv_hbm, wqkv)
    load_wout = load(4, wout_hbm, wout_block(t))
    load_cot = load(5, cot_hbm, u_ref)
    load_up = load(6, wup_hbm, wup)
    load_down = load(7, wdown_hbm, wdown)
    small_loads = [
        load(8 + i, src, dst)
        for i, (src, dst) in enumerate(
            (
                (gain1_hbm, gain1_ref),
                (shift1_hbm, shift1_ref),
                (bqv_hbm, bqv_ref),
                (bup_hbm, bup_ref),
                (flags_hbm, flags_ref),
                (mask_hbm, mask_ref),
                (bout_hbm, bout_ref),
                (gain2_hbm, gain2_ref),
                (shift2_hbm, shift2_ref),
                (bdown_hbm, bdown_ref),
            )
        )
    ]
    load_x(0).start()
    load_wqkv.start()
    if comm:
        barrier = pltpu.get_barrier_semaphore()
        peers = at.peers()
        for peer in peers:
            pl.semaphore_signal(barrier, inc=1, device_id=peer, device_id_type=MESH)
    for copy in small_loads:
        copy.start()
    load_wout.start()
    load_up.start()
    load_down.start()
    load_x(1).start()
    load_x(2).start()
    load_cot.start()
    sm[...] = jnp.zeros_like(sm)
    for copy in small_loads:
        copy.wait()
    bias[...] = jnp.broadcast_to(bup_ref[...].reshape(1, D), (8, D))
    weight[...] = jnp.maximum(flags_ref[...], mask_ref[...]).astype(F32).reshape(2 * SEQS, HALF)

    def fetch_part(i, count):
        first, second = (at.x, at.z) if i == 0 else (at.z, at.x)
        start = (second * 4 + (first if count == 1 else 0)) * 48
        return pl.ds(pl.multiple_of(start, 48), 48 * count)

    def fetch_copy(step, src, dst, device):
        return remote(src, dst, w_send.at[step], w_recv.at[step], device)

    def fetch_y(i):
        if i == 2:
            ref = wout_rows(t, at.x * 48, 48)
            return fetch_copy(0, ref, ref, at.part)
        src, dst = ((wup, fwup), (wdown, fwdown))[i]
        some = fetch_part(i, 1)
        return fetch_copy(1, src.at[some], dst.at[some], at.part)

    def fetch_a(i, j):
        peer = at.zpeer if i == 1 else at.xpeer
        if i == 2:
            ref = wout_rows(at.t_part, at.x * 48, 48)
            return fetch_copy(3, ref, ref, peer(j))
        ref = (fwup, fwdown)[i].at[fetch_part(i, 1)]
        return fetch_copy(4, ref, ref, peer(j))

    def fetch_b(i, j):
        peer = at.xpeer if i == 1 else at.zpeer
        ref = (fwup, fwdown)[i].at[fetch_part(i, 4)]
        return fetch_copy(5, ref, ref, peer(j))

    def fetch_all(step):
        ref = (wof.at[0:48], fwup.at[0:96], fbias, wof.at[0:144], fwup.at[0:288], nt2.at[0:576])[step]
        return fetch_copy(step, ref, ref, at.part)

    def fetch_first(kinds):
        if comm:
            for i in kinds:
                fetch_y(i).start()
            if 0 in kinds:
                fetch_copy(2, bias, fbias, at.part).start()

    def fetch_second(kinds):
        if comm:
            fetch_all(0 if 2 in kinds else 1).wait_recv()
            for i in kinds:
                for j in (1, 2, 3):
                    fetch_a(i, j).start()

    def fetch_third(kinds):
        if comm:
            fetch_all(3 if 2 in kinds else 4).wait_recv()
            for i in kinds:
                if i < 2:
                    for j in (1, 2, 3):
                        fetch_b(i, j).start()

    def fetch_wait():
        if comm:
            fetch_all(2).wait_recv()
            fetch_all(5).wait_recv()

    def fetch_left():
        if comm:
            for step in (0, 1, 2):
                fetch_all(step).wait_send()

    def fetch_drain():
        if comm:
            for step in (3, 4, 5):
                fetch_all(step).wait_send()

    def gather_copy(i, block, kind, t, device):
        ref = block(t)
        return remote(ref, ref, a_send.at[i], a_recv.at[i, kind], device)

    def gather_start(i, block):
        if comm:
            if not isinstance(i, int) or i != 3:
                gather_copy(i, block, 1, at.t, at.part).start()
            gather_copy(i, block, 0, at.t, at.sib).start()

    def gather_forward(i, block):
        if comm:
            if not isinstance(i, int) or i != 3:
                gather_copy(i, block, 1, at.t_part, at.part).wait_recv()
            gather_copy(i, block, 0, at.t_part, at.sib).start()

    def gather_all(i, block, count):
        if block is wout_block:
            ref = wof.at[0 : 192 * count]
        elif block.rows == 192:
            ref = att.at[0, 0 : 192 * count]
        else:
            ref = n1.at[0, 0 : QUART * count]
        return remote(ref, ref, a_send.at[i], a_recv.at[i, 0], at.sib)

    def gather_wait(i, block):
        if comm:
            gather_all(i, block, 2).wait_recv()

    def gather_drain(i, block):
        if comm:
            gather_all(i, block, 2 if block is wout_block else 3).wait_send()

    def core_copy(k, s):
        return remote(s1.at[k, s - 1], r1.at[k, s - 1], t_send.at[k, s - 1], t_recv.at[k, s - 1], at.sib)

    def core_sum(k, s, own):
        if comm:
            core_copy(k, s).wait()
        return own[s, core_rows(c), :] + r1[k, s - 1].astype(F32)

    def slot(kind, i):
        if isinstance(i, int) and i >= SEQS:
            return ex.at[kind, i - SEQS]
        rows = pl.ds(pl.multiple_of(i * HALF, HALF), HALF)
        if kind % 2 == 0:
            return actt.at[rows, pl.ds(kind // 2 * D, D)]
        return (wup, wdown)[kind // 2].at[rows]

    def chip_copy(i):
        return remote(slot(0, i), slot(1, i), x_send.at[0, i], x_recv.at[0, i], at.sib)

    def group_copy(i):
        return remote(slot(2, i), slot(3, i), x_send.at[1, i], x_recv.at[1, i], at.part)

    def share_copy(i, ref, s, core):
        some = ref.at[s, :, core]
        return remote(some, some, x_send.at[2, i], x_recv.at[2, i], at.sib)

    def chip_sum(i, own):
        if comm:
            chip_copy(i).wait()
        slot(2, i)[...] = (own[...] + slot(1, i)[...].astype(F32)).astype(BF)
        if comm:
            group_copy(i).start()

    def group_sum(i):
        if comm:
            group_copy(i).wait()
        return slot(2, i)[...].astype(F32) + slot(3, i)[...].astype(F32)

    def share(i, ref, s):
        if comm:
            share_copy(i, ref, s, c).start()

    def share_wait(i, ref, s):
        if comm:
            share_copy(i, ref, s, 1 - c).wait_recv()

    def core_part(v, core):
        return jnp.where(core == 0, v[:QUART], v[QUART:])

    def chip_rows_sum(v):
        return jnp.where(yh == 0, col_sum(v[:QUART]), col_sum(v[QUART:]))

    gain1, shift1, gain2, shift2, b_out, b_down = (
        ref[...].reshape(1, D)
        for ref in (gain1_ref, shift1_ref, gain2_ref, shift2_ref, bout_ref, bdown_ref)
    )

    def add_small(row, value):
        sm[row : row + 1, :] += value

    def project(s):
        load_x(s).wait()
        for half in range(2):
            n, _r = norm_parts(flat(x_ref[s, half]).astype(F32))
            n1[s, HALF * half : HALF * half + HALF, :] = (n * gain1 + shift1).astype(BF)
        normed = n1[s]
        q = (dot(normed, wqkv[0], NT) + bqv_ref[0:1, :]).astype(BF) * SCALE
        q8[s] = q
        k = dot(normed, wqkv[1], NT).astype(BF)
        keys[s] = k
        v = (dot(normed, wqkv[2], NT) + bqv_ref[1:2, :]).astype(BF)
        vals[s] = v

    def attend(s):
        q, k, vt = q8[s], keys[s], vals[s].T
        block = att_block(s)(t)
        for h in range(3):
            sc[...] = dot(head_part(k, h), q, NT)
            for part in range(4):
                cols = slice(part * 128, part * 128 + 128)
                scores = sc[:, cols]
                top = jnp.max(scores, axis=0, keepdims=True)
                e = jnp.exp(scores - top)
                total = col_sum(e)
                lse[3 * s + h, :, cols] = top + jnp.log(total)
                pr[:, cols] = (e * (1.0 / total)).astype(BF)
            mixed = dot(vt[HD * h : HD * h + HD], pr[...], NN)
            block[HD * h : HD * h + HD, :] = mixed.astype(BF)
        gather_start(s, att_block(s))

    def weigh(i, _):
        same = lax.broadcasted_iota(jnp.int32, (HALF, HALF), 0) == lax.broadcasted_iota(
            jnp.int32, (HALF, HALF), 1
        )
        diagonal = jnp.where(same, weight[pl.ds(i, 1), :], 0.0).astype(BF)
        rows = dot(diagonal, flat(u_ref[i // 2, i % 2]), NN).astype(BF)
        u_ref[i // 2, i % 2] = rows.reshape(2, QUART, D)
        return 0

    def hidden_units(normed, up, w_up, b_up, w_down):
        v = dot(normed, w_up[...], NN) + b_up
        back = dot(up, w_down[...], NT)
        square = v * v
        th = jnp.tanh(v * (GELU_A + (GELU_A * GELU_B) * square))
        cdf = 0.5 + 0.5 * th
        inner = v * (0.5 * GELU_A + (1.5 * GELU_A * GELU_B) * square)
        return (v * cdf).astype(BF), back * (cdf + inner * (1.0 - th * th))

    def feed(s, between):
        gather_wait(s, att_block(s))
        for own in (False, True):
            half = yh if own else 1 - yh
            some = lanes(s, half)
            cols = pl.ds(pl.multiple_of(half * HALF, HALF), HALF)
            middle = flat(x_ref[s, half]).astype(F32) + dot(att[s, :, cols], wof[...], TN) + b_out
            n, _r = norm_parts(middle)
            normed = (n * gain2 + shift2).astype(BF)
            nt2[:, some] = normed.T
            act, grad = hidden_units(normed, flat(u_ref[s, half]), wup, bias[0:1, :], wdown)
            add_small(BUP, col_sum(grad))
            grad = grad.astype(BF)
            actt[:, some] = act.T
            ghid[s, half] = grad.reshape(2, QUART, D)
            if own:
                between(1)
            if isinstance(s, int):
                piece = pl.ds(pl.multiple_of(half * QUART, QUART), QUART)
                mid[s, piece, :] = core_part(middle, c)
                for k, (ref, total) in enumerate(
                    ((own_a, dot(grad, wup[...], NT)), (own_b, dot(act, wdown[...], NN)))
                ):
                    ref[s, piece, :] = core_part(total, c)
                    slot(0, 3 + k)[piece, :] = core_part(total, 1 - c).astype(BF)
            elif own:
                mid[s] = middle
                n2[s - 1] = normed
                own_a[s] = dot(grad, wup[...], NT)
                own_b[s] = dot(act, wdown[...], NN)
            if not own:
                between(0)
        if isinstance(s, int) and comm:
            chip_copy(3).start()
            chip_copy(4).start()

    def feed_more(s):
        act, grad = hidden_units(n2[s - 1], flat(u_ref[s, yh]), fwup, fbias[0:1, :], fwdown)
        own_a[s] += dot(grad.astype(BF), fwup[...], NT)
        own_b[s] += dot(act, fwdown[...], NN)
        for k, ref in enumerate((own_a, own_b)):
            s1[k, s - 1] = ref[s, core_rows(1 - c), :].astype(BF)
            if comm:
                core_copy(k, s).start()

    def middle_back(s):
        e = core_sum(0, s, own_a)
        grad, n = norm_back(mid[s, core_rows(c), :], e, gain2)
        add_small(GAIN2, col_sum(e * n))
        add_small(SHIFT2, col_sum(e))
        up = u_ref[s, yh, c].astype(F32)
        grad = up + grad
        add_small(BOUT, col_sum(grad))
        add_small(BDOWN, col_sum(up))
        mlow[s, yh, c] = grad.astype(BF)
        gather_start(4 + s, row_block(mlow, s))

    def middle_back_first():
        e = group_sum(3)
        grad, n = norm_back(mid[0], e, gain2)
        add_small(GAIN2, chip_rows_sum(e * n))
        add_small(SHIFT2, chip_rows_sum(e))
        up = flat(u_ref[0, :, c]).astype(F32)
        grad = up + grad
        add_small(BOUT, chip_rows_sum(grad))
        add_small(BDOWN, chip_rows_sum(up))
        mlow[0, :, c] = grad.astype(BF).reshape(2, QUART, D)
        share(3, mlow, 0)

    def output_rows_first():
        total = mid[0] + group_sum(4) + b_down
        res[0, :, c] = total.astype(BF).reshape(2, QUART, D)
        share(4, res, 0)

    def output_rows(s):
        total = mid[s, core_rows(c), :] + core_sum(1, s, own_b) + b_down
        res[s, yh, c] = total.astype(BF)
        gather_start(7 + s, row_block(res, s))

    def reduction(i, ref, wide):
        if wide:
            r1, r2, ry = red1.at[i], red2.at[i], redy.at[i]
        else:
            j = i - 2
            r1 = red1.at[0, :, :, pl.ds(j * 64, 64)]
            r2 = red2.at[0, :, :, pl.ds(j * 16, 16)]
            ry = remy.at[j]
        return Reduction(at, ref, r1, r2, ry, d_send.at[i], d_recv.at[i], d_free.at[i])

    d_up, d_down = reduction(0, stg_u, True), reduction(1, stg_d, True)
    d_att = [reduction(2 + i, stg_q.at[pl.ds(i * HALF, HALF)], False) for i in range(3)]

    def reduce_step(name, which):
        if comm:
            getattr(which, name)()

    def stage(stg, start, count, value):
        stg[pl.ds(start, count), :] = value.astype(BF)

    def up_grads(i, _):
        start = pl.multiple_of(i * HALF, HALF)
        some = pl.ds(start, HALF)
        stage(stg_u, start, HALF, dot(nt2[some, :], flat(ghid[...]), NN))
        return 0

    def down_grads(i, _):
        start = pl.multiple_of(i * HALF, HALF)
        some = pl.ds(start, HALF)
        stage(stg_d, start, HALF, dot(actt[some, :], flat(u_ref[...]), NN))
        return 0

    def qkv_grads(start, count):
        stage(stg_q, start, count, dot(gpt[start : start + count, :], flat(n1[...]), NN))

    def out_grads():
        total = jnp.zeros((192, D), F32)
        for s in range(SEQS):
            total += dot(att_block(s)(t)[...], flat(mlow[s]), NN)
        stage(stg_q, 576, 192, total)

    def attend_back(s, between):
        some_lanes = lanes(s)
        mixed = dot(flat(mlow[s]), wout_block(t)[...], NT).astype(BF)
        q, k, v = q8[s], keys[s], vals[s]
        kt = k.T
        grad_k = jnp.zeros((LEN, 192), F32)
        grad_v = jnp.zeros((LEN, 192), F32)
        for h in range(3):
            sc[...] = dot(head_part(k, h), q, NT)
            back = dot(head_part(v, h), mixed, NT)
            some = slice(HD * h, HD * h + HD)
            for part in range(4):
                cols = slice(part * 128, part * 128 + 128)
                p = jnp.exp(sc[:, cols] - lse[3 * s + h, :, cols])
                pr[:, cols] = p.astype(BF)
                gp_part = back[:, cols]
                total = col_sum(gp_part * p)
                ds[:, cols] = (p * (gp_part - total)).astype(BF)
            grad_v += dot(pr[...], head_part(mixed, h), NN)
            grad_k += dot(ds[...], head_part(q, h), NN)
            gpt[some, some_lanes] = (dot(kt[some], ds[...], NN) * SCALE).astype(BF)
            between(h)
        grad_q = gpt[0:192, some_lanes].T
        grad_k = grad_k.astype(BF)
        grad_v = grad_v.astype(BF)
        gpt[192:384, some_lanes] = grad_k.T
        gpt[384:576, some_lanes] = grad_v.T
        for i, grad in enumerate((grad_q, grad_k, grad_v)):
            gp[i] = grad.reshape(2, 2, QUART, 192)
        sm[BQV : BQV + 1, 0:192] += col_sum(grad_q.astype(F32))
        sm[BQV : BQV + 1, 256:448] += col_sum(grad_v.astype(F32))
        for own in (False, True):
            core = c if own else 1 - c
            total = dot(flat(gp[0, :, core]), wqkv[0], NN)
            total += dot(flat(gp[1, :, core]), wqkv[1], NN)
            total += dot(flat(gp[2, :, core]), wqkv[2], NN)
            if own:
                own_a[s] = total
            else:
                slot(0, s)[...] = total.astype(BF)
                if comm:
                    chip_copy(s).start()

    def input_back(s):
        e = group_sum(s)
        grad, n = norm_back(flat(x_ref[s, :, c]).astype(F32), e, gain1)
        add_small(GAIN1, chip_rows_sum(e * n))
        add_small(SHIFT1, chip_rows_sum(e))
        total = flat(mlow[s, :, c]).astype(F32) + grad
        gin[s, :, c] = total.astype(BF).reshape(2, QUART, D)
        share(s, gin, s)

    LAST = SEQS - 1

    def last_copy():
        src = slot(2, LAST).at[core_rows(1 - yh)]
        dst = slot(3, LAST).at[0:QUART]
        return remote(src, dst, x_send.at[1, LAST], x_recv.at[1, LAST], at.part)

    def chip_sum_last():
        if comm:
            chip_copy(LAST).wait()
        total = own_a[LAST] + slot(1, LAST)[...].astype(F32)
        own_a[LAST] = total
        slot(2, LAST)[...] = total.astype(BF)
        if comm:
            last_copy().start()

    def input_back_last():
        if comm:
            last_copy().wait()
        e = own_a[LAST, core_rows(yh), :] + slot(3, LAST)[0:QUART, :].astype(F32)
        grad, n = norm_back(x_ref[LAST, yh, c].astype(F32), e, gain1)
        add_small(GAIN1, col_sum(e * n))
        add_small(SHIFT1, col_sum(e))
        small_part()
        gin[LAST, yh, c] = (mlow[LAST, yh, c].astype(F32) + grad).astype(BF)
        gather_start(7, row_block(gin, LAST))

    def small_copy(i, slots, slot, device):
        ref = slots.at[slot]
        return remote(ref, ref, m_send.at[i], m_recv.at[i], device)

    def small_row():
        return lax.broadcasted_iota(jnp.int32, (8, D), 0)

    def small_part():
        smp[yh] = sm[...]
        if comm:
            small_copy(0, smp, yh, at.part).start()

    def small_all(i, slots):
        return remote(slots.at[0:7], slots.at[0:7], m_send.at[i], m_recv.at[i], at.sib)

    def first_slot():
        return at.c * 4 + at.x

    def second_slot():
        return at.yl * 4 + at.z

    def small_first():
        small_copy(0, smp, 1 - yh, at.part).wait_recv()
        smx[first_slot()] = jnp.where(small_row() < BUP, smp[0] + smp[1], sm[...])
        for k in range(1, 8):
            small_copy(1, smx, first_slot(), at.core_and_x(k)).start()

    def small_second():
        small_all(1, smx).wait_recv()
        cores = [
            (smx[4 * i] + smx[4 * i + 1]) + (smx[4 * i + 2] + smx[4 * i + 3]) for i in (0, 1)
        ]
        mine = jnp.where(c == 0, cores[0], cores[1])
        smz[second_slot()] = jnp.where(small_row() < BUP, cores[0] + cores[1], mine)
        for k in range(1, 8):
            small_copy(2, smz, second_slot(), at.y_and_z(k)).start()

    def small_end():
        small_all(2, smz).wait_recv()
        total = smz[0]
        for i in range(1, 8):
            total = total + smz[i]
        small_ref[...] = total

    def small_drain():
        small_copy(0, smp, yh, at.part).wait_send()
        small_all(1, smx).wait_send()
        small_all(2, smz).wait_send()

    load_wqkv.wait()
    project(0)
    load_wout.wait()
    load_up.wait()
    load_down.wait()
    if comm:
        pl.semaphore_wait(barrier, len(peers))
    fetch_first((2,))
    gather_start(3, wout_block)

    def attend_all(s, _):
        @pl.when(s > 0)
        def _():
            project(s)

        @pl.when(s == 1)
        def _():
            fetch_second((2,))

        attend(s)

        @pl.when(s == 0)
        def _():
            fetch_first((0, 1))

        return 0

    lax.fori_loop(0, SEQS, attend_all, 0)
    load_cot.wait()
    lax.fori_loop(0, 2, weigh, 0)
    fetch_third((2,))
    gather_forward(3, wout_block)
    lax.fori_loop(2, 2 * SEQS, weigh, 0)
    gather_forward(0, att_block(0))
    fetch_second((0, 1))
    gather_wait(3, wout_block)

    def feed_first(slot):
        if slot == 1:
            gather_forward(1, att_block(1))

    feed(0, feed_first)
    fetch_third((0, 1))

    def feed_all(s, _):
        def between(slot):
            @pl.when(s == 1)
            def _():
                if slot == 0:
                    chip_sum(3, own_a.at[0])
                    chip_sum(4, own_b.at[0])
                else:
                    gather_forward(2, att_block(2))

        feed(s, between)
        return 0

    lax.fori_loop(1, SEQS, feed_all, 0)
    fetch_left()
    lax.fori_loop(0, 3, up_grads, 0)
    reduce_step("start", d_up)
    lax.fori_loop(0, 3, down_grads, 0)
    middle_back_first()
    fetch_wait()
    feed_more(1)
    feed_more(2)
    middle_back(1)
    fetch_drain()
    gather_drain(3, wout_block)
    for s in range(SEQS):
        gather_drain(s, att_block(s))
    middle_back(2)
    share_wait(3, mlow, 0)

    def attend_back_all(s, _):
        def between(h):
            if h == 0:

                @pl.when(s == 0)
                def _():
                    reduce_step("second", d_up)
                    reduce_step("start", d_down)

                @pl.when(s == 2)
                def _():
                    reduce_step("fifth", d_up)
                    chip_sum(1, own_a.at[1])

            if h == 1:

                @pl.when(s == 0)
                def _():
                    output_rows_first()

                @pl.when(s == 1)
                def _():
                    gather_forward(6, row_block(mlow, 2))
                    reduce_step("fourth", d_up)

                @pl.when(s == 2)
                def _():
                    reduce_step("third", d_down)

            if h == 2:

                @pl.when(s == 1)
                def _():
                    reduce_step("second", d_down)

        attend_back(s, between)

        @pl.when(s == 0)
        def _():
            gather_forward(5, row_block(mlow, 1))
            reduce_step("third", d_up)
            chip_sum(0, own_a.at[0])
            gather_wait(5, row_block(mlow, 1))

        @pl.when(s == 1)
        def _():
            gather_wait(6, row_block(mlow, 2))

        return 0

    lax.fori_loop(0, SEQS, attend_back_all, 0)
    qkv_grads(0, HALF)
    reduce_step("start", d_att[0])
    chip_sum_last()
    qkv_grads(HALF, HALF)
    reduce_step("start", d_att[1])
    qkv_grads(2 * HALF, 64)
    out_grads()
    reduce_step("start", d_att[2])
    output_rows(1)
    input_back(0)
    for s in (1, 2):
        gather_drain(4 + s, row_block(mlow, s))
    reduce_step("fourth", d_down)
    for part in d_att:
        reduce_step("second", part)
    reduce_step("fifth", d_down)
    input_back(1)
    for part in d_att:
        reduce_step("third", part)
    input_back_last()
    output_rows(2)
    for part in d_att:
        reduce_step("fourth", part)
    if comm:
        small_first()
    for s in range(LAST):
        share_wait(s, gin, s)
    share_wait(4, res, 0)
    for part in d_att:
        reduce_step("fifth", part)
    if comm:
        small_second()
    gather_forward(8, row_block(res, 1))
    gather_forward(7, row_block(gin, LAST))
    reduce_step("finish", d_up)
    reduce_step("drain", d_up)
    if comm:
        for i, ref, s in ((0, gin, 0), (1, gin, 1), (3, mlow, 0), (4, res, 0)):
            share_copy(i, ref, s, c).wait_send()
    gather_forward(9, row_block(res, 2))
    reduce_step("finish", d_down)
    reduce_step("drain", d_down)
    for i, ref, s in ((7, gin, LAST), (8, res, 1), (9, res, 2)):
        gather_wait(i, row_block(ref, s))
        gather_drain(i, row_block(ref, s))
    if comm:
        small_end()
        small_drain()
    else:
        small_ref[...] = sm[...]
    for part in d_att:
        reduce_step("finish", part)
        reduce_step("drain", part)


def layer(comm, x, cot, *rest):
    rows = (SEQS, 2, 2, QUART, D)
    half = (SEQS, HALF, D)
    dma = pltpu.SemaphoreType.DMA
    scratch = [
        pltpu.VMEM((ROWS,), jnp.int32),
        pltpu.VMEM((ROWS,), jnp.int32),
        pltpu.VMEM((2, 192), F32),
        pltpu.VMEM((D,), F32),
        pltpu.VMEM((D,), F32),
        pltpu.VMEM((D,), F32),
        pltpu.VMEM((D,), F32),
        pltpu.VMEM((D,), F32),
        pltpu.VMEM((D,), F32),
        pltpu.VMEM((D,), F32),
        pltpu.VMEM(rows, BF),
        pltpu.VMEM(rows, BF),
        pltpu.VMEM((3, 192, D), BF),
        pltpu.VMEM((D, D), BF),
        pltpu.VMEM((D, D), BF),
        pltpu.VMEM((D, D), BF),
        pltpu.VMEM((D, D), BF),
        pltpu.VMEM((D, D), BF),
        pltpu.VMEM((8, D), F32),
        pltpu.VMEM((8, D), F32),
        pltpu.VMEM((SEQS, LEN, D), BF),
        pltpu.VMEM((SEQS, LEN, 192), BF),
        pltpu.VMEM((SEQS, LEN, 192), BF),
        pltpu.VMEM((SEQS, LEN, 192), BF),
        pltpu.VMEM((SEQS, D, LEN), BF),
        pltpu.VMEM((3 * SEQS, 1, LEN), F32),
        pltpu.VMEM(half, F32),
        pltpu.VMEM((SEQS - 1, HALF, D), BF),
        pltpu.VMEM((D, ROWS), BF),
        pltpu.VMEM((D, ROWS), BF),
        pltpu.VMEM(half, F32),
        pltpu.VMEM(half, F32),
        pltpu.VMEM((2, SEQS - 1, QUART, D), BF),
        pltpu.VMEM((2, SEQS - 1, QUART, D), BF),
        pltpu.VMEM((4, 2, HALF, D), BF),
        pltpu.VMEM(rows, BF),
        pltpu.VMEM((3, 2, 2, QUART, 192), BF),
        pltpu.VMEM((LEN, LEN), F32),
        pltpu.VMEM((LEN, LEN), BF),
        pltpu.VMEM((LEN, LEN), BF),
        pltpu.VMEM((2, 2, 3, 192, 384), BF),
        pltpu.VMEM((2, 2, 3, 48, 384), BF),
        pltpu.VMEM((2, 2, 48, 384), BF),
        pltpu.VMEM((3, 2, 16, 384), BF),
        pltpu.VMEM((2 * SEQS, HALF), F32),
        pltpu.VMEM((8, D), F32),
        pltpu.VMEM((2, 8, D), F32),
        pltpu.VMEM((8, 8, D), F32),
        pltpu.VMEM((8, 8, D), F32),
        dma((18,)),
        dma((10,)),
        dma((10, 2)),
        dma((6,)),
        dma((6,)),
        dma((2, SEQS - 1)),
        dma((2, SEQS - 1)),
        dma((3, 5)),
        dma((3, 5)),
        dma((5, 5)),
        dma((5, 5)),
        pltpu.SemaphoreType.REGULAR((5, 2)),
        dma((3,)),
        dma((3,)),
    ]
    anywhere = pl.BlockSpec(memory_space=pl.ANY)
    vmem = pl.BlockSpec(memory_space=pltpu.VMEM)
    return pl.pallas_call(
        functools.partial(kernel, comm),
        out_shape=(
            pltpu.VMEM(rows, BF),
            pltpu.VMEM(rows, BF),
            pltpu.VMEM((D, D), BF),
            pltpu.VMEM((D, D), BF),
            pltpu.VMEM((D, D), BF),
            pltpu.VMEM((8, D), F32),
        ),
        in_specs=[anywhere] * 16,
        out_specs=(vmem,) * 6,
        scratch_shapes=scratch,
        compiler_params=pltpu.CompilerParams(
            collective_id=0 if comm else None,
            has_side_effects=True,
            vmem_limit_bytes=55 * 2**20,
        ),
        cost_estimate=pl.CostEstimate(
            flops=20 * 10**9, bytes_accessed=20 * 10**6, transcendentals=10**7
        ),
        name="layer",
    )(x.reshape(rows), cot.reshape(rows), *rest)


def results(out, gin, g_up, g_down, g_qkv, small):
    def kernel(out, gin, up, down, qkv, small, *rest):
        (out_to, gin_to, qkv_to, out_w_to, up_to, down_to, bqv_to), rest = rest[:7], rest[7:]
        vectors, (wide, narrow, pair, sem) = rest[:7], rest[7:]
        copies = []

        def start(i, src, dst):
            copy = pltpu.make_async_copy(src, dst, sem.at[i])
            copy.start()
            copies.append(copy)

        start(0, out, out_to)
        start(1, gin, gin_to)
        for i, (src, first, rows, dst) in enumerate(
            (
                (up, 0, D, up_to),
                (down, 0, D, down_to),
                (qkv, 0, 576, qkv_to),
                (qkv, 576, 192, out_w_to),
            )
        ):
            at = (0, D, 2 * D, 2 * D + 576)[i]
            wide[at : at + rows, :] = src[first : first + rows, :].astype(F32)
            start(2 + i, wide.at[pl.ds(at, rows)], dst)
        for i, row in enumerate((GAIN1, SHIFT1, BOUT, GAIN2, SHIFT2, BUP, BDOWN)):
            narrow[i][...] = small[row : row + 1, :].reshape(D)
            start(6 + i, narrow[i], vectors[i])
        pair[0:1, :] = small[BQV : BQV + 1, 0:192]
        pair[1:2, :] = small[BQV : BQV + 1, 256:448]
        start(13, pair, bqv_to)
        for copy in copies:
            copy.wait()

    anywhere = pl.BlockSpec(memory_space=pl.ANY)
    vmem = pl.BlockSpec(memory_space=pltpu.VMEM)

    def shape(*dims, dtype=F32):
        return jax.ShapeDtypeStruct(dims, dtype)

    return pl.pallas_call(
        kernel,
        out_shape=(
            shape(*out.shape, dtype=BF),
            shape(*gin.shape, dtype=BF),
            shape(576, D),
            shape(192, D),
            shape(D, D),
            shape(D, D),
            shape(2, 192),
        )
        + (shape(D),) * 7,
        in_specs=[vmem] * 6,
        out_specs=(anywhere,) * 14,
        scratch_shapes=[
            pltpu.VMEM((3 * D, D), F32),
            [pltpu.VMEM((D,), F32)] * 7,
            pltpu.VMEM((2, 192), F32),
            pltpu.SemaphoreType.DMA((14,)),
        ],
        compiler_params=pltpu.CompilerParams(vmem_limit_bytes=12 * 2**20),
        name="results",
    )(
        *(
            pltpu.with_memory_space_constraint(v, pltpu.VMEM)
            for v in (out, gin, g_up, g_down, g_qkv, small)
        )
    )


def shards(
    layer_input,
    flags,
    loss_mask,
    cotangent,
    gain_one,
    shift_one,
    w_qkv,
    b_qv,
    w_out,
    b_out,
    gain_two,
    shift_two,
    w_up,
    b_up,
    w_down,
    b_down,
    comm=True,
):
    parts = layer(
        comm,
        layer_input,
        cotangent,
        w_qkv.transpose(0, 2, 1),
        w_out,
        w_up,
        w_down,
        flags,
        loss_mask,
        b_qv,
        gain_one,
        shift_one,
        b_out,
        gain_two,
        shift_two,
        b_up,
        b_down,
    )
    out, gin, g_qkv, g_out, g_up, g_down, g_bqv, *vectors = results(*parts)
    g_gain1, g_shift1, g_bout, g_gain2, g_shift2, g_bup, g_bdown = vectors
    return (
        out.reshape(ROWS, D),
        gin.reshape(ROWS, D),
        g_gain1,
        g_shift1,
        g_qkv.reshape(3, 192, D).transpose(0, 2, 1),
        g_bqv,
        g_out,
        g_bout,
        g_gain2,
        g_shift2,
        g_up,
        g_bup,
        g_down,
        g_bdown,
    )


def solution(mesh):
    in_specs = (
        P("dp", None),
        P("dp"),
        P("dp"),
        P("dp", None),
        P(),
        P(),
        P(None, None, "tensor"),
        P(None, "tensor"),
        P("tensor", None),
        P(),
        P(),
        P(),
        P(None, "tensor"),
        P("tensor"),
        P("tensor", None),
        P(),
    )
    out_specs = (
        P("dp", None),
        P("dp", None),
        P(),
        P(),
        P(None, None, "tensor"),
        P(None, "tensor"),
        P("tensor", None),
        P(),
        P(),
        P(),
        P(None, "tensor"),
        P("tensor"),
        P("tensor", None),
        P(),
    )
    return jax.shard_map(shards, mesh=mesh, in_specs=in_specs, out_specs=out_specs, check_vma=False)
```

```python
import functools

import jax
import jax.numpy as jnp
from jax import lax
from jax.experimental import pallas as pl
from jax.experimental.pallas import tpu as pltpu
from jax.sharding import PartitionSpec as P

MESH = pl.DeviceIdType.MESH
BF = jnp.bfloat16
F32 = jnp.float32
D = 768
HD = 64
LEN = 512
HALF = 256
QUART = 128
SEQS = 3
ROWS = SEQS * LEN
EPS = 1e-05
SCALE = HD**-0.5
GELU_A = 0.7978845608028654
GELU_B = 0.044715

NN = (((1,), (0,)), ((), ()))
NT = (((1,), (1,)), ((), ()))
TN = (((0,), (0,)), ((), ()))

GAIN1, SHIFT1, GAIN2, SHIFT2, BOUT, BDOWN, BUP, BQV = range(8)


def dot(a, b, dims):
    return lax.dot_general(a, b, dims, preferred_element_type=F32)


def norm_parts(v):
    centred = v - jnp.mean(v, axis=1, keepdims=True)
    r = lax.rsqrt(jnp.mean(centred * centred, axis=1, keepdims=True) + EPS)
    return centred * r, r


def norm_back(v, e, gain):
    n, r = norm_parts(v)
    eg = e * gain
    grad = r * (
        eg
        - jnp.mean(eg, axis=1, keepdims=True)
        - n * jnp.mean(eg * n, axis=1, keepdims=True)
    )
    return grad, n


def col_sum(v):
    return jnp.sum(v, axis=0, keepdims=True)


def head_part(v, h):
    lane = lax.broadcasted_iota(jnp.int32, v.shape, 1)
    return jnp.where((lane >= HD * h) & (lane < HD * h + HD), v, jnp.zeros_like(v))


class Place:
    def __init__(self):
        dp = lax.axis_index("dp")
        self.t = t = lax.axis_index("tensor")
        self.z = dp // 8
        self.yl = (dp // 4) % 2
        self.x = dp % 4
        self.c = t % 2
        self.yh = t // 2
        self.t_sib = t + 1 - 2 * self.c
        self.t_part = (t + 2) % 4
        self.t_far = (self.t_sib + 2) % 4
        self.sib = (dp, self.t_sib)
        self.part = (dp, self.t_part)
        self.ypeer = (dp + 4 - 8 * self.yl, t)
        self.near = (dp + 4 - 8 * self.yl, self.t_part)
        self.dp = dp

    def xpeer(self, j):
        return (self.dp - self.x + (self.x + j) % 4, self.t)

    def zpeer(self, j):
        return (((self.z + j) % 4) * 8 + self.dp % 8, self.t)

    def core_and_x(self, k):
        dp, _ = self.xpeer(k % 4)
        return (dp, self.t if k < 4 else self.t_sib)

    def y_and_z(self, k):
        dp, _ = self.zpeer(k % 4)
        return (dp if k < 4 else dp + 4 - 8 * self.yl, self.t)

    def peers(self):
        return (
            [self.part, self.near]
            + [self.core_and_x(k) for k in range(1, 5)]
            + [self.y_and_z(k) for k in range(1, 5)]
        )


def remote(src, dst, send, recv, device):
    return pltpu.make_async_remote_copy(
        src_ref=src,
        dst_ref=dst,
        send_sem=send,
        recv_sem=recv,
        device_id=device,
        device_id_type=MESH,
    )


class Reduction:
    def __init__(self, at, stg, r1, r2, ry, send, recv, free):
        self.at, self.stg, self.r1, self.r2, self.ry = at, stg, r1, r2, ry
        self.send, self.recv, self.free = send, recv, free
        self.big = stg.shape[0] // 4
        self.small = stg.shape[0] // 16

    def axes(self, h):
        at = self.at
        if h == 0:
            return at.x, at.z, at.xpeer, at.zpeer
        return at.z, at.x, at.zpeer, at.xpeer

    def block(self, h, first):
        rows = pl.ds(pl.multiple_of(first * self.big, self.big), self.big)
        return self.stg.at[rows, pl.ds(h * 384, 384)]

    def part(self, h, first, second):
        start = pl.multiple_of(first * self.big + second * self.small, self.small)
        return self.stg.at[pl.ds(start, self.small), pl.ds(h * 384, 384)]

    def copy(self, step, src, dst, device):
        return remote(src, dst, self.send.at[step], self.recv.at[step], device)

    def all_of(self, step):
        ref = (self.r1, self.r2, self.ry, self.r2, self.r1)[step]
        return self.copy(step, ref, ref, self.at.sib)

    def arrived(self, step):
        self.all_of(step).wait_recv()

    def left(self, step):
        self.all_of(step).wait_send()

    def give_back(self, stage):
        self.left(stage)
        for h in (0, 1):
            peer = self.axes(h)[2 + stage]
            for j in (1, 2, 3):
                pl.semaphore_signal(
                    self.free.at[stage], inc=1, device_id=peer(j), device_id_type=MESH
                )

    def start(self):
        for h in (0, 1):
            first, _, peer, _ = self.axes(h)
            for j in (1, 2, 3):
                src = self.block(h, (first + j) % 4)
                self.copy(0, src, self.r1.at[h, j - 1], peer(j)).start()

    def second(self):
        self.arrived(0)
        for h in (0, 1):
            first, second, _, peer = self.axes(h)
            own = self.block(h, first)
            total = own[...].astype(F32)
            for j in (0, 1, 2):
                total = total + self.r1[h, j].astype(F32)
            own[...] = total.astype(BF)
            for j in (1, 2, 3):
                src = self.part(h, first, (second + j) % 4)
                self.copy(1, src, self.r2.at[h, j - 1], peer(j)).start()
        self.give_back(0)

    def third(self):
        self.arrived(1)
        for h in (0, 1):
            first, second, _, _ = self.axes(h)
            own = self.part(h, first, second)
            total = own[...].astype(F32)
            for j in (0, 1, 2):
                total = total + self.r2[h, j].astype(F32)
            own[...] = total.astype(BF)
            self.copy(2, own, self.ry.at[h], self.at.ypeer).start()
        self.give_back(1)

    def fourth(self):
        self.arrived(2)
        self.left(2)
        pl.semaphore_wait(self.free.at[1], 6)
        for h in (0, 1):
            first, second, _, peer = self.axes(h)
            own = self.part(h, first, second)
            own[...] = (own[...].astype(F32) + self.ry[h].astype(F32)).astype(BF)
            for j in (1, 2, 3):
                self.copy(3, own, own, peer(j)).start()

    def fifth(self):
        self.arrived(3)
        pl.semaphore_wait(self.free.at[0], 6)
        for h in (0, 1):
            first, _, peer, _ = self.axes(h)
            own = self.block(h, first)
            for j in (1, 2, 3):
                self.copy(4, own, own, peer(j)).start()

    def finish(self):
        self.arrived(4)

    def drain(self):
        self.left(3)
        self.left(4)


def kernel(
    comm,
    x_hbm,
    cot_hbm,
    wqkv_hbm,
    wout_hbm,
    wup_hbm,
    wdown_hbm,
    flags_hbm,
    mask_hbm,
    bqv_hbm,
    gain1_hbm,
    shift1_hbm,
    bout_hbm,
    gain2_hbm,
    shift2_hbm,
    bup_hbm,
    bdown_hbm,
    res,
    gin,
    stg_u,
    stg_d,
    stg_q,
    small_ref,
    flags_ref,
    mask_ref,
    bqv_ref,
    gain1_ref,
    shift1_ref,
    bout_ref,
    gain2_ref,
    shift2_ref,
    bup_ref,
    bdown_ref,
    x_ref,
    u_ref,
    wqkv,
    wof,
    wup,
    wdown,
    fwup,
    fwdown,
    bias,
    fbias,
    n1,
    q8,
    keys,
    vals,
    att,
    lse,
    mid,
    n2,
    nt2,
    actt,
    own_a,
    own_b,
    s1,
    r1,
    ex,
    mlow,
    gp,
    sc,
    pr,
    ds,
    red1,
    red2,
    redy,
    remy,
    weight,
    sm,
    smp,
    smx,
    smz,
    in_sem,
    a_send,
    a_recv,
    w_send,
    w_recv,
    t_send,
    t_recv,
    x_send,
    x_recv,
    d_send,
    d_recv,
    d_free,
    m_send,
    m_recv,
):
    at = Place()
    c, yh, t = (at.c, at.yh, at.t) if comm else (0, 0, 0)
    ghid = gin
    gpt = nt2.at[0:576]

    def lanes(s, half=None):
        if half is None:
            return pl.ds(pl.multiple_of(s * LEN, LEN), LEN)
        return pl.ds(pl.multiple_of(s * LEN + half * HALF, HALF), HALF)

    def core_rows(core):
        return pl.ds(pl.multiple_of(core * QUART, QUART), QUART)

    def flat(v):
        return v.reshape(-1, v.shape[-1])

    def wout_rows(t, start, count):
        return wof.at[pl.ds(pl.multiple_of(t * 192 + start, 48), count)]

    def wout_block(t):
        return wout_rows(t, 0, 192)

    def att_block(s):
        def block(t):
            return att.at[s, pl.ds(pl.multiple_of(t * 192, 192), 192)]

        block.rows = 192
        return block

    def row_block(ref, s):
        def block(t):
            return ref.at[s, t // 2, t % 2]

        block.rows = QUART
        return block

    def load(i, src, dst):
        return pltpu.make_async_copy(src, dst, in_sem.at[i])

    def load_x(s):
        return load(s, x_hbm.at[s], x_ref.at[s])

    load_wqkv = load(3, wqkv_hbm, wqkv)
    load_wout = load(4, wout_hbm, wout_block(t))
    load_cot = load(5, cot_hbm, u_ref)
    load_up = load(6, wup_hbm, wup)
    load_down = load(7, wdown_hbm, wdown)
    small_loads = [
        load(8 + i, src, dst)
        for i, (src, dst) in enumerate(
            (
                (gain1_hbm, gain1_ref),
                (shift1_hbm, shift1_ref),
                (bqv_hbm, bqv_ref),
                (bup_hbm, bup_ref),
                (flags_hbm, flags_ref),
                (mask_hbm, mask_ref),
                (bout_hbm, bout_ref),
                (gain2_hbm, gain2_ref),
                (shift2_hbm, shift2_ref),
                (bdown_hbm, bdown_ref),
            )
        )
    ]
    load_x(0).start()
    load_wqkv.start()
    if comm:
        barrier = pltpu.get_barrier_semaphore()
        peers = at.peers()
        for peer in peers:
            pl.semaphore_signal(barrier, inc=1, device_id=peer, device_id_type=MESH)
    for copy in small_loads:
        copy.start()
    load_wout.start()
    load_up.start()
    load_down.start()
    load_x(1).start()
    load_x(2).start()
    load_cot.start()
    sm[...] = jnp.zeros_like(sm)
    for copy in small_loads:
        copy.wait()
    bias[...] = jnp.broadcast_to(bup_ref[...].reshape(1, D), (8, D))
    weight[...] = jnp.maximum(flags_ref[...], mask_ref[...]).astype(F32).reshape(2 * SEQS, HALF)

    def fetch_part(i, count):
        first, second = (at.x, at.z) if i == 0 else (at.z, at.x)
        start = (second * 4 + (first if count == 1 else 0)) * 48
        return pl.ds(pl.multiple_of(start, 48), 48 * count)

    def fetch_copy(step, src, dst, device):
        return remote(src, dst, w_send.at[step], w_recv.at[step], device)

    def fetch_y(i):
        if i == 2:
            ref = wout_rows(t, at.x * 48, 48)
            return fetch_copy(0, ref, ref, at.near)
        src, dst = ((wup, fwup), (wdown, fwdown))[i]
        some = fetch_part(i, 1)
        return fetch_copy(1, src.at[some], dst.at[some], at.part)

    def fetch_a(i, j):
        peer = at.zpeer if i == 1 else at.xpeer
        if i == 2:
            ref = wout_rows(at.t_part, at.x * 48, 48)
            return fetch_copy(3, ref, ref, peer(j))
        ref = (fwup, fwdown)[i].at[fetch_part(i, 1)]
        return fetch_copy(4, ref, ref, peer(j))

    def fetch_b(i, j):
        peer = at.xpeer if i == 1 else at.zpeer
        ref = (fwup, fwdown)[i].at[fetch_part(i, 4)]
        return fetch_copy(5, ref, ref, peer(j))

    def fetch_all(step):
        ref = (wof.at[0:48], fwup.at[0:96], fbias, wof.at[0:144], fwup.at[0:288], nt2.at[0:576])[step]
        return fetch_copy(step, ref, ref, at.part)

    def fetch_first(kinds):
        if comm:
            for i in kinds:
                fetch_y(i).start()
            if 0 in kinds:
                fetch_copy(2, bias, fbias, at.part).start()

    def fetch_second(kinds):
        if comm:
            fetch_all(0 if 2 in kinds else 1).wait_recv()
            for i in kinds:
                for j in (1, 2, 3):
                    fetch_a(i, j).start()

    def fetch_third(kinds):
        if comm:
            fetch_all(3 if 2 in kinds else 4).wait_recv()
            for i in kinds:
                if i < 2:
                    for j in (1, 2, 3):
                        fetch_b(i, j).start()

    def fetch_wait():
        if comm:
            fetch_all(2).wait_recv()
            fetch_all(5).wait_recv()

    def fetch_left():
        if comm:
            for step in (0, 1, 2):
                fetch_all(step).wait_send()

    def fetch_drain():
        if comm:
            for step in (3, 4, 5):
                fetch_all(step).wait_send()

    def gather_copy(i, block, kind, t, device):
        ref = block(t)
        return remote(ref, ref, a_send.at[i], a_recv.at[i, kind], device)

    def gather_start(i, block):
        if comm:
            if not isinstance(i, int) or i != 3:
                gather_copy(i, block, 1, at.t, at.part).start()
            gather_copy(i, block, 0, at.t, at.sib).start()

    def gather_forward(i, block):
        if comm:
            if not isinstance(i, int) or i != 3:
                gather_copy(i, block, 1, at.t_part, at.part).wait_recv()
            gather_copy(i, block, 0, at.t_part, at.sib).start()

    def gather_all(i, block, count):
        if block is wout_block:
            ref = wof.at[0 : 192 * count]
        elif block.rows == 192:
            ref = att.at[0, 0 : 192 * count]
        else:
            ref = n1.at[0, 0 : QUART * count]
        return remote(ref, ref, a_send.at[i], a_recv.at[i, 0], at.sib)

    def gather_wait(i, block):
        if comm:
            gather_all(i, block, 2).wait_recv()

    def gather_drain(i, block):
        if comm:
            gather_all(i, block, 2 if block is wout_block else 3).wait_send()

    def core_copy(k, s):
        return remote(s1.at[k, s - 1], r1.at[k, s - 1], t_send.at[k, s - 1], t_recv.at[k, s - 1], at.sib)

    def core_sum(k, s, own):
        if comm:
            core_copy(k, s).wait()
        return own[s, core_rows(c), :] + r1[k, s - 1].astype(F32)

    def slot(kind, i):
        if isinstance(i, int) and i >= SEQS:
            return ex.at[kind, i - SEQS]
        rows = pl.ds(pl.multiple_of(i * HALF, HALF), HALF)
        if kind % 2 == 0:
            return actt.at[rows, pl.ds(kind // 2 * D, D)]
        return (wup, wdown)[kind // 2].at[rows]

    def chip_copy(i):
        return remote(slot(0, i), slot(1, i), x_send.at[0, i], x_recv.at[0, i], at.sib)

    def group_copy(i):
        return remote(slot(2, i), slot(3, i), x_send.at[1, i], x_recv.at[1, i], at.part)

    def share_copy(i, ref, s, core):
        some = ref.at[s, :, core]
        return remote(some, some, x_send.at[2, i], x_recv.at[2, i], at.sib)

    def chip_sum(i, own):
        if comm:
            chip_copy(i).wait()
        slot(2, i)[...] = (own[...] + slot(1, i)[...].astype(F32)).astype(BF)
        if comm:
            group_copy(i).start()

    def group_sum(i):
        if comm:
            group_copy(i).wait()
        return slot(2, i)[...].astype(F32) + slot(3, i)[...].astype(F32)

    def share(i, ref, s):
        if comm:
            share_copy(i, ref, s, c).start()

    def share_wait(i, ref, s):
        if comm:
            share_copy(i, ref, s, 1 - c).wait_recv()

    def core_part(v, core):
        return jnp.where(core == 0, v[:QUART], v[QUART:])

    def chip_rows_sum(v):
        return jnp.where(yh == 0, col_sum(v[:QUART]), col_sum(v[QUART:]))

    gain1, shift1, gain2, shift2, b_out, b_down = (
        ref[...].reshape(1, D)
        for ref in (gain1_ref, shift1_ref, gain2_ref, shift2_ref, bout_ref, bdown_ref)
    )

    def add_small(row, value):
        sm[row : row + 1, :] += value

    def project(s):
        load_x(s).wait()
        for half in range(2):
            n, _r = norm_parts(flat(x_ref[s, half]).astype(F32))
            n1[s, HALF * half : HALF * half + HALF, :] = (n * gain1 + shift1).astype(BF)
        normed = n1[s]
        q = (dot(normed, wqkv[0], NT) + bqv_ref[0:1, :]).astype(BF) * SCALE
        q8[s] = q
        k = dot(normed, wqkv[1], NT).astype(BF)
        keys[s] = k
        v = (dot(normed, wqkv[2], NT) + bqv_ref[1:2, :]).astype(BF)
        vals[s] = v

    def attend(s):
        q, k, vt = q8[s], keys[s], vals[s].T
        block = att_block(s)(t)
        for h in range(3):
            sc[...] = dot(head_part(k, h), q, NT)
            for part in range(4):
                cols = slice(part * 128, part * 128 + 128)
                scores = sc[:, cols]
                top = jnp.max(scores, axis=0, keepdims=True)
                e = jnp.exp(scores - top)
                total = col_sum(e)
                lse[3 * s + h, :, cols] = top + jnp.log(total)
                pr[:, cols] = (e * (1.0 / total)).astype(BF)
            mixed = dot(vt[HD * h : HD * h + HD], pr[...], NN)
            block[HD * h : HD * h + HD, :] = mixed.astype(BF)
        gather_start(s, att_block(s))

    def weigh(i, _):
        same = lax.broadcasted_iota(jnp.int32, (HALF, HALF), 0) == lax.broadcasted_iota(
            jnp.int32, (HALF, HALF), 1
        )
        diagonal = jnp.where(same, weight[pl.ds(i, 1), :], 0.0).astype(BF)
        rows = dot(diagonal, flat(u_ref[i // 2, i % 2]), NN).astype(BF)
        u_ref[i // 2, i % 2] = rows.reshape(2, QUART, D)
        return 0

    def hidden_units(normed, up, w_up, b_up, w_down):
        v = dot(normed, w_up[...], NN) + b_up
        back = dot(up, w_down[...], NT)
        square = v * v
        th = jnp.tanh(v * (GELU_A + (GELU_A * GELU_B) * square))
        cdf = 0.5 + 0.5 * th
        inner = v * (0.5 * GELU_A + (1.5 * GELU_A * GELU_B) * square)
        return (v * cdf).astype(BF), back * (cdf + inner * (1.0 - th * th))

    def feed(s, between):
        gather_wait(s, att_block(s))
        for own in (False, True):
            half = yh if own else 1 - yh
            some = lanes(s, half)
            cols = pl.ds(pl.multiple_of(half * HALF, HALF), HALF)
            middle = flat(x_ref[s, half]).astype(F32) + dot(att[s, :, cols], wof[...], TN) + b_out
            n, _r = norm_parts(middle)
            normed = (n * gain2 + shift2).astype(BF)
            nt2[:, some] = normed.T
            act, grad = hidden_units(normed, flat(u_ref[s, half]), wup, bias[0:1, :], wdown)
            add_small(BUP, col_sum(grad))
            grad = grad.astype(BF)
            actt[:, some] = act.T
            ghid[s, half] = grad.reshape(2, QUART, D)
            if own:
                between(1)
            if isinstance(s, int):
                piece = pl.ds(pl.multiple_of(half * QUART, QUART), QUART)
                mid[s, piece, :] = core_part(middle, c)
                for k, (ref, total) in enumerate(
                    ((own_a, dot(grad, wup[...], NT)), (own_b, dot(act, wdown[...], NN)))
                ):
                    ref[s, piece, :] = core_part(total, c)
                    slot(0, 3 + k)[piece, :] = core_part(total, 1 - c).astype(BF)
            elif own:
                mid[s] = middle
                n2[s - 1] = normed
                own_a[s] = dot(grad, wup[...], NT)
                own_b[s] = dot(act, wdown[...], NN)
            if not own:
                between(0)
        if isinstance(s, int) and comm:
            chip_copy(3).start()
            chip_copy(4).start()

    def feed_more(s):
        act, grad = hidden_units(n2[s - 1], flat(u_ref[s, yh]), fwup, fbias[0:1, :], fwdown)
        own_a[s] += dot(grad.astype(BF), fwup[...], NT)
        own_b[s] += dot(act, fwdown[...], NN)
        for k, ref in enumerate((own_a, own_b)):
            s1[k, s - 1] = ref[s, core_rows(1 - c), :].astype(BF)
            if comm:
                core_copy(k, s).start()

    def middle_back(s):
        e = core_sum(0, s, own_a)
        grad, n = norm_back(mid[s, core_rows(c), :], e, gain2)
        add_small(GAIN2, col_sum(e * n))
        add_small(SHIFT2, col_sum(e))
        up = u_ref[s, yh, c].astype(F32)
        grad = up + grad
        add_small(BOUT, col_sum(grad))
        add_small(BDOWN, col_sum(up))
        mlow[s, yh, c] = grad.astype(BF)
        gather_start(4 + s, row_block(mlow, s))

    def middle_back_first():
        e = group_sum(3)
        grad, n = norm_back(mid[0], e, gain2)
        add_small(GAIN2, chip_rows_sum(e * n))
        add_small(SHIFT2, chip_rows_sum(e))
        up = flat(u_ref[0, :, c]).astype(F32)
        grad = up + grad
        add_small(BOUT, chip_rows_sum(grad))
        add_small(BDOWN, chip_rows_sum(up))
        mlow[0, :, c] = grad.astype(BF).reshape(2, QUART, D)
        share(3, mlow, 0)

    def output_rows_first():
        total = mid[0] + group_sum(4) + b_down
        res[0, :, c] = total.astype(BF).reshape(2, QUART, D)
        share(4, res, 0)

    def output_rows(s):
        total = mid[s, core_rows(c), :] + core_sum(1, s, own_b) + b_down
        res[s, yh, c] = total.astype(BF)
        gather_start(7 + s, row_block(res, s))

    def reduction(i, ref, wide):
        if wide:
            r1, r2, ry = red1.at[i], red2.at[i], redy.at[i]
        else:
            j = i - 2
            r1 = red1.at[0, :, :, pl.ds(j * 64, 64)]
            r2 = red2.at[0, :, :, pl.ds(j * 16, 16)]
            ry = remy.at[j]
        return Reduction(at, ref, r1, r2, ry, d_send.at[i], d_recv.at[i], d_free.at[i])

    d_up, d_down = reduction(0, stg_u, True), reduction(1, stg_d, True)
    d_att = [reduction(2 + i, stg_q.at[pl.ds(i * HALF, HALF)], False) for i in range(3)]

    def reduce_step(name, which):
        if comm:
            getattr(which, name)()

    def stage(stg, start, count, value):
        stg[pl.ds(start, count), :] = value.astype(BF)

    def up_grads(i, _):
        start = pl.multiple_of(i * HALF, HALF)
        some = pl.ds(start, HALF)
        stage(stg_u, start, HALF, dot(nt2[some, :], flat(ghid[...]), NN))
        return 0

    def down_grads(i, _):
        start = pl.multiple_of(i * HALF, HALF)
        some = pl.ds(start, HALF)
        stage(stg_d, start, HALF, dot(actt[some, :], flat(u_ref[...]), NN))
        return 0

    def qkv_grads(start, count):
        stage(stg_q, start, count, dot(gpt[start : start + count, :], flat(n1[...]), NN))

    def out_grads():
        total = jnp.zeros((192, D), F32)
        for s in range(SEQS):
            total += dot(att_block(s)(t)[...], flat(mlow[s]), NN)
        stage(stg_q, 576, 192, total)

    def attend_back(s, between):
        some_lanes = lanes(s)
        mixed = dot(flat(mlow[s]), wout_block(t)[...], NT).astype(BF)
        q, k, v = q8[s], keys[s], vals[s]
        kt = k.T
        grad_k = jnp.zeros((LEN, 192), F32)
        grad_v = jnp.zeros((LEN, 192), F32)
        for h in range(3):
            sc[...] = dot(head_part(k, h), q, NT)
            back = dot(head_part(v, h), mixed, NT)
            some = slice(HD * h, HD * h + HD)
            for part in range(4):
                cols = slice(part * 128, part * 128 + 128)
                p = jnp.exp(sc[:, cols] - lse[3 * s + h, :, cols])
                pr[:, cols] = p.astype(BF)
                gp_part = back[:, cols]
                total = col_sum(gp_part * p)
                ds[:, cols] = (p * (gp_part - total)).astype(BF)
            grad_v += dot(pr[...], head_part(mixed, h), NN)
            grad_k += dot(ds[...], head_part(q, h), NN)
            gpt[some, some_lanes] = (dot(kt[some], ds[...], NN) * SCALE).astype(BF)
            between(h)
        grad_q = gpt[0:192, some_lanes].T
        grad_k = grad_k.astype(BF)
        grad_v = grad_v.astype(BF)
        gpt[192:384, some_lanes] = grad_k.T
        gpt[384:576, some_lanes] = grad_v.T
        for i, grad in enumerate((grad_q, grad_k, grad_v)):
            gp[i] = grad.reshape(2, 2, QUART, 192)
        sm[BQV : BQV + 1, 0:192] += col_sum(grad_q.astype(F32))
        sm[BQV : BQV + 1, 256:448] += col_sum(grad_v.astype(F32))
        for own in (False, True):
            core = c if own else 1 - c
            total = dot(flat(gp[0, :, core]), wqkv[0], NN)
            total += dot(flat(gp[1, :, core]), wqkv[1], NN)
            total += dot(flat(gp[2, :, core]), wqkv[2], NN)
            if own:
                own_a[s] = total
            else:
                slot(0, s)[...] = total.astype(BF)
                if comm:
                    chip_copy(s).start()

    def input_back(s):
        e = group_sum(s)
        grad, n = norm_back(flat(x_ref[s, :, c]).astype(F32), e, gain1)
        add_small(GAIN1, chip_rows_sum(e * n))
        add_small(SHIFT1, chip_rows_sum(e))
        total = flat(mlow[s, :, c]).astype(F32) + grad
        gin[s, :, c] = total.astype(BF).reshape(2, QUART, D)
        share(s, gin, s)

    LAST = SEQS - 1

    def last_copy():
        src = slot(2, LAST).at[core_rows(1 - yh)]
        dst = slot(3, LAST).at[0:QUART]
        return remote(src, dst, x_send.at[1, LAST], x_recv.at[1, LAST], at.part)

    def chip_sum_last():
        if comm:
            chip_copy(LAST).wait()
        total = own_a[LAST] + slot(1, LAST)[...].astype(F32)
        own_a[LAST] = total
        slot(2, LAST)[...] = total.astype(BF)
        if comm:
            last_copy().start()

    def input_back_last():
        if comm:
            last_copy().wait()
        e = own_a[LAST, core_rows(yh), :] + slot(3, LAST)[0:QUART, :].astype(F32)
        grad, n = norm_back(x_ref[LAST, yh, c].astype(F32), e, gain1)
        add_small(GAIN1, col_sum(e * n))
        add_small(SHIFT1, col_sum(e))
        small_part()
        gin[LAST, yh, c] = (mlow[LAST, yh, c].astype(F32) + grad).astype(BF)
        gather_start(7, row_block(gin, LAST))

    def small_copy(i, slots, slot, device):
        ref = slots.at[slot]
        return remote(ref, ref, m_send.at[i], m_recv.at[i], device)

    def small_row():
        return lax.broadcasted_iota(jnp.int32, (8, D), 0)

    def small_part():
        smp[yh] = sm[...]
        if comm:
            small_copy(0, smp, yh, at.part).start()

    def small_all(i, slots):
        return remote(slots.at[0:7], slots.at[0:7], m_send.at[i], m_recv.at[i], at.sib)

    def first_slot():
        return at.c * 4 + at.x

    def second_slot():
        return at.yl * 4 + at.z

    def small_first():
        small_copy(0, smp, 1 - yh, at.part).wait_recv()
        smx[first_slot()] = jnp.where(small_row() < BUP, smp[0] + smp[1], sm[...])
        for k in range(1, 8):
            small_copy(1, smx, first_slot(), at.core_and_x(k)).start()

    def small_second():
        small_all(1, smx).wait_recv()
        cores = [
            (smx[4 * i] + smx[4 * i + 1]) + (smx[4 * i + 2] + smx[4 * i + 3]) for i in (0, 1)
        ]
        mine = jnp.where(c == 0, cores[0], cores[1])
        smz[second_slot()] = jnp.where(small_row() < BUP, cores[0] + cores[1], mine)
        for k in range(1, 8):
            small_copy(2, smz, second_slot(), at.y_and_z(k)).start()

    def small_end():
        small_all(2, smz).wait_recv()
        total = smz[0]
        for i in range(1, 8):
            total = total + smz[i]
        small_ref[...] = total

    def small_drain():
        small_copy(0, smp, yh, at.part).wait_send()
        small_all(1, smx).wait_send()
        small_all(2, smz).wait_send()

    load_wqkv.wait()
    project(0)
    load_wout.wait()
    load_up.wait()
    load_down.wait()
    if comm:
        pl.semaphore_wait(barrier, len(peers))
    fetch_first((2,))
    gather_start(3, wout_block)

    def attend_all(s, _):
        @pl.when(s > 0)
        def _():
            project(s)

        @pl.when(s == 1)
        def _():
            fetch_second((2,))

        attend(s)

        @pl.when(s == 0)
        def _():
            fetch_first((0, 1))

        return 0

    lax.fori_loop(0, SEQS, attend_all, 0)
    load_cot.wait()
    lax.fori_loop(0, 2, weigh, 0)
    fetch_third((2,))
    gather_forward(3, wout_block)
    lax.fori_loop(2, 2 * SEQS, weigh, 0)
    gather_forward(0, att_block(0))
    fetch_second((0, 1))
    gather_wait(3, wout_block)

    def feed_first(slot):
        if slot == 1:
            gather_forward(1, att_block(1))

    feed(0, feed_first)
    fetch_third((0, 1))

    def feed_all(s, _):
        def between(slot):
            @pl.when(s == 1)
            def _():
                if slot == 0:
                    chip_sum(3, own_a.at[0])
                    chip_sum(4, own_b.at[0])
                else:
                    gather_forward(2, att_block(2))

        feed(s, between)
        return 0

    lax.fori_loop(1, SEQS, feed_all, 0)
    fetch_left()
    lax.fori_loop(0, 3, up_grads, 0)
    reduce_step("start", d_up)
    lax.fori_loop(0, 3, down_grads, 0)
    middle_back_first()
    fetch_wait()
    feed_more(1)
    feed_more(2)
    middle_back(1)
    fetch_drain()
    gather_drain(3, wout_block)
    for s in range(SEQS):
        gather_drain(s, att_block(s))
    middle_back(2)
    share_wait(3, mlow, 0)

    def attend_back_all(s, _):
        def between(h):
            if h == 0:

                @pl.when(s == 0)
                def _():
                    reduce_step("second", d_up)
                    reduce_step("start", d_down)

                @pl.when(s == 2)
                def _():
                    reduce_step("fifth", d_up)
                    chip_sum(1, own_a.at[1])

            if h == 1:

                @pl.when(s == 0)
                def _():
                    output_rows_first()

                @pl.when(s == 1)
                def _():
                    gather_forward(6, row_block(mlow, 2))
                    reduce_step("fourth", d_up)

                @pl.when(s == 2)
                def _():
                    reduce_step("third", d_down)

            if h == 2:

                @pl.when(s == 1)
                def _():
                    reduce_step("second", d_down)

        attend_back(s, between)

        @pl.when(s == 0)
        def _():
            gather_forward(5, row_block(mlow, 1))
            reduce_step("third", d_up)
            chip_sum(0, own_a.at[0])
            gather_wait(5, row_block(mlow, 1))

        @pl.when(s == 1)
        def _():
            gather_wait(6, row_block(mlow, 2))

        return 0

    lax.fori_loop(0, SEQS, attend_back_all, 0)
    qkv_grads(0, HALF)
    reduce_step("start", d_att[0])
    chip_sum_last()
    qkv_grads(HALF, HALF)
    reduce_step("start", d_att[1])
    qkv_grads(2 * HALF, 64)
    out_grads()
    reduce_step("start", d_att[2])
    output_rows(1)
    input_back(0)
    for s in (1, 2):
        gather_drain(4 + s, row_block(mlow, s))
    reduce_step("fourth", d_down)
    for part in d_att:
        reduce_step("second", part)
    reduce_step("fifth", d_down)
    input_back(1)
    for part in d_att:
        reduce_step("third", part)
    input_back_last()
    output_rows(2)
    for part in d_att:
        reduce_step("fourth", part)
    if comm:
        small_first()
    for s in range(LAST):
        share_wait(s, gin, s)
    share_wait(4, res, 0)
    for part in d_att:
        reduce_step("fifth", part)
    if comm:
        small_second()
    gather_forward(8, row_block(res, 1))
    gather_forward(7, row_block(gin, LAST))
    reduce_step("finish", d_up)
    reduce_step("drain", d_up)
    if comm:
        for i, ref, s in ((0, gin, 0), (1, gin, 1), (3, mlow, 0), (4, res, 0)):
            share_copy(i, ref, s, c).wait_send()
    gather_forward(9, row_block(res, 2))
    reduce_step("finish", d_down)
    reduce_step("drain", d_down)
    for i, ref, s in ((7, gin, LAST), (8, res, 1), (9, res, 2)):
        gather_wait(i, row_block(ref, s))
        gather_drain(i, row_block(ref, s))
    if comm:
        small_end()
        small_drain()
    else:
        small_ref[...] = sm[...]
    for part in d_att:
        reduce_step("finish", part)
        reduce_step("drain", part)


def layer(comm, x, cot, *rest):
    rows = (SEQS, 2, 2, QUART, D)
    half = (SEQS, HALF, D)
    dma = pltpu.SemaphoreType.DMA
    scratch = [
        pltpu.VMEM((ROWS,), jnp.int32),
        pltpu.VMEM((ROWS,), jnp.int32),
        pltpu.VMEM((2, 192), F32),
        pltpu.VMEM((D,), F32),
        pltpu.VMEM((D,), F32),
        pltpu.VMEM((D,), F32),
        pltpu.VMEM((D,), F32),
        pltpu.VMEM((D,), F32),
        pltpu.VMEM((D,), F32),
        pltpu.VMEM((D,), F32),
        pltpu.VMEM(rows, BF),
        pltpu.VMEM(rows, BF),
        pltpu.VMEM((3, 192, D), BF),
        pltpu.VMEM((D, D), BF),
        pltpu.VMEM((D, D), BF),
        pltpu.VMEM((D, D), BF),
        pltpu.VMEM((D, D), BF),
        pltpu.VMEM((D, D), BF),
        pltpu.VMEM((8, D), F32),
        pltpu.VMEM((8, D), F32),
        pltpu.VMEM((SEQS, LEN, D), BF),
        pltpu.VMEM((SEQS, LEN, 192), BF),
        pltpu.VMEM((SEQS, LEN, 192), BF),
        pltpu.VMEM((SEQS, LEN, 192), BF),
        pltpu.VMEM((SEQS, D, LEN), BF),
        pltpu.VMEM((3 * SEQS, 1, LEN), F32),
        pltpu.VMEM(half, F32),
        pltpu.VMEM((SEQS - 1, HALF, D), BF),
        pltpu.VMEM((D, ROWS), BF),
        pltpu.VMEM((D, ROWS), BF),
        pltpu.VMEM(half, F32),
        pltpu.VMEM(half, F32),
        pltpu.VMEM((2, SEQS - 1, QUART, D), BF),
        pltpu.VMEM((2, SEQS - 1, QUART, D), BF),
        pltpu.VMEM((4, 2, HALF, D), BF),
        pltpu.VMEM(rows, BF),
        pltpu.VMEM((3, 2, 2, QUART, 192), BF),
        pltpu.VMEM((LEN, LEN), F32),
        pltpu.VMEM((LEN, LEN), BF),
        pltpu.VMEM((LEN, LEN), BF),
        pltpu.VMEM((2, 2, 3, 192, 384), BF),
        pltpu.VMEM((2, 2, 3, 48, 384), BF),
        pltpu.VMEM((2, 2, 48, 384), BF),
        pltpu.VMEM((3, 2, 16, 384), BF),
        pltpu.VMEM((2 * SEQS, HALF), F32),
        pltpu.VMEM((8, D), F32),
        pltpu.VMEM((2, 8, D), F32),
        pltpu.VMEM((8, 8, D), F32),
        pltpu.VMEM((8, 8, D), F32),
        dma((18,)),
        dma((10,)),
        dma((10, 2)),
        dma((6,)),
        dma((6,)),
        dma((2, SEQS - 1)),
        dma((2, SEQS - 1)),
        dma((3, 5)),
        dma((3, 5)),
        dma((5, 5)),
        dma((5, 5)),
        pltpu.SemaphoreType.REGULAR((5, 2)),
        dma((3,)),
        dma((3,)),
    ]
    anywhere = pl.BlockSpec(memory_space=pl.ANY)
    vmem = pl.BlockSpec(memory_space=pltpu.VMEM)
    return pl.pallas_call(
        functools.partial(kernel, comm),
        out_shape=(
            pltpu.VMEM(rows, BF),
            pltpu.VMEM(rows, BF),
            pltpu.VMEM((D, D), BF),
            pltpu.VMEM((D, D), BF),
            pltpu.VMEM((D, D), BF),
            pltpu.VMEM((8, D), F32),
        ),
        in_specs=[anywhere] * 16,
        out_specs=(vmem,) * 6,
        scratch_shapes=scratch,
        compiler_params=pltpu.CompilerParams(
            collective_id=0 if comm else None,
            has_side_effects=True,
            vmem_limit_bytes=55 * 2**20,
        ),
        cost_estimate=pl.CostEstimate(
            flops=20 * 10**9, bytes_accessed=20 * 10**6, transcendentals=10**7
        ),
        name="layer",
    )(x.reshape(rows), cot.reshape(rows), *rest)


def results(out, gin, g_up, g_down, g_qkv, small):
    def kernel(out, gin, up, down, qkv, small, *rest):
        (out_to, gin_to, qkv_to, out_w_to, up_to, down_to, bqv_to), rest = rest[:7], rest[7:]
        vectors, (wide, narrow, pair, sem) = rest[:7], rest[7:]
        copies = []

        def start(i, src, dst):
            copy = pltpu.make_async_copy(src, dst, sem.at[i])
            copy.start()
            copies.append(copy)

        start(0, out, out_to)
        start(1, gin, gin_to)
        for i, (src, first, rows, dst) in enumerate(
            (
                (up, 0, D, up_to),
                (down, 0, D, down_to),
                (qkv, 0, 576, qkv_to),
                (qkv, 576, 192, out_w_to),
            )
        ):
            at = (0, D, 2 * D, 2 * D + 576)[i]
            wide[at : at + rows, :] = src[first : first + rows, :].astype(F32)
            start(2 + i, wide.at[pl.ds(at, rows)], dst)
        for i, row in enumerate((GAIN1, SHIFT1, BOUT, GAIN2, SHIFT2, BUP, BDOWN)):
            narrow[i][...] = small[row : row + 1, :].reshape(D)
            start(6 + i, narrow[i], vectors[i])
        pair[0:1, :] = small[BQV : BQV + 1, 0:192]
        pair[1:2, :] = small[BQV : BQV + 1, 256:448]
        start(13, pair, bqv_to)
        for copy in copies:
            copy.wait()

    anywhere = pl.BlockSpec(memory_space=pl.ANY)
    vmem = pl.BlockSpec(memory_space=pltpu.VMEM)

    def shape(*dims, dtype=F32):
        return jax.ShapeDtypeStruct(dims, dtype)

    return pl.pallas_call(
        kernel,
        out_shape=(
            shape(*out.shape, dtype=BF),
            shape(*gin.shape, dtype=BF),
            shape(576, D),
            shape(192, D),
            shape(D, D),
            shape(D, D),
            shape(2, 192),
        )
        + (shape(D),) * 7,
        in_specs=[vmem] * 6,
        out_specs=(anywhere,) * 14,
        scratch_shapes=[
            pltpu.VMEM((3 * D, D), F32),
            [pltpu.VMEM((D,), F32)] * 7,
            pltpu.VMEM((2, 192), F32),
            pltpu.SemaphoreType.DMA((14,)),
        ],
        compiler_params=pltpu.CompilerParams(vmem_limit_bytes=12 * 2**20),
        name="results",
    )(
        *(
            pltpu.with_memory_space_constraint(v, pltpu.VMEM)
            for v in (out, gin, g_up, g_down, g_qkv, small)
        )
    )


def shards(
    layer_input,
    flags,
    loss_mask,
    cotangent,
    gain_one,
    shift_one,
    w_qkv,
    b_qv,
    w_out,
    b_out,
    gain_two,
    shift_two,
    w_up,
    b_up,
    w_down,
    b_down,
    comm=True,
):
    parts = layer(
        comm,
        layer_input,
        cotangent,
        w_qkv.transpose(0, 2, 1),
        w_out,
        w_up,
        w_down,
        flags,
        loss_mask,
        b_qv,
        gain_one,
        shift_one,
        b_out,
        gain_two,
        shift_two,
        b_up,
        b_down,
    )
    out, gin, g_qkv, g_out, g_up, g_down, g_bqv, *vectors = results(*parts)
    g_gain1, g_shift1, g_bout, g_gain2, g_shift2, g_bup, g_bdown = vectors
    return (
        out.reshape(ROWS, D),
        gin.reshape(ROWS, D),
        g_gain1,
        g_shift1,
        g_qkv.reshape(3, 192, D).transpose(0, 2, 1),
        g_bqv,
        g_out,
        g_bout,
        g_gain2,
        g_shift2,
        g_up,
        g_bup,
        g_down,
        g_bdown,
    )


def solution(mesh):
    in_specs = (
        P("dp", None),
        P("dp"),
        P("dp"),
        P("dp", None),
        P(),
        P(),
        P(None, None, "tensor"),
        P(None, "tensor"),
        P("tensor", None),
        P(),
        P(),
        P(),
        P(None, "tensor"),
        P("tensor"),
        P("tensor", None),
        P(),
    )
    out_specs = (
        P("dp", None),
        P("dp", None),
        P(),
        P(),
        P(None, None, "tensor"),
        P(None, "tensor"),
        P("tensor", None),
        P(),
        P(),
        P(),
        P(None, "tensor"),
        P("tensor"),
        P("tensor", None),
        P(),
    )
    return jax.shard_map(shards, mesh=mesh, in_specs=in_specs, out_specs=out_specs, check_vma=False)
```

```python
import functools

import jax
import jax.numpy as jnp
from jax import lax
from jax.experimental import pallas as pl
from jax.experimental.pallas import tpu as pltpu
from jax.sharding import PartitionSpec as P

MESH = pl.DeviceIdType.MESH
BF = jnp.bfloat16
F32 = jnp.float32
D = 768
HD = 64
LEN = 512
HALF = 256
QUART = 128
SEQS = 3
ROWS = SEQS * LEN
EPS = 1e-05
SCALE = HD**-0.5
GELU_A = 0.7978845608028654
GELU_B = 0.044715

NN = (((1,), (0,)), ((), ()))
NT = (((1,), (1,)), ((), ()))
TN = (((0,), (0,)), ((), ()))

GAIN1, SHIFT1, GAIN2, SHIFT2, BOUT, BDOWN, BUP, BQV = range(8)


def dot(a, b, dims):
    return lax.dot_general(a, b, dims, preferred_element_type=F32)


def norm_parts(v):
    centred = v - jnp.mean(v, axis=1, keepdims=True)
    r = lax.rsqrt(jnp.mean(centred * centred, axis=1, keepdims=True) + EPS)
    return centred * r, r


def norm_back(v, e, gain):
    n, r = norm_parts(v)
    eg = e * gain
    grad = r * (
        eg
        - jnp.mean(eg, axis=1, keepdims=True)
        - n * jnp.mean(eg * n, axis=1, keepdims=True)
    )
    return grad, n


def col_sum(v):
    return jnp.sum(v, axis=0, keepdims=True)


def head_part(v, h):
    lane = lax.broadcasted_iota(jnp.int32, v.shape, 1)
    return jnp.where((lane >= HD * h) & (lane < HD * h + HD), v, jnp.zeros_like(v))


class Place:
    def __init__(self):
        dp = lax.axis_index("dp")
        self.t = t = lax.axis_index("tensor")
        self.z = dp // 8
        self.yl = (dp // 4) % 2
        self.x = dp % 4
        self.c = t % 2
        self.yh = t // 2
        self.t_sib = t + 1 - 2 * self.c
        self.t_part = (t + 2) % 4
        self.t_far = (self.t_sib + 2) % 4
        self.sib = (dp, self.t_sib)
        self.part = (dp, self.t_part)
        self.ypeer = (dp + 4 - 8 * self.yl, t)
        self.near = (dp + 4 - 8 * self.yl, self.t_part)
        self.dp = dp

    def xpeer(self, j):
        return (self.dp - self.x + (self.x + j) % 4, self.t)

    def zpeer(self, j):
        return (((self.z + j) % 4) * 8 + self.dp % 8, self.t)

    def core_and_x(self, k):
        dp, _ = self.xpeer(k % 4)
        return (dp, self.t if k < 4 else self.t_sib)

    def y_and_z(self, k):
        dp, _ = self.zpeer(k % 4)
        return (dp if k < 4 else dp + 4 - 8 * self.yl, self.t)

    def peers(self):
        return (
            [self.part, self.near]
            + [self.core_and_x(k) for k in range(1, 5)]
            + [self.y_and_z(k) for k in range(1, 5)]
        )


def remote(src, dst, send, recv, device):
    return pltpu.make_async_remote_copy(
        src_ref=src,
        dst_ref=dst,
        send_sem=send,
        recv_sem=recv,
        device_id=device,
        device_id_type=MESH,
    )


class Reduction:
    def __init__(self, at, stg, r1, r2, ry, send, recv, free):
        self.at, self.stg, self.r1, self.r2, self.ry = at, stg, r1, r2, ry
        self.send, self.recv, self.free = send, recv, free
        self.big = stg.shape[0] // 4
        self.small = stg.shape[0] // 16

    def axes(self, h):
        at = self.at
        if h == 0:
            return at.x, at.z, at.xpeer, at.zpeer
        return at.z, at.x, at.zpeer, at.xpeer

    def block(self, h, first):
        rows = pl.ds(pl.multiple_of(first * self.big, self.big), self.big)
        return self.stg.at[rows, pl.ds(h * 384, 384)]

    def part(self, h, first, second):
        start = pl.multiple_of(first * self.big + second * self.small, self.small)
        return self.stg.at[pl.ds(start, self.small), pl.ds(h * 384, 384)]

    def copy(self, step, src, dst, device):
        return remote(src, dst, self.send.at[step], self.recv.at[step], device)

    def all_of(self, step):
        ref = (self.r1, self.r2, self.ry, self.r2, self.r1)[step]
        return self.copy(step, ref, ref, self.at.sib)

    def arrived(self, step):
        self.all_of(step).wait_recv()

    def left(self, step):
        self.all_of(step).wait_send()

    def give_back(self, stage):
        self.left(stage)
        for h in (0, 1):
            peer = self.axes(h)[2 + stage]
            for j in (1, 2, 3):
                pl.semaphore_signal(
                    self.free.at[stage], inc=1, device_id=peer(j), device_id_type=MESH
                )

    def start(self):
        for h in (0, 1):
            first, _, peer, _ = self.axes(h)
            for j in (1, 2, 3):
                src = self.block(h, (first + j) % 4)
                self.copy(0, src, self.r1.at[h, j - 1], peer(j)).start()

    def second(self):
        self.arrived(0)
        for h in (0, 1):
            first, second, _, peer = self.axes(h)
            own = self.block(h, first)
            total = own[...].astype(F32)
            for j in (0, 1, 2):
                total = total + self.r1[h, j].astype(F32)
            own[...] = total.astype(BF)
            for j in (1, 2, 3):
                src = self.part(h, first, (second + j) % 4)
                self.copy(1, src, self.r2.at[h, j - 1], peer(j)).start()
        self.give_back(0)

    def third(self):
        self.arrived(1)
        for h in (0, 1):
            first, second, _, _ = self.axes(h)
            own = self.part(h, first, second)
            total = own[...].astype(F32)
            for j in (0, 1, 2):
                total = total + self.r2[h, j].astype(F32)
            own[...] = total.astype(BF)
            self.copy(2, own, self.ry.at[h], self.at.ypeer).start()
        self.give_back(1)

    def fourth(self):
        self.arrived(2)
        self.left(2)
        pl.semaphore_wait(self.free.at[1], 6)
        for h in (0, 1):
            first, second, _, peer = self.axes(h)
            own = self.part(h, first, second)
            own[...] = (own[...].astype(F32) + self.ry[h].astype(F32)).astype(BF)
            for j in (1, 2, 3):
                self.copy(3, own, own, peer(j)).start()

    def fifth(self):
        self.arrived(3)
        pl.semaphore_wait(self.free.at[0], 6)
        for h in (0, 1):
            first, _, peer, _ = self.axes(h)
            own = self.block(h, first)
            for j in (1, 2, 3):
                self.copy(4, own, own, peer(j)).start()

    def finish(self):
        self.arrived(4)

    def drain(self):
        self.left(3)
        self.left(4)


def kernel(
    comm,
    x_hbm,
    cot_hbm,
    wqkv_hbm,
    wout_hbm,
    wup_hbm,
    wdown_hbm,
    flags_hbm,
    mask_hbm,
    bqv_hbm,
    gain1_hbm,
    shift1_hbm,
    bout_hbm,
    gain2_hbm,
    shift2_hbm,
    bup_hbm,
    bdown_hbm,
    res,
    gin,
    stg_u,
    stg_d,
    stg_q,
    small_ref,
    flags_ref,
    mask_ref,
    bqv_ref,
    gain1_ref,
    shift1_ref,
    bout_ref,
    gain2_ref,
    shift2_ref,
    bup_ref,
    bdown_ref,
    x_ref,
    u_ref,
    wqkv,
    wof,
    wup,
    wdown,
    fwup,
    fwdown,
    bias,
    fbias,
    n1,
    q8,
    keys,
    vals,
    att,
    lse,
    mid,
    n2,
    nt2,
    actt,
    own_a,
    own_b,
    s1,
    r1,
    ex,
    mlow,
    gp,
    sc,
    pr,
    ds,
    red1,
    red2,
    redy,
    remy,
    weight,
    sm,
    smp,
    smx,
    smz,
    in_sem,
    a_send,
    a_recv,
    w_send,
    w_recv,
    t_send,
    t_recv,
    x_send,
    x_recv,
    d_send,
    d_recv,
    d_free,
    m_send,
    m_recv,
):
    at = Place()
    c, yh, t = (at.c, at.yh, at.t) if comm else (0, 0, 0)
    ghid = gin
    gpt = nt2.at[0:576]

    def lanes(s, half=None):
        if half is None:
            return pl.ds(pl.multiple_of(s * LEN, LEN), LEN)
        return pl.ds(pl.multiple_of(s * LEN + half * HALF, HALF), HALF)

    def core_rows(core):
        return pl.ds(pl.multiple_of(core * QUART, QUART), QUART)

    def flat(v):
        return v.reshape(-1, v.shape[-1])

    def wout_rows(t, start, count):
        return wof.at[pl.ds(pl.multiple_of(t * 192 + start, 48), count)]

    def wout_block(t):
        return wout_rows(t, 0, 192)

    def att_block(s):
        def block(t):
            return att.at[s, pl.ds(pl.multiple_of(t * 192, 192), 192)]

        block.rows = 192
        return block

    def row_block(ref, s):
        def block(t):
            return ref.at[s, t // 2, t % 2]

        block.rows = QUART
        return block

    def load(i, src, dst):
        return pltpu.make_async_copy(src, dst, in_sem.at[i])

    def load_x(s):
        return load(s, x_hbm.at[s], x_ref.at[s])

    load_wqkv = load(3, wqkv_hbm, wqkv)
    load_wout = load(4, wout_hbm, wout_block(t))
    load_cot = load(5, cot_hbm, u_ref)
    load_up = load(6, wup_hbm, wup)
    load_down = load(7, wdown_hbm, wdown)
    small_loads = [
        load(8 + i, src, dst)
        for i, (src, dst) in enumerate(
            (
                (gain1_hbm, gain1_ref),
                (shift1_hbm, shift1_ref),
                (bqv_hbm, bqv_ref),
                (bup_hbm, bup_ref),
                (flags_hbm, flags_ref),
                (mask_hbm, mask_ref),
                (bout_hbm, bout_ref),
                (gain2_hbm, gain2_ref),
                (shift2_hbm, shift2_ref),
                (bdown_hbm, bdown_ref),
            )
        )
    ]
    load_x(0).start()
    load_wqkv.start()
    if comm:
        barrier = pltpu.get_barrier_semaphore()
        peers = at.peers()
        for peer in peers:
            pl.semaphore_signal(barrier, inc=1, device_id=peer, device_id_type=MESH)
    for copy in small_loads:
        copy.start()
    load_wout.start()
    load_up.start()
    load_down.start()
    load_x(1).start()
    load_x(2).start()
    load_cot.start()
    sm[...] = jnp.zeros_like(sm)
    for copy in small_loads:
        copy.wait()
    bias[...] = jnp.broadcast_to(bup_ref[...].reshape(1, D), (8, D))
    weight[...] = jnp.maximum(flags_ref[...], mask_ref[...]).astype(F32).reshape(2 * SEQS, HALF)

    def fetch_part(i, count):
        first, second = (at.x, at.z) if i == 0 else (at.z, at.x)
        start = (second * 4 + (first if count == 1 else 0)) * 48
        return pl.ds(pl.multiple_of(start, 48), 48 * count)

    def fetch_copy(step, src, dst, device):
        return remote(src, dst, w_send.at[step], w_recv.at[step], device)

    def fetch_y(i):
        if i == 2:
            ref = wout_rows(t, at.x * 48, 48)
            return fetch_copy(0, ref, ref, at.near)
        src, dst = ((wup, fwup), (wdown, fwdown))[i]
        some = fetch_part(i, 1)
        return fetch_copy(1, src.at[some], dst.at[some], at.part)

    def fetch_a(i, j):
        peer = at.zpeer if i == 1 else at.xpeer
        if i == 2:
            ref = wout_rows(at.t_part, at.x * 48, 48)
            return fetch_copy(3, ref, ref, peer(j))
        ref = (fwup, fwdown)[i].at[fetch_part(i, 1)]
        return fetch_copy(4, ref, ref, peer(j))

    def fetch_b(i, j):
        peer = at.xpeer if i == 1 else at.zpeer
        ref = (fwup, fwdown)[i].at[fetch_part(i, 4)]
        return fetch_copy(5, ref, ref, peer(j))

    def fetch_all(step):
        ref = (wof.at[0:48], fwup.at[0:96], fbias, wof.at[0:144], fwup.at[0:288], nt2.at[0:576])[step]
        return fetch_copy(step, ref, ref, at.part)

    def fetch_first(kinds):
        if comm:
            for i in kinds:
                fetch_y(i).start()
            if 0 in kinds:
                fetch_copy(2, bias, fbias, at.part).start()

    def fetch_second(kinds):
        if comm:
            fetch_all(0 if 2 in kinds else 1).wait_recv()
            for i in kinds:
                for j in (1, 2, 3):
                    fetch_a(i, j).start()

    def fetch_third(kinds):
        if comm:
            fetch_all(3 if 2 in kinds else 4).wait_recv()
            for i in kinds:
                if i < 2:
                    for j in (1, 2, 3):
                        fetch_b(i, j).start()

    def fetch_wait():
        if comm:
            fetch_all(2).wait_recv()
            fetch_all(5).wait_recv()

    def fetch_left():
        if comm:
            for step in (0, 1, 2):
                fetch_all(step).wait_send()

    def fetch_drain():
        if comm:
            for step in (3, 4, 5):
                fetch_all(step).wait_send()

    def gather_copy(i, block, kind, t, device):
        ref = block(t)
        return remote(ref, ref, a_send.at[i], a_recv.at[i, kind], device)

    def gather_start(i, block):
        if comm:
            if not isinstance(i, int) or i != 3:
                gather_copy(i, block, 1, at.t, at.part).start()
            gather_copy(i, block, 0, at.t, at.sib).start()

    def gather_forward(i, block):
        if comm:
            if not isinstance(i, int) or i != 3:
                gather_copy(i, block, 1, at.t_part, at.part).wait_recv()
            gather_copy(i, block, 0, at.t_part, at.sib).start()

    def gather_all(i, block, count):
        if block is wout_block:
            ref = wof.at[0 : 192 * count]
        elif block.rows == 192:
            ref = att.at[0, 0 : 192 * count]
        else:
            ref = n1.at[0, 0 : QUART * count]
        return remote(ref, ref, a_send.at[i], a_recv.at[i, 0], at.sib)

    def gather_wait(i, block):
        if comm:
            gather_all(i, block, 2).wait_recv()

    def gather_drain(i, block):
        if comm:
            gather_all(i, block, 2 if block is wout_block else 3).wait_send()

    def core_copy(k, s):
        return remote(s1.at[k, s - 1], r1.at[k, s - 1], t_send.at[k, s - 1], t_recv.at[k, s - 1], at.sib)

    def core_sum(k, s, own):
        if comm:
            core_copy(k, s).wait()
        return own[s, core_rows(c), :] + r1[k, s - 1].astype(F32)

    def slot(kind, i):
        if isinstance(i, int) and i >= SEQS:
            return ex.at[kind, i - SEQS]
        rows = pl.ds(pl.multiple_of(i * HALF, HALF), HALF)
        if kind % 2 == 0:
            return actt.at[rows, pl.ds(kind // 2 * D, D)]
        return (wup, wdown)[kind // 2].at[rows]

    def chip_copy(i):
        return remote(slot(0, i), slot(1, i), x_send.at[0, i], x_recv.at[0, i], at.sib)

    def group_copy(i):
        return remote(slot(2, i), slot(3, i), x_send.at[1, i], x_recv.at[1, i], at.part)

    def share_copy(i, ref, s, core):
        some = ref.at[s, :, core]
        return remote(some, some, x_send.at[2, i], x_recv.at[2, i], at.sib)

    def chip_sum(i, own):
        if comm:
            chip_copy(i).wait()
        slot(2, i)[...] = (own[...] + slot(1, i)[...].astype(F32)).astype(BF)
        if comm:
            group_copy(i).start()

    def group_sum(i):
        if comm:
            group_copy(i).wait()
        return slot(2, i)[...].astype(F32) + slot(3, i)[...].astype(F32)

    def share(i, ref, s):
        if comm:
            share_copy(i, ref, s, c).start()

    def share_wait(i, ref, s):
        if comm:
            share_copy(i, ref, s, 1 - c).wait_recv()

    def core_part(v, core):
        return jnp.where(core == 0, v[:QUART], v[QUART:])

    def chip_rows_sum(v):
        return jnp.where(yh == 0, col_sum(v[:QUART]), col_sum(v[QUART:]))

    gain1, shift1, gain2, shift2, b_out, b_down = (
        ref[...].reshape(1, D)
        for ref in (gain1_ref, shift1_ref, gain2_ref, shift2_ref, bout_ref, bdown_ref)
    )

    def add_small(row, value):
        sm[row : row + 1, :] += value

    def project(s):
        load_x(s).wait()
        for half in range(2):
            n, _r = norm_parts(flat(x_ref[s, half]).astype(F32))
            n1[s, HALF * half : HALF * half + HALF, :] = (n * gain1 + shift1).astype(BF)
        normed = n1[s]
        q = (dot(normed, wqkv[0], NT) + bqv_ref[0:1, :]).astype(BF) * SCALE
        q8[s] = q
        k = dot(normed, wqkv[1], NT).astype(BF)
        keys[s] = k
        v = (dot(normed, wqkv[2], NT) + bqv_ref[1:2, :]).astype(BF)
        vals[s] = v

    def attend(s):
        q, k, vt = q8[s], keys[s], vals[s].T
        block = att_block(s)(t)
        for h in range(3):
            sc[...] = dot(head_part(k, h), q, NT)
            for part in range(4):
                cols = slice(part * 128, part * 128 + 128)
                scores = sc[:, cols]
                top = jnp.max(scores, axis=0, keepdims=True)
                e = jnp.exp(scores - top)
                total = col_sum(e)
                lse[3 * s + h, :, cols] = top + jnp.log(total)
                pr[:, cols] = (e * (1.0 / total)).astype(BF)
            mixed = dot(vt[HD * h : HD * h + HD], pr[...], NN)
            block[HD * h : HD * h + HD, :] = mixed.astype(BF)
        gather_start(s, att_block(s))

    def weigh(i, _):
        same = lax.broadcasted_iota(jnp.int32, (HALF, HALF), 0) == lax.broadcasted_iota(
            jnp.int32, (HALF, HALF), 1
        )
        diagonal = jnp.where(same, weight[pl.ds(i, 1), :], 0.0).astype(BF)
        rows = dot(diagonal, flat(u_ref[i // 2, i % 2]), NN).astype(BF)
        u_ref[i // 2, i % 2] = rows.reshape(2, QUART, D)
        return 0

    def hidden_units(normed, up, w_up, b_up, w_down):
        v = dot(normed, w_up[...], NN) + b_up
        back = dot(up, w_down[...], NT)
        square = v * v
        th = jnp.tanh(v * (GELU_A + (GELU_A * GELU_B) * square))
        cdf = 0.5 + 0.5 * th
        inner = v * (0.5 * GELU_A + (1.5 * GELU_A * GELU_B) * square)
        return (v * cdf).astype(BF), back * (cdf + inner * (1.0 - th * th))

    def feed(s, between):
        gather_wait(s, att_block(s))
        for own in (False, True):
            half = yh if own else 1 - yh
            some = lanes(s, half)
            cols = pl.ds(pl.multiple_of(half * HALF, HALF), HALF)
            middle = flat(x_ref[s, half]).astype(F32) + dot(att[s, :, cols], wof[...], TN) + b_out
            n, _r = norm_parts(middle)
            normed = (n * gain2 + shift2).astype(BF)
            nt2[:, some] = normed.T
            act, grad = hidden_units(normed, flat(u_ref[s, half]), wup, bias[0:1, :], wdown)
            add_small(BUP, col_sum(grad))
            grad = grad.astype(BF)
            actt[:, some] = act.T
            ghid[s, half] = grad.reshape(2, QUART, D)
            if own:
                between(1)
            if isinstance(s, int):
                piece = pl.ds(pl.multiple_of(half * QUART, QUART), QUART)
                mid[s, piece, :] = core_part(middle, c)
                for k, (ref, total) in enumerate(
                    ((own_a, dot(grad, wup[...], NT)), (own_b, dot(act, wdown[...], NN)))
                ):
                    ref[s, piece, :] = core_part(total, c)
                    slot(0, 3 + k)[piece, :] = core_part(total, 1 - c).astype(BF)
            elif own:
                mid[s] = middle
                n2[s - 1] = normed
                own_a[s] = dot(grad, wup[...], NT)
                own_b[s] = dot(act, wdown[...], NN)
            if not own:
                between(0)
        if isinstance(s, int) and comm:
            chip_copy(3).start()
            chip_copy(4).start()

    def feed_more(s):
        act, grad = hidden_units(n2[s - 1], flat(u_ref[s, yh]), fwup, fbias[0:1, :], fwdown)
        own_a[s] += dot(grad.astype(BF), fwup[...], NT)
        own_b[s] += dot(act, fwdown[...], NN)
        for k, ref in enumerate((own_a, own_b)):
            s1[k, s - 1] = ref[s, core_rows(1 - c), :].astype(BF)
            if comm:
                core_copy(k, s).start()

    def middle_back(s):
        e = core_sum(0, s, own_a)
        grad, n = norm_back(mid[s, core_rows(c), :], e, gain2)
        add_small(GAIN2, col_sum(e * n))
        add_small(SHIFT2, col_sum(e))
        up = u_ref[s, yh, c].astype(F32)
        grad = up + grad
        add_small(BOUT, col_sum(grad))
        add_small(BDOWN, col_sum(up))
        mlow[s, yh, c] = grad.astype(BF)
        gather_start(4 + s, row_block(mlow, s))

    def middle_back_first():
        e = group_sum(3)
        grad, n = norm_back(mid[0], e, gain2)
        add_small(GAIN2, chip_rows_sum(e * n))
        add_small(SHIFT2, chip_rows_sum(e))
        up = flat(u_ref[0, :, c]).astype(F32)
        grad = up + grad
        add_small(BOUT, chip_rows_sum(grad))
        add_small(BDOWN, chip_rows_sum(up))
        mlow[0, :, c] = grad.astype(BF).reshape(2, QUART, D)
        share(3, mlow, 0)

    def output_rows_first():
        total = mid[0] + group_sum(4) + b_down
        res[0, :, c] = total.astype(BF).reshape(2, QUART, D)
        share(4, res, 0)

    def output_rows(s):
        total = mid[s, core_rows(c), :] + core_sum(1, s, own_b) + b_down
        res[s, yh, c] = total.astype(BF)
        gather_start(7 + s, row_block(res, s))

    def reduction(i, ref, wide):
        if wide:
            r1, r2, ry = red1.at[i], red2.at[i], redy.at[i]
        else:
            j = i - 2
            r1 = red1.at[0, :, :, pl.ds(j * 64, 64)]
            r2 = red2.at[0, :, :, pl.ds(j * 16, 16)]
            ry = remy.at[j]
        return Reduction(at, ref, r1, r2, ry, d_send.at[i], d_recv.at[i], d_free.at[i])

    d_up, d_down = reduction(0, stg_u, True), reduction(1, stg_d, True)
    d_att = [reduction(2 + i, stg_q.at[pl.ds(i * HALF, HALF)], False) for i in range(3)]

    def reduce_step(name, which):
        if comm:
            getattr(which, name)()

    def stage(stg, start, count, value):
        stg[pl.ds(start, count), :] = value.astype(BF)

    def up_grads(i, _):
        start = pl.multiple_of(i * HALF, HALF)
        some = pl.ds(start, HALF)
        stage(stg_u, start, HALF, dot(nt2[some, :], flat(ghid[...]), NN))
        return 0

    def down_grads(i, _):
        start = pl.multiple_of(i * HALF, HALF)
        some = pl.ds(start, HALF)
        stage(stg_d, start, HALF, dot(actt[some, :], flat(u_ref[...]), NN))
        return 0

    def qkv_grads(start, count):
        stage(stg_q, start, count, dot(gpt[start : start + count, :], flat(n1[...]), NN))

    def out_grads():
        total = jnp.zeros((192, D), F32)
        for s in range(SEQS):
            total += dot(att_block(s)(t)[...], flat(mlow[s]), NN)
        stage(stg_q, 576, 192, total)

    def attend_back(s, between):
        some_lanes = lanes(s)
        mixed = dot(flat(mlow[s]), wout_block(t)[...], NT).astype(BF)
        q, k, v = q8[s], keys[s], vals[s]
        kt = k.T
        grad_k = jnp.zeros((LEN, 192), F32)
        grad_v = jnp.zeros((LEN, 192), F32)
        for h in range(3):
            sc[...] = dot(head_part(k, h), q, NT)
            back = dot(head_part(v, h), mixed, NT)
            some = slice(HD * h, HD * h + HD)
            for part in range(4):
                cols = slice(part * 128, part * 128 + 128)
                p = jnp.exp(sc[:, cols] - lse[3 * s + h, :, cols])
                pr[:, cols] = p.astype(BF)
                gp_part = back[:, cols]
                total = col_sum(gp_part * p)
                ds[:, cols] = (p * (gp_part - total)).astype(BF)
            grad_v += dot(pr[...], head_part(mixed, h), NN)
            grad_k += dot(ds[...], head_part(q, h), NN)
            gpt[some, some_lanes] = (dot(kt[some], ds[...], NN) * SCALE).astype(BF)
            between(h)
        grad_q = gpt[0:192, some_lanes].T
        grad_k = grad_k.astype(BF)
        grad_v = grad_v.astype(BF)
        gpt[192:384, some_lanes] = grad_k.T
        gpt[384:576, some_lanes] = grad_v.T
        for i, grad in enumerate((grad_q, grad_k, grad_v)):
            gp[i] = grad.reshape(2, 2, QUART, 192)
        sm[BQV : BQV + 1, 0:192] += col_sum(grad_q.astype(F32))
        sm[BQV : BQV + 1, 256:448] += col_sum(grad_v.astype(F32))
        for own in (False, True):
            core = c if own else 1 - c
            total = dot(flat(gp[0, :, core]), wqkv[0], NN)
            total += dot(flat(gp[1, :, core]), wqkv[1], NN)
            total += dot(flat(gp[2, :, core]), wqkv[2], NN)
            if own:
                own_a[s] = total
            else:
                slot(0, s)[...] = total.astype(BF)
                if comm:
                    chip_copy(s).start()

    def input_back(s):
        e = group_sum(s)
        grad, n = norm_back(flat(x_ref[s, :, c]).astype(F32), e, gain1)
        add_small(GAIN1, chip_rows_sum(e * n))
        add_small(SHIFT1, chip_rows_sum(e))
        total = flat(mlow[s, :, c]).astype(F32) + grad
        gin[s, :, c] = total.astype(BF).reshape(2, QUART, D)
        share(s, gin, s)

    LAST = SEQS - 1

    def later_copy(s):
        src = slot(2, s).at[core_rows(1 - yh)]
        dst = slot(3, s).at[0:QUART]
        return remote(src, dst, x_send.at[1, s], x_recv.at[1, s], at.part)

    def chip_sum_later(s):
        if comm:
            chip_copy(s).wait()
        total = own_a[s] + slot(1, s)[...].astype(F32)
        own_a[s] = total
        slot(2, s)[...] = total.astype(BF)
        if comm:
            later_copy(s).start()

    def input_back_later(s):
        if comm:
            later_copy(s).wait()
        e = own_a[s, core_rows(yh), :] + slot(3, s)[0:QUART, :].astype(F32)
        grad, n = norm_back(x_ref[s, yh, c].astype(F32), e, gain1)
        add_small(GAIN1, col_sum(e * n))
        add_small(SHIFT1, col_sum(e))
        if s == LAST:
            small_part()
        gin[s, yh, c] = (mlow[s, yh, c].astype(F32) + grad).astype(BF)
        gather_start(7 if s == LAST else 4, row_block(gin, s))

    def small_copy(i, slots, slot, device):
        ref = slots.at[slot]
        return remote(ref, ref, m_send.at[i], m_recv.at[i], device)

    def small_row():
        return lax.broadcasted_iota(jnp.int32, (8, D), 0)

    def small_part():
        smp[yh] = sm[...]
        if comm:
            small_copy(0, smp, yh, at.part).start()

    def small_all(i, slots):
        return remote(slots.at[0:7], slots.at[0:7], m_send.at[i], m_recv.at[i], at.sib)

    def first_slot():
        return at.c * 4 + at.x

    def second_slot():
        return at.yl * 4 + at.z

    def small_first():
        small_copy(0, smp, 1 - yh, at.part).wait_recv()
        smx[first_slot()] = jnp.where(small_row() < BUP, smp[0] + smp[1], sm[...])
        for k in range(1, 8):
            small_copy(1, smx, first_slot(), at.core_and_x(k)).start()

    def small_second():
        small_all(1, smx).wait_recv()
        cores = [
            (smx[4 * i] + smx[4 * i + 1]) + (smx[4 * i + 2] + smx[4 * i + 3]) for i in (0, 1)
        ]
        mine = jnp.where(c == 0, cores[0], cores[1])
        smz[second_slot()] = jnp.where(small_row() < BUP, cores[0] + cores[1], mine)
        for k in range(1, 8):
            small_copy(2, smz, second_slot(), at.y_and_z(k)).start()

    def small_end():
        small_all(2, smz).wait_recv()
        total = smz[0]
        for i in range(1, 8):
            total = total + smz[i]
        small_ref[...] = total

    def small_drain():
        small_copy(0, smp, yh, at.part).wait_send()
        small_all(1, smx).wait_send()
        small_all(2, smz).wait_send()

    load_wqkv.wait()
    project(0)
    load_wout.wait()
    load_up.wait()
    load_down.wait()
    if comm:
        pl.semaphore_wait(barrier, len(peers))
    fetch_first((2,))
    gather_start(3, wout_block)

    def attend_all(s, _):
        @pl.when(s > 0)
        def _():
            project(s)

        @pl.when(s == 1)
        def _():
            fetch_second((2,))

        attend(s)

        @pl.when(s == 0)
        def _():
            fetch_first((0, 1))

        return 0

    lax.fori_loop(0, SEQS, attend_all, 0)
    load_cot.wait()
    lax.fori_loop(0, 2, weigh, 0)
    fetch_third((2,))
    gather_forward(3, wout_block)
    lax.fori_loop(2, 2 * SEQS, weigh, 0)
    gather_forward(0, att_block(0))
    fetch_second((0, 1))
    gather_wait(3, wout_block)

    def feed_first(slot):
        if slot == 1:
            gather_forward(1, att_block(1))

    feed(0, feed_first)
    fetch_third((0, 1))

    def feed_all(s, _):
        def between(slot):
            @pl.when(s == 1)
            def _():
                if slot == 0:
                    chip_sum(3, own_a.at[0])
                    chip_sum(4, own_b.at[0])
                else:
                    gather_forward(2, att_block(2))

        feed(s, between)
        return 0

    lax.fori_loop(1, SEQS, feed_all, 0)
    fetch_left()
    lax.fori_loop(0, 3, up_grads, 0)
    reduce_step("start", d_up)
    lax.fori_loop(0, 3, down_grads, 0)
    middle_back_first()
    fetch_wait()
    feed_more(1)
    feed_more(2)
    middle_back(1)
    fetch_drain()
    gather_drain(3, wout_block)
    for s in range(SEQS):
        gather_drain(s, att_block(s))
    middle_back(2)
    share_wait(3, mlow, 0)

    def attend_back_all(s, _):
        def between(h):
            if h == 0:

                @pl.when(s == 0)
                def _():
                    reduce_step("second", d_up)
                    reduce_step("start", d_down)

                @pl.when(s == 2)
                def _():
                    reduce_step("fifth", d_up)
                    chip_sum_later(1)

            if h == 1:

                @pl.when(s == 0)
                def _():
                    output_rows_first()

                @pl.when(s == 1)
                def _():
                    gather_forward(6, row_block(mlow, 2))
                    reduce_step("fourth", d_up)

                @pl.when(s == 2)
                def _():
                    reduce_step("third", d_down)

            if h == 2:

                @pl.when(s == 1)
                def _():
                    reduce_step("second", d_down)

        attend_back(s, between)

        @pl.when(s == 0)
        def _():
            gather_forward(5, row_block(mlow, 1))
            reduce_step("third", d_up)
            chip_sum(0, own_a.at[0])
            gather_wait(5, row_block(mlow, 1))

        @pl.when(s == 1)
        def _():
            gather_wait(6, row_block(mlow, 2))

        return 0

    lax.fori_loop(0, SEQS, attend_back_all, 0)
    qkv_grads(0, HALF)
    reduce_step("start", d_att[0])
    chip_sum_later(LAST)
    qkv_grads(HALF, HALF)
    reduce_step("start", d_att[1])
    qkv_grads(2 * HALF, 64)
    out_grads()
    reduce_step("start", d_att[2])
    output_rows(1)
    input_back(0)
    input_back_later(1)
    for s in (1, 2):
        gather_drain(4 + s, row_block(mlow, s))
    reduce_step("fourth", d_down)
    for part in d_att:
        reduce_step("second", part)
    reduce_step("fifth", d_down)
    for part in d_att:
        reduce_step("third", part)
    input_back_later(LAST)
    output_rows(2)
    for part in d_att:
        reduce_step("fourth", part)
    if comm:
        small_first()
    share_wait(0, gin, 0)
    share_wait(4, res, 0)
    for part in d_att:
        reduce_step("fifth", part)
    if comm:
        small_second()
    gather_forward(8, row_block(res, 1))
    gather_forward(4, row_block(gin, 1))
    gather_forward(7, row_block(gin, LAST))
    reduce_step("finish", d_up)
    reduce_step("drain", d_up)
    if comm:
        for i, ref, s in ((0, gin, 0), (3, mlow, 0), (4, res, 0)):
            share_copy(i, ref, s, c).wait_send()
    gather_forward(9, row_block(res, 2))
    reduce_step("finish", d_down)
    reduce_step("drain", d_down)
    for i, ref, s in ((8, res, 1), (4, gin, 1), (7, gin, LAST), (9, res, 2)):
        gather_wait(i, row_block(ref, s))
        gather_drain(i, row_block(ref, s))
    if comm:
        small_end()
        small_drain()
    else:
        small_ref[...] = sm[...]
    for part in d_att:
        reduce_step("finish", part)
        reduce_step("drain", part)


def layer(comm, x, cot, *rest):
    rows = (SEQS, 2, 2, QUART, D)
    half = (SEQS, HALF, D)
    dma = pltpu.SemaphoreType.DMA
    scratch = [
        pltpu.VMEM((ROWS,), jnp.int32),
        pltpu.VMEM((ROWS,), jnp.int32),
        pltpu.VMEM((2, 192), F32),
        pltpu.VMEM((D,), F32),
        pltpu.VMEM((D,), F32),
        pltpu.VMEM((D,), F32),
        pltpu.VMEM((D,), F32),
        pltpu.VMEM((D,), F32),
        pltpu.VMEM((D,), F32),
        pltpu.VMEM((D,), F32),
        pltpu.VMEM(rows, BF),
        pltpu.VMEM(rows, BF),
        pltpu.VMEM((3, 192, D), BF),
        pltpu.VMEM((D, D), BF),
        pltpu.VMEM((D, D), BF),
        pltpu.VMEM((D, D), BF),
        pltpu.VMEM((D, D), BF),
        pltpu.VMEM((D, D), BF),
        pltpu.VMEM((8, D), F32),
        pltpu.VMEM((8, D), F32),
        pltpu.VMEM((SEQS, LEN, D), BF),
        pltpu.VMEM((SEQS, LEN, 192), BF),
        pltpu.VMEM((SEQS, LEN, 192), BF),
        pltpu.VMEM((SEQS, LEN, 192), BF),
        pltpu.VMEM((SEQS, D, LEN), BF),
        pltpu.VMEM((3 * SEQS, 1, LEN), F32),
        pltpu.VMEM(half, F32),
        pltpu.VMEM((SEQS - 1, HALF, D), BF),
        pltpu.VMEM((D, ROWS), BF),
        pltpu.VMEM((D, ROWS), BF),
        pltpu.VMEM(half, F32),
        pltpu.VMEM(half, F32),
        pltpu.VMEM((2, SEQS - 1, QUART, D), BF),
        pltpu.VMEM((2, SEQS - 1, QUART, D), BF),
        pltpu.VMEM((4, 2, HALF, D), BF),
        pltpu.VMEM(rows, BF),
        pltpu.VMEM((3, 2, 2, QUART, 192), BF),
        pltpu.VMEM((LEN, LEN), F32),
        pltpu.VMEM((LEN, LEN), BF),
        pltpu.VMEM((LEN, LEN), BF),
        pltpu.VMEM((2, 2, 3, 192, 384), BF),
        pltpu.VMEM((2, 2, 3, 48, 384), BF),
        pltpu.VMEM((2, 2, 48, 384), BF),
        pltpu.VMEM((3, 2, 16, 384), BF),
        pltpu.VMEM((2 * SEQS, HALF), F32),
        pltpu.VMEM((8, D), F32),
        pltpu.VMEM((2, 8, D), F32),
        pltpu.VMEM((8, 8, D), F32),
        pltpu.VMEM((8, 8, D), F32),
        dma((18,)),
        dma((10,)),
        dma((10, 2)),
        dma((6,)),
        dma((6,)),
        dma((2, SEQS - 1)),
        dma((2, SEQS - 1)),
        dma((3, 5)),
        dma((3, 5)),
        dma((5, 5)),
        dma((5, 5)),
        pltpu.SemaphoreType.REGULAR((5, 2)),
        dma((3,)),
        dma((3,)),
    ]
    anywhere = pl.BlockSpec(memory_space=pl.ANY)
    vmem = pl.BlockSpec(memory_space=pltpu.VMEM)
    return pl.pallas_call(
        functools.partial(kernel, comm),
        out_shape=(
            pltpu.VMEM(rows, BF),
            pltpu.VMEM(rows, BF),
            pltpu.VMEM((D, D), BF),
            pltpu.VMEM((D, D), BF),
            pltpu.VMEM((D, D), BF),
            pltpu.VMEM((8, D), F32),
        ),
        in_specs=[anywhere] * 16,
        out_specs=(vmem,) * 6,
        scratch_shapes=scratch,
        compiler_params=pltpu.CompilerParams(
            collective_id=0 if comm else None,
            has_side_effects=True,
            vmem_limit_bytes=55 * 2**20,
        ),
        cost_estimate=pl.CostEstimate(
            flops=20 * 10**9, bytes_accessed=20 * 10**6, transcendentals=10**7
        ),
        name="layer",
    )(x.reshape(rows), cot.reshape(rows), *rest)


def results(out, gin, g_up, g_down, g_qkv, small):
    def kernel(out, gin, up, down, qkv, small, *rest):
        (out_to, gin_to, qkv_to, out_w_to, up_to, down_to, bqv_to), rest = rest[:7], rest[7:]
        vectors, (wide, narrow, pair, sem) = rest[:7], rest[7:]
        copies = []

        def start(i, src, dst):
            copy = pltpu.make_async_copy(src, dst, sem.at[i])
            copy.start()
            copies.append(copy)

        start(0, out, out_to)
        start(1, gin, gin_to)
        for i, (src, first, rows, dst) in enumerate(
            (
                (up, 0, D, up_to),
                (down, 0, D, down_to),
                (qkv, 0, 576, qkv_to),
                (qkv, 576, 192, out_w_to),
            )
        ):
            at = (0, D, 2 * D, 2 * D + 576)[i]
            wide[at : at + rows, :] = src[first : first + rows, :].astype(F32)
            start(2 + i, wide.at[pl.ds(at, rows)], dst)
        for i, row in enumerate((GAIN1, SHIFT1, BOUT, GAIN2, SHIFT2, BUP, BDOWN)):
            narrow[i][...] = small[row : row + 1, :].reshape(D)
            start(6 + i, narrow[i], vectors[i])
        pair[0:1, :] = small[BQV : BQV + 1, 0:192]
        pair[1:2, :] = small[BQV : BQV + 1, 256:448]
        start(13, pair, bqv_to)
        for copy in copies:
            copy.wait()

    anywhere = pl.BlockSpec(memory_space=pl.ANY)
    vmem = pl.BlockSpec(memory_space=pltpu.VMEM)

    def shape(*dims, dtype=F32):
        return jax.ShapeDtypeStruct(dims, dtype)

    return pl.pallas_call(
        kernel,
        out_shape=(
            shape(*out.shape, dtype=BF),
            shape(*gin.shape, dtype=BF),
            shape(576, D),
            shape(192, D),
            shape(D, D),
            shape(D, D),
            shape(2, 192),
        )
        + (shape(D),) * 7,
        in_specs=[vmem] * 6,
        out_specs=(anywhere,) * 14,
        scratch_shapes=[
            pltpu.VMEM((3 * D, D), F32),
            [pltpu.VMEM((D,), F32)] * 7,
            pltpu.VMEM((2, 192), F32),
            pltpu.SemaphoreType.DMA((14,)),
        ],
        compiler_params=pltpu.CompilerParams(vmem_limit_bytes=12 * 2**20),
        name="results",
    )(
        *(
            pltpu.with_memory_space_constraint(v, pltpu.VMEM)
            for v in (out, gin, g_up, g_down, g_qkv, small)
        )
    )


def shards(
    layer_input,
    flags,
    loss_mask,
    cotangent,
    gain_one,
    shift_one,
    w_qkv,
    b_qv,
    w_out,
    b_out,
    gain_two,
    shift_two,
    w_up,
    b_up,
    w_down,
    b_down,
    comm=True,
):
    parts = layer(
        comm,
        layer_input,
        cotangent,
        w_qkv.transpose(0, 2, 1),
        w_out,
        w_up,
        w_down,
        flags,
        loss_mask,
        b_qv,
        gain_one,
        shift_one,
        b_out,
        gain_two,
        shift_two,
        b_up,
        b_down,
    )
    out, gin, g_qkv, g_out, g_up, g_down, g_bqv, *vectors = results(*parts)
    g_gain1, g_shift1, g_bout, g_gain2, g_shift2, g_bup, g_bdown = vectors
    return (
        out.reshape(ROWS, D),
        gin.reshape(ROWS, D),
        g_gain1,
        g_shift1,
        g_qkv.reshape(3, 192, D).transpose(0, 2, 1),
        g_bqv,
        g_out,
        g_bout,
        g_gain2,
        g_shift2,
        g_up,
        g_bup,
        g_down,
        g_bdown,
    )


def solution(mesh):
    in_specs = (
        P("dp", None),
        P("dp"),
        P("dp"),
        P("dp", None),
        P(),
        P(),
        P(None, None, "tensor"),
        P(None, "tensor"),
        P("tensor", None),
        P(),
        P(),
        P(),
        P(None, "tensor"),
        P("tensor"),
        P("tensor", None),
        P(),
    )
    out_specs = (
        P("dp", None),
        P("dp", None),
        P(),
        P(),
        P(None, None, "tensor"),
        P(None, "tensor"),
        P("tensor", None),
        P(),
        P(),
        P(),
        P(None, "tensor"),
        P("tensor"),
        P("tensor", None),
        P(),
    )
    return jax.shard_map(shards, mesh=mesh, in_specs=in_specs, out_specs=out_specs, check_vma=False)
```
